256 devices in a mesh: enc: 8 (over y, core), seq: 32 (over z, x).
Axes of the slice: x: 4, y: 4, z: 8, core: 2. Of those that a mesh axis runs over, the one named last changes fastest.
Arguments:
- patches: bfloat16 [32, 896, 1280], P('seq', 'enc'), may hold values from -6 to 6
- vision_gain: float32 [1280], replicated, may hold values from 0.2 to 3
- merge_up: bfloat16 [5120, 2560], P(None, 'enc'), may hold values from -0.078125 to 0.078125
- merge_up_bias: float32 [2560], P('enc'), may hold values from -3 to 3
- merge_down: bfloat16 [2560, 4096], P('enc'), may hold values from -0.15625 to 0.15625
- merge_down_bias: float32 [4096], P('enc'), may hold values from -3 to 3
- text_embed: bfloat16 [8192, 4096], P('seq', 'enc'), may hold values from -6 to 6
- image_lengths: int32 [32, 16], replicated, may hold values from 1 to 16, as said below
- image_offsets: int32 [32, 16], replicated, may hold values from 0 to 8191, as said below
- input_gain: float32 [4096], replicated, may hold values from 0.1 to 1.9
- qkv_weight: bfloat16 [4096, 5120], P(None, 'enc'), may hold values from -0.09375 to 0.09375
- qkv_bias: float32 [5120], P('enc'), may hold values from -24 to 24
Outputs:
- attention: bfloat16 [8192, 4096], P('seq', 'enc')
The draws below stay inside these ranges and needn't reach their ends.
Inputs may be any that keep to these rules, and one draw needn't show every extreme that they name: `image_lengths`: each row sums to 224; every row has a frame of exactly 16 merged tokens. `image_offsets`: A frame's tokens are consecutive and lie within one sequence shard of 256 tokens; no two frames share a token. The 16 frames of one group go to 16 different shards, and every shard receives 16 frames, each from a different group.
All inputs are finite; a program needn't handle non-finite values.
Results may differ from the reference program's by a relative error of at most 0.025.
Values may be sent and summed in bfloat16 or wider, within the bound.
A program may use at most 64 MiB of HBM per device.

```python
import math
import jax
import jax.numpy as jnp
from jax import lax

VW = 1280
DM = 4096
HD = 128
HEADS_DEV = 4
HM_DEV = 320
LMAX = 16
T_DEV = 256
FRAMES = 16
MG = 224
PATCH_DEV = 112
QKV_DEV = 640
MH = 2560
Q_HEADS = 32
KV_HEADS = 4
TOKENS = 8192
N_ENC = 8
N_SEQ = 32


def compose_parts(key, remain, part_count, upper_cap):
    pieces = []
    for part_id in range(part_count - 1):
        later_parts = part_count - 1 - part_id
        low_bound = jnp.maximum(remain - later_parts * upper_cap, 0)
        high_bound = jnp.minimum(remain, upper_cap)
        chosen = jax.random.randint(jax.random.fold_in(key, part_id), remain.shape, low_bound, high_bound + 1, dtype=jnp.int32)
        pieces.append(chosen)
        remain = remain - chosen
    pieces.append(remain)
    return jnp.stack(pieces, axis=1)


def shuffle_rows(key, int_table):
    columns = int_table.shape[1]
    scores = jax.random.randint(key, int_table.shape, 0, 1 << 20, dtype=jnp.int32) * columns + jnp.arange(columns, dtype=jnp.int32)[None, :]
    new_order = jnp.argsort(scores, axis=1, stable=True)
    return jnp.take_along_axis(int_table, new_order, axis=1)


def frame_plan(key):
    groups = jnp.arange(N_SEQ, dtype=jnp.int32)
    frame_ids = jnp.arange(FRAMES, dtype=jnp.int32)
    shortfall = compose_parts(jax.random.fold_in(key, 1), jnp.full((N_SEQ,), 2 * FRAMES, jnp.int32), FRAMES - 1, LMAX - 1)
    shortfall = jnp.concatenate([jnp.zeros((N_SEQ, 1), jnp.int32), shortfall], axis=1)
    lengths = LMAX - shuffle_rows(jax.random.fold_in(key, 2), shortfall)
    shifts = jax.random.permutation(jax.random.fold_in(key, 3), N_SEQ)[:FRAMES].astype(jnp.int32)
    owners = (groups[:, None] + shifts[None, :]) % N_SEQ
    senders = (groups[:, None] - shifts[None, :]) % N_SEQ
    owner_lengths = lengths[senders, frame_ids[None, :]]
    spare_rows = T_DEV - jnp.sum(owner_lengths, axis=1)
    text_gaps = shuffle_rows(jax.random.fold_in(key, 5), compose_parts(jax.random.fold_in(key, 4), spare_rows, FRAMES + 1, T_DEV))
    local_start = jnp.cumsum(owner_lengths, axis=1) - owner_lengths + jnp.cumsum(text_gaps[:, :FRAMES], axis=1)
    begins = groups[:, None] * T_DEV + local_start
    offsets = begins[owners, frame_ids[None, :]]
    return (lengths.astype(jnp.int32), offsets.astype(jnp.int32))


def draw_image_lengths(key, part):
    lengths, offsets = frame_plan(key)
    return lengths


def draw_image_offsets(key, part):
    lengths, offsets = frame_plan(key)
    return offsets


def bias_table(key, base, levels, jitter_lo, jitter_hi):
    total = N_ENC * QKV_DEV
    column = jnp.arange(total, dtype=jnp.int32)
    block = column // QKV_DEV
    within = column % QKV_DEV
    slot = within // HD
    inner = within % HD
    strong = inner % (HD // 2) >= 3 * HD // 8
    is_query = slot < HEADS_DEV
    head_id = jnp.clip(block * HEADS_DEV + slot, 0, 7)
    query_part = jnp.logical_and(is_query, block < 2)
    key_part = jnp.logical_and(jnp.logical_not(is_query), block == 0)
    level = jnp.where(query_part, levels[head_id], jnp.where(key_part, 1.0, 0.0))
    amplitude = (880.0 / HD ** 0.5) ** 0.5
    signs = (jax.random.randint(jax.random.fold_in(key, 3), (HD,), 0, 2, dtype=jnp.int32) * 2 - 1).astype(jnp.float32)
    jitter = jax.random.uniform(jax.random.fold_in(key, 2), (HD,), jnp.float32, jitter_lo, jitter_hi)
    pattern = signs * jitter * amplitude
    chosen = jnp.logical_and(strong, jnp.logical_or(query_part, key_part))
    return jnp.where(chosen, pattern[inner] * level, base).astype(jnp.float32)


def draw_qkv_bias(key, part):
    key = jax.random.fold_in(key, 7)
    total = N_ENC * QKV_DEV
    base = jnp.clip(0.5 * jax.random.normal(jax.random.fold_in(key, 1), (total,), jnp.float32), -3.0, 3.0)
    levels = jnp.array([1.0, 0.75, 0.5, 0.3, 0.0, 0.9, 0.6, 0.15], jnp.float32)
    return bias_table(key, base, levels, 0.95, 1.05)


def raised(values, own_key, source, target, shards_of, factor):
    owner, partner = [(jnp.arange(values.shape[axis_at]) // (values.shape[axis_at] // shards_of)).reshape([-1 if axis == axis_at else 1 for axis in range(values.ndim)]) for axis_at in (source, target)]
    chosen = jax.random.permutation(own_key, shards_of)[partner]
    strong = (owner == chosen) | (owner == (partner + shards_of // 2) % shards_of)
    return jnp.where(strong, factor * values, values)


def steps_of(rng, shape, split, smallest, high):
    loudness = 1.0
    for axis_at, shards_of in split:
        heights = jax.random.uniform(jax.random.fold_in(jax.random.fold_in(rng, 6), axis_at), (shards_of,), jnp.float32, smallest / len(split), high / len(split))
        loudness = loudness * jnp.repeat(jnp.exp(heights), shape[axis_at] // shards_of).reshape((-1,) + (1,) * (len(shape) - 1 - axis_at))
    return loudness


def bell_draw(rng, extent, scale, most, shards=(), kind=jnp.bfloat16):
    entries = scale * jax.random.normal(rng, extent, jnp.float32)
    if shards:
        entries = entries * steps_of(rng, extent, shards, -0.22, 0.18)
    return jnp.clip(entries, -most, most).astype(kind)


def noise_with(rng, extent, width, bound, split, heavy, kind=jnp.bfloat16):
    drawn = width * jax.random.normal(rng, extent, jnp.float32)
    if split:
        drawn = drawn * steps_of(rng, extent, split, -0.22, 0.18)
    return jnp.clip(raised(drawn, jax.random.fold_in(rng, 3), *heavy), -bound, bound).astype(kind)


def setup_inputs(seed: int = 0) -> dict:
    streams_of = jax.random.split(jax.random.key(seed), 13)
    return {
        "patches": bell_draw(streams_of[0], (N_SEQ, N_ENC * PATCH_DEV, VW), 1.0, 6.0, ((0, 32), (1, 8))),
        "vision_gain": jnp.clip(jnp.exp(jax.random.uniform(streams_of[1], (VW,), jnp.float32, math.log(0.2), math.log(3.0))), 0.2, 3.0),
        "merge_up": bell_draw(streams_of[2], (4 * VW, MH), (4 * VW) ** -0.5, 0.078125, ((1, 8),)),
        "merge_up_bias": bell_draw(streams_of[3], (MH,), 0.5, 3.0, ((0, 8),), jnp.float32),
        "merge_down": noise_with(streams_of[4], (MH, DM), MH ** -0.5, 0.15625, ((0, 8),), (0, 1, 8, 2.0)),
        "merge_down_bias": bell_draw(streams_of[5], (DM,), 0.5, 3.0, ((0, 8),), jnp.float32),
        "text_embed": bell_draw(streams_of[6], (TOKENS, DM), 1.0, 6.0, ((0, 32), (1, 8))),
        "image_lengths": draw_image_lengths(jax.random.fold_in(streams_of[12], 71), 0),
        "image_offsets": draw_image_offsets(jax.random.fold_in(streams_of[12], 71), 0),
        "input_gain": jnp.clip(1.0 + 0.18 * jax.random.normal(streams_of[9], (DM,), jnp.float32), 0.1, 1.9),
        "qkv_weight": bell_draw(streams_of[10], (DM, N_ENC * QKV_DEV), DM ** -0.5, 0.09375, ((1, 8),)),
        "qkv_bias": draw_qkv_bias(jax.random.fold_in(streams_of[12], 71), 0),
    }


EPSILON = 1e-06
THETA = 1000000.0

def rms_norm(values, scale_gain):
    widened = values.astype(jnp.float32)
    mean_square = lax.optimization_barrier(jnp.mean(widened * widened, axis=-1, keepdims=True))
    return widened * lax.rsqrt(mean_square + EPSILON) * scale_gain

def rotate(values, positions):
    half_dim = values.shape[-1] // 2
    steps_f = jnp.arange(half_dim).astype(jnp.float32)
    inv_freq = jnp.exp(steps_f * (-2.0 * jnp.log(THETA) / values.shape[-1]))
    angles = positions[:, None] * inv_freq[None, :]
    cosine = jnp.cos(angles)[:, None, :]
    sine_part = jnp.sin(angles)[:, None, :]
    first_half = values[..., :half_dim]
    second_half = values[..., half_dim:]
    return jnp.concatenate([first_half * cosine - second_half * sine_part, second_half * cosine + first_half * sine_part], axis=-1)

def reference(patches, vision_gain, merge_up, merge_up_bias, merge_down, merge_down_bias, text_embed, image_lengths, image_offsets, input_gain, qkv_weight, qkv_bias):
    normed = rms_norm(patches, vision_gain).astype(jnp.bfloat16)
    grouped = normed.reshape(N_SEQ * MG, 4 * VW)
    hidden = jax.nn.gelu(jnp.dot(grouped, merge_up, preferred_element_type=jnp.float32) + merge_up_bias, approximate=False).astype(jnp.bfloat16)
    hidden_blocks = hidden.reshape(N_SEQ * MG, N_ENC, HM_DEV)
    down_blocks = merge_down.reshape(N_ENC, HM_DEV, DM)

    def add_share(running, block_id):
        part_hidden = lax.dynamic_index_in_dim(hidden_blocks, block_id, 1, keepdims=False)
        part_down = lax.dynamic_index_in_dim(down_blocks, block_id, 0, keepdims=False)
        share = jnp.dot(part_hidden, part_down, preferred_element_type=jnp.float32).astype(jnp.bfloat16)
        share = lax.optimization_barrier(share)
        return (running + share.astype(jnp.float32), None)
    summed, _ = lax.scan(add_share, jnp.zeros((N_SEQ * MG, DM), jnp.float32), jnp.arange(N_ENC, dtype=jnp.int32))
    embeddings = (summed + merge_down_bias).astype(jnp.bfloat16)
    cum_end = jnp.cumsum(image_lengths, axis=1).astype(jnp.int32)
    starts = (cum_end - image_lengths).astype(jnp.int32)
    row_ids = jnp.arange(MG, dtype=jnp.int32)
    frame_of = lax.optimization_barrier(jnp.sum((row_ids[None, :, None] >= cum_end[:, None, :]).astype(jnp.int32), axis=2)).astype(jnp.int32)
    destination = (jnp.take_along_axis(image_offsets, frame_of, axis=1) + row_ids[None, :] - jnp.take_along_axis(starts, frame_of, axis=1)).astype(jnp.int32)
    sequence = text_embed.at[destination.reshape(-1)].set(embeddings)
    normed_tokens = rms_norm(sequence, input_gain).astype(jnp.bfloat16)
    projected = jnp.dot(normed_tokens, qkv_weight, preferred_element_type=jnp.float32) + qkv_bias
    projected = projected.reshape(TOKENS, N_ENC, QKV_DEV)
    positions = jnp.arange(TOKENS).astype(jnp.float32)
    queries = rotate(projected[:, :, :HEADS_DEV * HD].reshape(TOKENS, Q_HEADS, HD), positions)
    kv_parts = projected[:, :, HEADS_DEV * HD:]
    key_rows = rotate(kv_parts[:, 0::2, :], positions)
    value_rows = kv_parts[:, 1::2, :].astype(jnp.bfloat16)
    causal = jnp.arange(TOKENS)[:, None] >= jnp.arange(TOKENS)[None, :]
    score_scale = HD ** (-0.5)
    group_size = Q_HEADS // KV_HEADS

    def one_head(head_id):
        query_head = lax.dynamic_index_in_dim(queries, head_id, 1, keepdims=False)
        group_id = head_id // group_size
        key_head = lax.dynamic_index_in_dim(key_rows, group_id, 1, keepdims=False)
        value_head = lax.dynamic_index_in_dim(value_rows, group_id, 1, keepdims=False)
        scores = jnp.dot(query_head, key_head.T, preferred_element_type=jnp.float32, precision=lax.Precision.HIGHEST) * score_scale
        scores = jnp.where(causal, scores, -jnp.inf)
        row_max = lax.optimization_barrier(jnp.max(scores, axis=1, keepdims=True))
        weights = jnp.exp(scores - row_max)
        row_total = lax.optimization_barrier(jnp.sum(weights, axis=1, keepdims=True))
        head_out = jnp.dot(weights.astype(jnp.bfloat16), value_head, preferred_element_type=jnp.float32) / row_total
        return head_out.astype(jnp.bfloat16)
    heads_out = lax.map(one_head, jnp.arange(Q_HEADS, dtype=jnp.int32))
    return heads_out.transpose(1, 0, 2).reshape(TOKENS, Q_HEADS * HD)
```

```python
import math

import jax
import jax.numpy as jnp
import numpy as np
from jax import lax
from jax.experimental import pallas as pl
from jax.experimental.pallas import tpu as pltpu
from jax.sharding import PartitionSpec as P

HD = 128
LMAX = 16
NX = 4
EPSILON = 1e-06
THETA = 1000000.0
NEG = -1e30
MESH = pl.DeviceIdType.MESH


def wrap(value, size):
    return lax.rem(value + 2 * size, size)


def remote(src, dst, to, send_sem, recv_sem):
    return pltpu.make_async_remote_copy(
        src_ref=src, dst_ref=dst, send_sem=send_sem, recv_sem=recv_sem, device_id=to, device_id_type=MESH
    )


def sine_cosine(angle):
    turns = jnp.floor(angle * (2.0 / math.pi) + 0.5)
    rest = ((angle - turns * 1.5703125) - turns * 4.837512969970703125e-4) - turns * 7.54978995489188216e-8
    square = rest * rest
    sine = ((-1.9515295891e-4 * square + 8.3321608736e-3) * square - 1.6666654611e-1) * square * rest + rest
    cosine = (
        ((2.443315711809948e-5 * square - 1.388731625493765e-3) * square + 4.166664568298827e-2) * square * square
        - 0.5 * square
        + 1.0
    )
    quadrant = turns - 4.0 * jnp.floor(turns * 0.25)
    odd = (quadrant == 1.0) | (quadrant == 3.0)
    sine, cosine = jnp.where(odd, cosine, sine), jnp.where(odd, sine, cosine)
    sine = jnp.where(quadrant >= 2.0, -sine, sine)
    cosine = jnp.where((quadrant == 1.0) | (quadrant == 2.0), -cosine, cosine)
    return sine, cosine


class EncGather:
    def __init__(self, place, buf, part, sems):
        self.place, self.buf, self.part = place, buf, part
        self.near_send, self.near_recv, self.far_send, self.far_recv, self.give_send, self.give_recv = sems

    def near(self, side, index, h):
        place = self.place
        slot = self.part(self.buf.at[place.ys[index], place.core], h)
        return remote(slot, slot, place.y_side[side], self.near_send.at[side, h], self.near_recv.at[side, h])

    def far(self, side, index):
        place = self.place
        slot = self.part(self.buf.at[place.ys[index], place.core], side)
        return remote(slot, slot, place.y_side[side], self.far_send.at[side], self.far_recv.at[side])

    def give(self, index, h, mine=True):
        place = self.place
        slot = self.part(self.buf.at[place.ys[index], place.core if mine else 1 - place.core], h)
        return remote(slot, slot, place.sibling, self.give_send.at[index, h], self.give_recv.at[index, h])

    def take(self, index):
        for h in range(2):
            self.give(index, h, mine=False).wait_recv()

    def start(self):
        for order in range(2):
            for side in range(2):
                self.near(side, 0, side if order == 0 else 1 - side).start()
        for h in range(2):
            self.give(0, h).start()

    def run(self, work):
        self.take(0)
        work(self.place.ys[0])
        for side in range(2):
            self.near(side, 1 + side, side).wait_recv()
            self.far(side, 1 + side).start()
            self.give(1 + side, side).start()
        for side in range(2):
            self.near(side, 1 + side, 1 - side).wait_recv()
            self.give(1 + side, 1 - side).start()
        for side in range(2):
            self.take(1 + side)
            work(self.place.ys[1 + side])
        for side in range(2):
            self.far(side, 3).wait_recv()
            self.give(3, side).start()
        self.take(3)
        work(self.place.ys[3])

    def drain(self):
        for side in range(2):
            for h in range(2):
                self.near(side, 0, h).wait_send()
            self.far(side, 1 + side).wait_send()
        for index in range(4):
            for h in range(2):
                self.give(index, h).wait_send()


class Place:
    def __init__(self, ny, nz, nx):
        e = lax.axis_index("enc")
        s = lax.axis_index("seq")
        self.e, self.s = e, s
        self.core, self.y = lax.rem(e, 2), lax.div(e, 2)
        self.z, self.x = lax.div(s, nx), lax.rem(s, nx)
        up, down = wrap(self.y + 1, ny), wrap(self.y - 1, ny)
        self.ys = (self.y, down, up, wrap(self.y + 2, ny))
        self.y_side = ((up * 2 + self.core, s), (down * 2 + self.core, s))
        self.sibling = (e + 1 - 2 * self.core, s)
        self.x_side = tuple((e, self.z * nx + wrap(self.x + d, nx)) for d in (1, -1))
        self.z_side = tuple((e, wrap(self.z + d, nz) * nx + self.x) for d in (1, -1))
        self.cols = (self.x, wrap(self.x - 1, nx), wrap(self.x + 1, nx), wrap(self.x + 2, nx))


class PlaneAttention:
    def __init__(self, place, kv, q3, mx, den, acc, sems, nz, nx):
        self.place, self.kv, self.q3, self.mx, self.den, self.acc, self.nz, self.nx = place, kv, q3, mx, den, acc, nz, nx
        self.xs, self.xr, self.hs, self.hr, self.zs, self.zr, self.ss, self.sr = sems
        self.far = nz // 2
        self.half = kv.shape[3]
        self.rows = 2 * self.half
        self.heads = q3.shape[0] // self.rows
        self.group = min(2, self.heads) * self.rows

    def along_x(self, j, side, i):
        place = self.place
        slot = self.kv.at[self.row_at(j), place.core, place.cols[i]]
        return remote(slot, slot, place.x_side[side], self.xs.at[j, side], self.xr.at[j, side])

    def half_on(self, j, side, i):
        place = self.place
        part = pl.ds(side * (self.half // 2), self.half // 2)
        slot = self.kv.at[self.row_at(j), place.core, place.cols[i], part]
        return remote(slot, slot, place.x_side[side], self.hs.at[j, side], self.hr.at[j, side])

    def along_z(self, j, side, i, k):
        place = self.place
        slot = self.kv.at[self.row_at(j), place.core, place.cols[i]]
        at = 4 * (k - 1) + i
        return remote(slot, slot, place.z_side[side], self.zs.at[side, at], self.zr.at[side, at])

    def half_along_z(self, j, side):
        place = self.place
        slot = self.kv.at[self.row_at(j), place.core, place.x, pl.ds(side * (self.half // 2), self.half // 2)]
        at = 4 * (self.far - 1)
        return remote(slot, slot, place.z_side[side], self.zs.at[side, at], self.zr.at[side, at])

    def give(self, j, mine=True):
        place = self.place
        slot = self.kv.at[self.row_at(j), place.core if mine else 1 - place.core]
        return remote(slot, slot, place.sibling, self.ss.at[j], self.sr.at[j])

    def row_at(self, j):
        k = (j + 1) // 2
        return wrap(self.place.z - k, self.nz) if j % 2 == 1 else wrap(self.place.z + k, self.nz)

    def ring_rows(self, k):
        far = self.far
        return [] if not 0 <= k <= far else [0] if k == 0 else [2 * k - 1] if k == far else [2 * k - 1, 2 * k]

    def comes(self, side, k):
        z = self.place.z
        return z >= k if side == 0 else wrap(z + k, self.nz) < self.far

    def goes(self, side, k):
        z = self.place.z
        if side == 0:
            return (z >= k - 1) & (z <= self.nz - 2)
        return wrap(z + k - 1, self.nz) < self.far

    def needed(self, j):
        k = (j + 1) // 2
        z = self.place.z
        return z >= k if j % 2 == 1 else z + k >= self.nz if j else z >= 0

    def start(self):
        for side in range(2):
            self.along_x(0, side, 0).start()

            @pl.when(self.goes(side, 1))
            def _(side=side):
                self.along_z(0, side, 0, 1).start()

    def attend(self, high, low, v, restrict, fresh=False):
        stacked = jnp.concatenate([high, low, high], axis=0)
        pieces = stacked.shape[1] // HD
        parts = [slice(i, i + self.group) for i in range(0, self.heads * self.rows, self.group)]
        scores = [jnp.dot(self.q3[at], stacked, preferred_element_type=jnp.float32) for at in parts]
        for at, score in zip(parts, scores):
            if restrict is not None:
                score = jnp.concatenate([restrict(i, score[:, i * HD : (i + 1) * HD]) for i in range(pieces)], axis=1)
            top = jnp.max(score, axis=1, keepdims=True)
            new = jnp.broadcast_to(top, (self.group, HD)) if fresh else jnp.maximum(self.mx[at], top)
            weights = jnp.exp2(score - jnp.concatenate([new] * pieces, axis=1))
            summed = weights[:, :HD]
            for g in range(1, pieces):
                summed = summed + weights[:, g * HD : (g + 1) * HD]
            product = jnp.dot(weights.astype(jnp.bfloat16), v, preferred_element_type=jnp.float32)
            if fresh:
                self.den[at] = summed
                self.acc[at] = product
            else:
                factor = jnp.exp2(self.mx[at] - new)
                self.den[at] = self.den[at] * factor + summed
                self.acc[at] = self.acc[at] * factor + product
            self.mx[at] = new

    def compute(self, row, c, restrict=None):
        block = self.kv[row, c]
        high = jnp.concatenate([block[i, :, :HD] for i in range(self.nx)], axis=1)
        low = jnp.concatenate([block[i, :, HD : 2 * HD] for i in range(self.nx)], axis=1)
        self.attend(high, low, block[:, :, 2 * HD :].reshape(self.nx * self.half, HD), restrict)

    def own_shard(self, key_high, key_low, value):
        shape = (self.group, HD)
        token = lax.broadcasted_iota(jnp.int32, shape, 0) & (self.rows - 1)
        ahead = lax.broadcasted_iota(jnp.int32, shape, 1) - token
        self.attend(key_high, key_low, value, lambda i, piece: jnp.where(ahead <= -i * HD, piece, NEG), fresh=True)

    def own_row(self, c):
        x = self.place.x

        @pl.when(x > 0)
        def _():
            self.compute(self.place.z, c, lambda i, piece: jnp.where(i < x, piece, NEG))

    def far_rows(self, k, c):
        def step(i, carry):
            row = wrap(self.place.z + k * (2 * i - 1), self.nz)

            @pl.when(row < self.place.z)
            def _():
                self.compute(row, c)

            return carry

        lax.fori_loop(0, len(self.ring_rows(k)), step, 0)

    def pass_rows(self, k, chosen):
        far = self.far
        if not 1 <= k <= far:
            return
        for side in range(2):
            j = min(2 * k - 1 + side, 2 * far - 1)
            mine = [i for i in chosen if k < far or i // 2 == side]
            onward = [i for i in chosen if k + 1 < far or (k + 1 == far and i // 2 == side)]

            @pl.when(self.comes(side, k))
            def _(side=side, j=j, mine=mine):
                for i in mine:
                    self.along_z(j, side, i, k).wait_recv()

            if onward:
                @pl.when(self.goes(side, k + 1))
                def _(side=side, j=j, onward=onward):
                    for i in onward:
                        self.along_z(j, side, i, k + 1).start()

    def early(self, t):
        far = self.far

        @pl.when(self.place.core == 0)
        def _():
            if t == 1:
                for side in range(2):
                    self.along_x(0, side, 1 + side).wait_recv()
                    self.half_on(0, side, 1 + side).start()
                    for direction in range(2):
                        @pl.when(self.goes(direction, 1))
                        def _(side=side, direction=direction):
                            self.along_z(0, direction, 1 + side, 1).start()
            self.pass_rows(t - 2, (0, 1))

        @pl.when(self.place.core == 1)
        def _():
            if 1 <= t <= far:
                for side in range(2):
                    j = min(2 * t - 1 + side, 2 * far - 1)

                    @pl.when(self.comes(side, t))
                    def _(side=side, j=j):
                        if t < far:
                            self.along_z(j, side, 0, t).wait_recv()
                        else:
                            self.half_along_z(j, side).wait_recv()

                    if t < far:
                        @pl.when(self.goes(side, t + 1))
                        def _(side=side, j=j):
                            if t + 1 < far:
                                self.along_z(j, side, 0, t + 1).start()
                            else:
                                self.half_along_z(j, side).start()
                for j in self.ring_rows(t):
                    @pl.when(self.needed(j))
                    def _(j=j):
                        for side in range(2):
                            self.along_x(j, side, 0).start()
            for j in self.ring_rows(t - 1):
                @pl.when(self.needed(j))
                def _(j=j):
                    for side in range(2):
                        self.along_x(j, side, 1 + side).wait_recv()
                        self.half_on(j, side, 1 + side).start()

        for j in self.ring_rows(t - 3):
            @pl.when(self.needed(j))
            def _(j=j):
                self.give(j, mine=False).wait_recv()

    def late(self, t):
        @pl.when(self.place.core == 0)
        def _():
            if t == 2:
                for side in range(2):
                    self.half_on(0, side, 3).wait_recv()
                for direction in range(2):
                    @pl.when(self.goes(direction, 1))
                    def _(direction=direction):
                        self.along_z(0, direction, 3, 1).start()
            self.pass_rows(t - 2, (2, 3))

        for j in self.ring_rows(t - 2):
            @pl.when(self.needed(j))
            def _(j=j):
                @pl.when(self.place.core == 1)
                def _():
                    for side in range(2):
                        self.half_on(j, side, 3).wait_recv()

                self.give(j).start()

    def run(self):
        core, far = self.place.core, self.far
        for t in range(1, far + 4):
            self.early(t)
            if t == 3:
                self.own_row(1 - core)
            elif t > 3:
                self.far_rows(t - 3, 1 - core)
            self.late(t)
            if t == 2:
                self.own_row(core)
            elif 3 <= t <= far + 2:
                self.far_rows(t - 2, core)

    def result(self, h):
        at = slice(h * self.rows, (h + 1) * self.rows)
        return self.acc[at] / jnp.sum(self.den[at], axis=1, keepdims=True)

    def drain(self):
        far = self.far
        for side in range(2):
            self.along_x(0, side, 0).wait_send()
            self.half_on(0, side, 1 + side).wait_send()
        for j in range(2 * far):
            @pl.when(self.needed(j))
            def _(j=j):
                self.give(j).wait_send()

                @pl.when((self.place.core == 1) & (j > 0))
                def _():
                    for side in range(2):
                        self.along_x(j, side, 0).wait_send()
                        self.half_on(j, side, 1 + side).wait_send()

        for side in range(2):
            for k in range(1, far + 1):
                @pl.when(self.goes(side, k))
                def _(side=side, k=k):
                    j = 0 if k == 1 else 2 * k - 3 + side

                    @pl.when(self.place.core == 0)
                    def _():
                        for i in range(4):
                            if k < far or i // 2 == side:
                                self.along_z(j, side, i, k).wait_send()

                    @pl.when(self.place.core == 1)
                    def _():
                        if k < far:
                            self.along_z(j, side, 0, k).wait_send()
                        else:
                            self.half_along_z(j, side).wait_send()


def prefill(
    patches, gain, up_t, up_bias, merge_down, down_bias, text, lengths, offsets, input_gain, qkv_weight, qkv_bias, freq,
    ny, nz, nx,
):
    patch_rows, vision = patches.shape
    units, joined = up_t.shape
    part = patch_rows // 4
    pad = -(-part // 16) * 16
    blocks = 2 * ny
    groups = nz * nx
    slots = groups * LMAX
    rows, width = text.shape
    half = rows // 2
    model = merge_down.shape[1]
    query_width = qkv_weight.shape[1] - HD
    heads = query_width // HD
    far = nz // 2

    def kernel(
        p_ref, g_ref, up_hbm, ub_ref, down_hbm, db_ref, text_ref, len_s, off_s, len_v, off_v, gain_ref, qkv_hbm, qb_ref,
        freq_ref, o_ref,
        buf, turned, up, hid, out, inn, down, w_q, w_kv, kv_bias, sib_out, sib_in, own, rel_out, rel_in, d_out, d_in,
        full, squares, normed, kv, q3, mx, den, acc,
        w_sem, c_send, c_recv, a_send, a_recv, p_send, p_recv, r_send, r_recv, d_send, d_recv,
        fns, fnr, ffs, ffr, fgs, fgr, bns, bnr, bfs, bfr, bgs, bgr,
        xs, xr, hs, hr, zs, zr, ss, sr,
    ):
        place = Place(ny, nz, nx)
        qkv_bias_row = qb_ref[...].reshape(1, query_width + HD)
        input_gain_row = gain_ref[...].reshape(1, model)
        e, s, core, z, x = place.e, place.s, place.core, place.z, place.x

        kv_at = pl.ds(pl.multiple_of(core * HD, HD), HD)
        other_at = pl.ds(pl.multiple_of((1 - core) * HD, HD), HD)
        query_at, rest_at = pl.ds(0, query_width), pl.ds(query_width, HD)
        loads = (
            pltpu.make_async_copy(up_hbm, turned, w_sem.at[0]),
            pltpu.make_async_copy(down_hbm, down, w_sem.at[1]),
            pltpu.make_async_copy(qkv_hbm.at[:, rest_at], w_kv.at[:, kv_at], w_sem.at[2]),
            pltpu.make_async_copy(qkv_hbm.at[:, query_at], w_q, w_sem.at[3]),
        )
        for load in loads:
            load.start()
        barrier = pltpu.get_barrier_semaphore()

        def greet(p, carry):
            pl.semaphore_signal(barrier, inc=1, device_id=(e, wrap(s + p, groups)), device_id_type=MESH)
            return carry

        lax.fori_loop(1, groups, greet, 0)
        for other in (*place.y_side, place.sibling):
            pl.semaphore_signal(barrier, inc=1, device_id=other, device_id_type=MESH)

        front = EncGather(place, buf, lambda block, h: block.at[pl.ds(2 * h, 2)], (fns, fnr, ffs, ffr, fgs, fgr))
        values = p_ref[...].astype(jnp.float32)
        mean_square = jnp.mean(values * values, axis=1, keepdims=True)
        vision_rows = (values * lax.rsqrt(mean_square + EPSILON) * g_ref[...].reshape(1, vision)).astype(jnp.bfloat16)
        to = lax.broadcasted_iota(jnp.int32, (4 * pad, patch_rows), 0)
        source = lax.broadcasted_iota(jnp.int32, (4 * pad, patch_rows), 1)
        moved = (source == 4 * (to % pad) + to // pad) & (to % pad < part)
        order = jnp.where(moved, 1.0, 0.0).astype(jnp.bfloat16)
        sorted_rows = jnp.dot(order, vision_rows, preferred_element_type=jnp.float32).astype(jnp.bfloat16)
        for q in range(4):
            buf[place.y, core, q] = sorted_rows[q * pad : (q + 1) * pad]
        pl.semaphore_wait(barrier, groups - 1 + 3)
        front.start()
        kv_columns = remote(
            qkv_hbm.at[:, rest_at], w_kv.at[:, kv_at], place.sibling, c_send.at[0], c_recv.at[0]
        )
        kv_columns.start()
        kv_bias[core] = qkv_bias_row[:, query_width:]
        bias_columns = remote(kv_bias.at[core], kv_bias.at[core], place.sibling, c_send.at[1], c_recv.at[1])
        bias_columns.start()

        loads[0].wait()
        if joined % 512 == 0:
            def turn(i, carry):
                at = pl.ds(pl.multiple_of(i * 512, 512), 512)
                up[at, :] = turned[:, at].T
                return carry

            lax.fori_loop(0, joined // 512, turn, 0)
        else:
            up[...] = turned[...].T

        lane = lax.broadcasted_iota(jnp.int32, (1, blocks * pad), 1)
        merged = jnp.where(lane % pad < part, lane // pad * part + lane % pad, -1)
        code = jnp.full((1, blocks * pad), -1, jnp.int32)
        begin = jnp.int32(0)
        for j in range(len_s.shape[0]):
            end = begin + len_s[j, s]
            inside = (merged >= begin) & (merged < end)
            code = jnp.where(inside, off_s[j, s] // rows * LMAX + merged - begin, code)
            begin = end
        slot = lax.broadcasted_iota(jnp.int32, (slots, blocks * pad), 0)
        pick = jnp.where(slot == code, 1.0, 0.0).astype(jnp.bfloat16)

        ours = off_v[...] // rows == s
        first = jnp.sum(jnp.where(ours, off_v[...] - s * rows, 0).astype(jnp.float32), axis=0, keepdims=True)
        count = jnp.sum(jnp.where(ours, len_v[...], 0).astype(jnp.float32), axis=0, keepdims=True)
        group = lax.broadcasted_iota(jnp.int32, (groups, slots), 0)
        position = lax.broadcasted_iota(jnp.int32, (groups, slots), 1)
        spread_groups = jnp.where(position // LMAX == group, 1.0, 0.0).astype(jnp.bfloat16)
        both = jnp.concatenate([jnp.broadcast_to(first, (8, groups)), jnp.broadcast_to(count, (8, groups))], axis=0)
        both = jnp.dot(both.astype(jnp.bfloat16), spread_groups, preferred_element_type=jnp.float32)
        index = (lax.broadcasted_iota(jnp.int32, (1, slots), 1) % LMAX).astype(jnp.float32)
        target = jnp.where(index < both[8:9], both[:1] + index, -1.0)
        token = lax.broadcasted_iota(jnp.int32, (rows, slots), 0).astype(jnp.float32)
        placing = jnp.where(token == target, 1.0, 0.0)
        covered = jnp.sum(placing, axis=1, keepdims=True) > 0.5

        def merge(y):
            grouped = jnp.concatenate([buf[y, :, q].reshape(2 * pad, vision) for q in range(4)], axis=1)
            inner = jnp.dot(grouped, up[...], preferred_element_type=jnp.float32) + ub_ref[...].reshape(1, units)
            inner = 0.5 * inner * (1.0 + lax.erf(inner * math.sqrt(0.5)))
            hid[y] = inner.astype(jnp.bfloat16)

        front.run(merge)

        chosen = jnp.dot(pick, hid[...].reshape(blocks * pad, units), preferred_element_type=jnp.float32)
        out[...] = chosen.astype(jnp.bfloat16).reshape(groups, LMAX, units)

        def swap(p, at, arrives):
            return remote(out.at[at], inn.at[arrives], (e, at), a_send.at[p], a_recv.at[p])

        def begin_swap(p, carry):
            swap(p, wrap(s + p, groups), s).start()
            return carry

        lax.fori_loop(1, groups, begin_swap, 0)
        inn[s] = out[s]
        loads[1].wait()

        def end_swap(p, carry):
            swap(p, wrap(s + p, groups), wrap(s - p + groups, groups)).wait()
            return carry

        lax.fori_loop(1, groups, end_swap, 0)
        placed = jnp.dot(
            placing.astype(jnp.bfloat16), inn[...].reshape(slots, units), preferred_element_type=jnp.float32
        ).astype(jnp.bfloat16)

        targets = (place.ys[3], place.ys[2], place.ys[1], place.y)

        def share(y_to, c_to):
            start = pl.multiple_of((y_to * 2 + c_to) * width, width)
            return jnp.dot(placed, down[:, pl.ds(start, width)], preferred_element_type=jnp.float32)

        def pair(i):
            return remote(sib_out.at[i], sib_in.at[i], place.sibling, p_send.at[i], p_recv.at[i])

        def relay(side):
            return remote(rel_out.at[side], rel_in.at[side], place.y_side[side], r_send.at[side], r_recv.at[side])

        def deliver(side, h):
            return remote(
                d_out.at[side, h], d_in.at[side, h], place.y_side[side], d_send.at[side, h], d_recv.at[side, h]
            )

        halves = (slice(0, half), slice(half, rows))
        for i in range(4):
            sib_out[i] = share(targets[i], 1 - core).astype(jnp.bfloat16)
            pair(i).start()
        for i in range(4):
            own[i] = share(targets[i], core)
        pair(0).wait_recv()
        for side in range(2):
            at = halves[side]
            rel_out[side] = (own[0, at] + sib_in[0, at].astype(jnp.float32)).astype(jnp.bfloat16)
            relay(side).start()
        for side in range(2):
            pair(1 + side).wait_recv()
            own[1 + side] = own[1 + side] + sib_in[1 + side].astype(jnp.float32)
            d_out[side, 1 - side] = own[1 + side, halves[1 - side]].astype(jnp.bfloat16)
            deliver(side, 1 - side).start()
        pair(3).wait_recv()
        own[3] = own[3] + sib_in[3].astype(jnp.float32) + db_ref[...].reshape(1, width)
        for side in range(2):
            relay(side).wait_recv()
            d_out[side, side] = (own[1 + side, halves[side]] + rel_in[side].astype(jnp.float32)).astype(jnp.bfloat16)
            deliver(side, side).start()

        token_id = lax.broadcasted_iota(jnp.int32, (rows, HD), 0) + s * rows
        sine, cosine = sine_cosine(token_id.astype(jnp.float32) * freq_ref[...])
        signed = jnp.where(lax.broadcasted_iota(jnp.int32, (rows, HD), 1) < HD // 2, -sine, sine)

        def rotate(block):
            return block * cosine + pltpu.roll(block, HD // 2, 1) * signed

        back = EncGather(place, full, lambda block, h: block.at[pl.ds(h * half, half)], (bns, bnr, bfs, bfr, bgs, bgr))
        for h in range(2):
            at = halves[h]
            total = own[3, at]
            for side in range(2):
                deliver(side, h).wait_recv()
                total = total + d_in[side, h].astype(jnp.float32)
            kept = jnp.where(covered[at], total, text_ref[at].astype(jnp.float32))
            full[place.y, core, at] = kept.astype(jnp.bfloat16)
        back.start()
        squares[...] = jnp.zeros(squares.shape, jnp.float32)

        def add_squares(y):
            for c in range(2):
                block = full[y, c].astype(jnp.float32)
                block = block * block
                for g in range(width // HD):
                    squares[...] += block[:, g * HD : (g + 1) * HD]

        back.run(add_squares)

        scale = lax.rsqrt(jnp.sum(squares[...], axis=1, keepdims=True) * (1.0 / model) + EPSILON)
        for block in range(blocks):
            at = slice(block * width, (block + 1) * width)
            normed[:, at] = (full[block // 2, block % 2].astype(jnp.float32) * scale * input_gain_row[:, at]).astype(
                jnp.bfloat16
            )
        loads[2].wait()
        remote(
            qkv_hbm.at[:, rest_at], w_kv.at[:, other_at], place.sibling, c_send.at[0], c_recv.at[0]
        ).wait_recv()
        remote(kv_bias.at[core], kv_bias.at[1 - core], place.sibling, c_send.at[1], c_recv.at[1]).wait_recv()
        both = jnp.dot(normed[...], w_kv[...], preferred_element_type=jnp.float32)
        key = rotate(both[:, :HD] + kv_bias[0]).T
        key_high = key.astype(jnp.bfloat16)
        key_low = (key - key_high.astype(jnp.float32)).astype(jnp.bfloat16)
        value = (both[:, HD:] + kv_bias[1]).astype(jnp.bfloat16)

        for c in range(2):
            @pl.when(core == c)
            def _(c=c):
                kv[z, c, x, :, :HD] = key_high[:, halves[c]]
                kv[z, c, x, :, HD : 2 * HD] = key_low[:, halves[c]]
                kv[z, c, x, :, 2 * HD :] = value[halves[c]]

        plane = PlaneAttention(place, kv, q3, mx, den, acc, (xs, xr, hs, hr, zs, zr, ss, sr), nz, nx)
        plane.start()

        loads[3].wait()
        scaling = HD ** (-0.5) * math.log2(math.e)
        for pair_of in range(heads // 2):
            at = slice(pair_of * 2 * HD, (pair_of + 1) * 2 * HD)
            query = jnp.dot(normed[...], w_q[:, at], preferred_element_type=jnp.float32) + qkv_bias_row[:, at]
            for i in range(2):
                rows_of = slice((pair_of * 2 + i) * rows, (pair_of * 2 + i + 1) * rows)
                turned_query = rotate(query[:, i * HD : (i + 1) * HD]) * scaling
                high = turned_query.astype(jnp.bfloat16)
                q3[rows_of, :HD] = high
                q3[rows_of, HD : 2 * HD] = high
                q3[rows_of, 2 * HD :] = (turned_query - high.astype(jnp.float32)).astype(jnp.bfloat16)

        plane.own_shard(key_high, key_low, value)
        plane.run()
        for h in range(heads):
            o_ref[:, h * HD : (h + 1) * HD] = plane.result(h).astype(o_ref.dtype)

        front.drain()
        back.drain()
        kv_columns.wait_send()
        bias_columns.wait_send()
        for i in range(4):
            pair(i).wait_send()
        for side in range(2):
            relay(side).wait_send()
            for h in range(2):
                deliver(side, h).wait_send()
        plane.drain()

    dma = pltpu.SemaphoreType.DMA
    bf16, f32 = jnp.bfloat16, jnp.float32
    vmem = pl.BlockSpec(memory_space=pltpu.VMEM)
    smem = pl.BlockSpec(memory_space=pltpu.SMEM)
    any_space = pl.BlockSpec(memory_space=pl.ANY)
    enc_sems = [dma((2, 2)), dma((2, 2)), dma((2,)), dma((2,)), dma((4, 2)), dma((4, 2))]
    return pl.pallas_call(
        kernel,
        out_shape=jax.ShapeDtypeStruct((rows, query_width), bf16),
        in_specs=[
            vmem, vmem, any_space, vmem, any_space, vmem, vmem, smem, smem, vmem, vmem, vmem, any_space, vmem, vmem,
        ],
        out_specs=vmem,
        scratch_shapes=[
            pltpu.VMEM((ny, 2, 4, pad, vision), bf16),
            pltpu.VMEM((units, joined), bf16),
            pltpu.VMEM((joined, units), bf16),
            pltpu.VMEM((ny, 2 * pad, units), bf16),
            pltpu.VMEM((groups, LMAX, units), bf16),
            pltpu.VMEM((groups, LMAX, units), bf16),
            pltpu.VMEM(merge_down.shape, bf16),
            pltpu.VMEM((model, query_width), bf16),
            pltpu.VMEM((model, 2 * HD), bf16),
            pltpu.VMEM((2, 1, HD), f32),
            pltpu.VMEM((4, rows, width), bf16),
            pltpu.VMEM((4, rows, width), bf16),
            pltpu.VMEM((4, rows, width), f32),
            pltpu.VMEM((2, half, width), bf16),
            pltpu.VMEM((2, half, width), bf16),
            pltpu.VMEM((2, 2, half, width), bf16),
            pltpu.VMEM((2, 2, half, width), bf16),
            pltpu.VMEM((ny, 2, rows, width), bf16),
            pltpu.VMEM((rows, HD), f32),
            pltpu.VMEM((rows, model), bf16),
            pltpu.VMEM((nz, 2, nx, half, 3 * HD), bf16),
            pltpu.VMEM((heads * rows, 3 * HD), bf16),
            pltpu.VMEM((heads * rows, HD), f32),
            pltpu.VMEM((heads * rows, HD), f32),
            pltpu.VMEM((heads * rows, HD), f32),
            dma((4,)),
            dma((2,)),
            dma((2,)),
            dma((groups,)),
            dma((groups,)),
            dma((4,)),
            dma((4,)),
            dma((2,)),
            dma((2,)),
            dma((2, 2)),
            dma((2, 2)),
            *enc_sems,
            *enc_sems,
            dma((nz, 2)),
            dma((nz, 2)),
            dma((nz, 2)),
            dma((nz, 2)),
            dma((2, 4 * far)),
            dma((2, 4 * far)),
            dma((nz,)),
            dma((nz,)),
        ],
        compiler_params=pltpu.CompilerParams(
            collective_id=1, has_side_effects=True, vmem_limit_bytes=56 * 1024 * 1024
        ),
        name="prefill",
    )(
        patches, gain, up_t, up_bias, merge_down, down_bias, text, lengths, offsets, lengths, offsets, input_gain,
        qkv_weight, qkv_bias, freq,
    )


def local(
    patches, vision_gain, merge_up, merge_up_bias, merge_down, merge_down_bias, text_embed, image_lengths, image_offsets,
    input_gain, qkv_weight, qkv_bias,
):
    freq = np.exp(np.arange(HD // 2) * (-2.0 * np.log(THETA) / HD)).astype(np.float32)
    return prefill(
        patches[0], vision_gain, merge_up.T, merge_up_bias, merge_down, merge_down_bias, text_embed,
        image_lengths.T, image_offsets.T, input_gain, qkv_weight, qkv_bias,
        jnp.asarray(np.concatenate([freq, freq])[None]),
        lax.axis_size("enc") // 2, lax.axis_size("seq") // NX, NX,
    )


def solution(mesh):
    in_specs = (
        P("seq", "enc", None),
        P(),
        P(None, "enc"),
        P("enc"),
        P("enc", None),
        P("enc"),
        P("seq", "enc"),
        P(),
        P(),
        P(),
        P(None, "enc"),
        P("enc"),
    )
    out_specs = P("seq", "enc")
    return jax.shard_map(local, mesh=mesh, in_specs=in_specs, out_specs=out_specs, check_vma=False)
```

```python
import math

import jax
import jax.numpy as jnp
import numpy as np
from jax import lax
from jax.experimental import pallas as pl
from jax.experimental.pallas import tpu as pltpu
from jax.sharding import PartitionSpec as P

HD = 128
LMAX = 16
NX = 4
EPSILON = 1e-06
THETA = 1000000.0
NEG = -1e30
MESH = pl.DeviceIdType.MESH


def wrap(value, size):
    return lax.rem(value + 2 * size, size)


def remote(src, dst, to, send_sem, recv_sem):
    return pltpu.make_async_remote_copy(
        src_ref=src, dst_ref=dst, send_sem=send_sem, recv_sem=recv_sem, device_id=to, device_id_type=MESH
    )


def sine_cosine(angle):
    turns = jnp.floor(angle * (2.0 / math.pi) + 0.5)
    rest = ((angle - turns * 1.5703125) - turns * 4.837512969970703125e-4) - turns * 7.54978995489188216e-8
    square = rest * rest
    sine = ((-1.9515295891e-4 * square + 8.3321608736e-3) * square - 1.6666654611e-1) * square * rest + rest
    cosine = (
        ((2.443315711809948e-5 * square - 1.388731625493765e-3) * square + 4.166664568298827e-2) * square * square
        - 0.5 * square
        + 1.0
    )
    quadrant = turns - 4.0 * jnp.floor(turns * 0.25)
    odd = (quadrant == 1.0) | (quadrant == 3.0)
    sine, cosine = jnp.where(odd, cosine, sine), jnp.where(odd, sine, cosine)
    sine = jnp.where(quadrant >= 2.0, -sine, sine)
    cosine = jnp.where((quadrant == 1.0) | (quadrant == 2.0), -cosine, cosine)
    return sine, cosine


class EncGather:
    def __init__(self, place, buf, part, sems):
        self.place, self.buf, self.part = place, buf, part
        self.near_send, self.near_recv, self.far_send, self.far_recv, self.give_send, self.give_recv = sems

    def near(self, side, index, h):
        place = self.place
        slot = self.part(self.buf.at[place.ys[index], place.core], h)
        return remote(slot, slot, place.y_side[side], self.near_send.at[side, h], self.near_recv.at[side, h])

    def far(self, side, index):
        place = self.place
        slot = self.part(self.buf.at[place.ys[index], place.core], side)
        return remote(slot, slot, place.y_side[side], self.far_send.at[side], self.far_recv.at[side])

    def give(self, index, h, mine=True):
        place = self.place
        slot = self.part(self.buf.at[place.ys[index], place.core if mine else 1 - place.core], h)
        return remote(slot, slot, place.sibling, self.give_send.at[index, h], self.give_recv.at[index, h])

    def take(self, index):
        for h in range(2):
            self.give(index, h, mine=False).wait_recv()

    def start(self, h):
        for side in range(2):
            self.near(side, 0, h).start()
        self.give(0, h).start()

    def relay(self):
        for side in range(2):
            self.near(side, 1 + side, side).wait_recv()
            self.far(side, 1 + side).start()
            self.give(1 + side, side).start()

    def finish_near(self):
        for side in range(2):
            self.near(side, 1 + side, 1 - side).wait_recv()
            self.give(1 + side, 1 - side).start()

    def finish_far(self):
        for side in range(2):
            self.far(side, 3).wait_recv()
            self.give(3, side).start()

    def drain(self):
        for side in range(2):
            for h in range(2):
                self.near(side, 0, h).wait_send()
            self.far(side, 1 + side).wait_send()
        for index in range(4):
            for h in range(2):
                self.give(index, h).wait_send()


class Place:
    def __init__(self, ny, nz, nx):
        e = lax.axis_index("enc")
        s = lax.axis_index("seq")
        self.e, self.s = e, s
        self.core, self.y = lax.rem(e, 2), lax.div(e, 2)
        self.z, self.x = lax.div(s, nx), lax.rem(s, nx)
        up, down = wrap(self.y + 1, ny), wrap(self.y - 1, ny)
        self.ys = (self.y, down, up, wrap(self.y + 2, ny))
        self.y_side = ((up * 2 + self.core, s), (down * 2 + self.core, s))
        self.sibling = (e + 1 - 2 * self.core, s)
        self.x_side = tuple((e, self.z * nx + wrap(self.x + d, nx)) for d in (1, -1))
        self.z_side = tuple((e, wrap(self.z + d, nz) * nx + self.x) for d in (1, -1))
        self.cols = (self.x, wrap(self.x - 1, nx), wrap(self.x + 1, nx), wrap(self.x + 2, nx))


class PlaneAttention:
    def __init__(self, place, kv, q3, mx, den, acc, sems, nz, nx):
        self.place, self.kv, self.q3, self.mx, self.den, self.acc, self.nz, self.nx = place, kv, q3, mx, den, acc, nz, nx
        self.xs, self.xr, self.hs, self.hr, self.zs, self.zr, self.ss, self.sr = sems
        self.far = nz // 2
        self.half = kv.shape[3]
        self.rows = 2 * self.half
        self.heads = q3.shape[0] // self.rows
        self.group = min(2, self.heads) * self.rows

    def along_x(self, j, side, i):
        place = self.place
        slot = self.kv.at[self.row_at(j), place.core, place.cols[i]]
        return remote(slot, slot, place.x_side[side], self.xs.at[j, side], self.xr.at[j, side])

    def half_on(self, j, side, i):
        place = self.place
        part = pl.ds(side * (self.half // 2), self.half // 2)
        slot = self.kv.at[self.row_at(j), place.core, place.cols[i], part]
        return remote(slot, slot, place.x_side[side], self.hs.at[j, side], self.hr.at[j, side])

    def along_z(self, j, side, i, k):
        place = self.place
        slot = self.kv.at[self.row_at(j), place.core, place.cols[i]]
        at = 4 * (k - 1) + i
        return remote(slot, slot, place.z_side[side], self.zs.at[side, at], self.zr.at[side, at])

    def half_along_z(self, j, side):
        place = self.place
        slot = self.kv.at[self.row_at(j), place.core, place.x, pl.ds(side * (self.half // 2), self.half // 2)]
        at = 4 * (self.far - 1)
        return remote(slot, slot, place.z_side[side], self.zs.at[side, at], self.zr.at[side, at])

    def give(self, j, mine=True):
        place = self.place
        slot = self.kv.at[self.row_at(j), place.core if mine else 1 - place.core]
        return remote(slot, slot, place.sibling, self.ss.at[j], self.sr.at[j])

    def row_at(self, j):
        k = (j + 1) // 2
        return wrap(self.place.z - k, self.nz) if j % 2 == 1 else wrap(self.place.z + k, self.nz)

    def ring_rows(self, k):
        far = self.far
        return [] if not 0 <= k <= far else [0] if k == 0 else [2 * k - 1] if k == far else [2 * k - 1, 2 * k]

    def comes(self, side, k):
        z = self.place.z
        return z >= k if side == 0 else wrap(z + k, self.nz) < self.far

    def goes(self, side, k):
        z = self.place.z
        if side == 0:
            return (z >= k - 1) & (z <= self.nz - 2)
        return wrap(z + k - 1, self.nz) < self.far

    def needed(self, j):
        k = (j + 1) // 2
        z = self.place.z
        return z >= k if j % 2 == 1 else z + k >= self.nz if j else z >= 0

    def start(self):
        for side in range(2):
            self.along_x(0, side, 0).start()

            @pl.when(self.goes(side, 1))
            def _(side=side):
                self.along_z(0, side, 0, 1).start()

    def attend(self, high, low, v, restrict, fresh=False):
        stacked = jnp.concatenate([high, low, high], axis=0)
        pieces = stacked.shape[1] // HD
        parts = [slice(i, i + self.group) for i in range(0, self.heads * self.rows, self.group)]
        scores = [jnp.dot(self.q3[at], stacked, preferred_element_type=jnp.float32) for at in parts]
        for at, score in zip(parts, scores):
            if restrict is not None:
                score = jnp.concatenate([restrict(i, score[:, i * HD : (i + 1) * HD]) for i in range(pieces)], axis=1)
            top = jnp.max(score, axis=1, keepdims=True)
            new = jnp.broadcast_to(top, (self.group, HD)) if fresh else jnp.maximum(self.mx[at], top)
            weights = jnp.exp2(score - jnp.concatenate([new] * pieces, axis=1))
            summed = weights[:, :HD]
            for g in range(1, pieces):
                summed = summed + weights[:, g * HD : (g + 1) * HD]
            product = jnp.dot(weights.astype(jnp.bfloat16), v, preferred_element_type=jnp.float32)
            if fresh:
                self.den[at] = summed
                self.acc[at] = product
            else:
                factor = jnp.exp2(self.mx[at] - new)
                self.den[at] = self.den[at] * factor + summed
                self.acc[at] = self.acc[at] * factor + product
            self.mx[at] = new

    def compute(self, row, c, restrict=None):
        block = self.kv[row, c]
        high = jnp.concatenate([block[i, :, :HD] for i in range(self.nx)], axis=1)
        low = jnp.concatenate([block[i, :, HD : 2 * HD] for i in range(self.nx)], axis=1)
        self.attend(high, low, block[:, :, 2 * HD :].reshape(self.nx * self.half, HD), restrict)

    def own_shard(self, key_high, key_low, value):
        shape = (self.group, HD)
        token = lax.broadcasted_iota(jnp.int32, shape, 0) & (self.rows - 1)
        ahead = lax.broadcasted_iota(jnp.int32, shape, 1) - token
        self.attend(key_high, key_low, value, lambda i, piece: jnp.where(ahead <= -i * HD, piece, NEG), fresh=True)

    def own_row(self, c):
        x = self.place.x

        @pl.when(x > 0)
        def _():
            self.compute(self.place.z, c, lambda i, piece: jnp.where(i < x, piece, NEG))

    def far_rows(self, k, c):
        def step(i, carry):
            row = wrap(self.place.z + k * (2 * i - 1), self.nz)

            @pl.when(row < self.place.z)
            def _():
                self.compute(row, c)

            return carry

        lax.fori_loop(0, len(self.ring_rows(k)), step, 0)

    def pass_rows(self, k, chosen):
        far = self.far
        if not 1 <= k <= far:
            return
        for side in range(2):
            j = min(2 * k - 1 + side, 2 * far - 1)
            mine = [i for i in chosen if k < far or i // 2 == side]
            onward = [i for i in chosen if k + 1 < far or (k + 1 == far and i // 2 == side)]

            @pl.when(self.comes(side, k))
            def _(side=side, j=j, mine=mine):
                for i in mine:
                    self.along_z(j, side, i, k).wait_recv()

            if onward:
                @pl.when(self.goes(side, k + 1))
                def _(side=side, j=j, onward=onward):
                    for i in onward:
                        self.along_z(j, side, i, k + 1).start()

    def early(self, t):
        far = self.far

        @pl.when(self.place.core == 0)
        def _():
            if t == 1:
                for side in range(2):
                    self.along_x(0, side, 1 + side).wait_recv()
                    self.half_on(0, side, 1 + side).start()
                    for direction in range(2):
                        @pl.when(self.goes(direction, 1))
                        def _(side=side, direction=direction):
                            self.along_z(0, direction, 1 + side, 1).start()
            self.pass_rows(t - 2, (0, 1))

        @pl.when(self.place.core == 1)
        def _():
            if 1 <= t <= far:
                for side in range(2):
                    j = min(2 * t - 1 + side, 2 * far - 1)

                    @pl.when(self.comes(side, t))
                    def _(side=side, j=j):
                        if t < far:
                            self.along_z(j, side, 0, t).wait_recv()
                        else:
                            self.half_along_z(j, side).wait_recv()

                    if t < far:
                        @pl.when(self.goes(side, t + 1))
                        def _(side=side, j=j):
                            if t + 1 < far:
                                self.along_z(j, side, 0, t + 1).start()
                            else:
                                self.half_along_z(j, side).start()
                for j in self.ring_rows(t):
                    @pl.when(self.needed(j))
                    def _(j=j):
                        for side in range(2):
                            self.along_x(j, side, 0).start()
            for j in self.ring_rows(t - 1):
                @pl.when(self.needed(j))
                def _(j=j):
                    for side in range(2):
                        self.along_x(j, side, 1 + side).wait_recv()
                        self.half_on(j, side, 1 + side).start()

    def from_sibling(self, k):
        for j in self.ring_rows(k):
            @pl.when(self.needed(j))
            def _(j=j):
                self.give(j, mine=False).wait_recv()

    def late(self, t):
        @pl.when(self.place.core == 0)
        def _():
            if t == 2:
                for side in range(2):
                    self.half_on(0, side, 3).wait_recv()
                for direction in range(2):
                    @pl.when(self.goes(direction, 1))
                    def _(direction=direction):
                        self.along_z(0, direction, 3, 1).start()
            self.pass_rows(t - 2, (2, 3))

        for j in self.ring_rows(t - 2):
            @pl.when(self.needed(j))
            def _(j=j):
                @pl.when(self.place.core == 1)
                def _():
                    for side in range(2):
                        self.half_on(j, side, 3).wait_recv()

                self.give(j).start()

    def run(self):
        core, far = self.place.core, self.far
        for t in range(1, far + 4):
            self.early(t)
            if t > 3:
                self.from_sibling(t - 3)
                self.far_rows(t - 3, 1 - core)
            self.late(t)
            if t == 3:
                self.from_sibling(0)
                self.own_row(1 - core)
            if t == 2:
                self.own_row(core)
            elif 3 <= t <= far + 2:
                self.far_rows(t - 2, core)

    def result(self, h):
        at = slice(h * self.rows, (h + 1) * self.rows)
        return self.acc[at] / jnp.sum(self.den[at], axis=1, keepdims=True)

    def drain(self):
        far = self.far
        for side in range(2):
            self.along_x(0, side, 0).wait_send()
            self.half_on(0, side, 1 + side).wait_send()
        for j in range(2 * far):
            @pl.when(self.needed(j))
            def _(j=j):
                self.give(j).wait_send()

                @pl.when((self.place.core == 1) & (j > 0))
                def _():
                    for side in range(2):
                        self.along_x(j, side, 0).wait_send()
                        self.half_on(j, side, 1 + side).wait_send()

        for side in range(2):
            for k in range(1, far + 1):
                @pl.when(self.goes(side, k))
                def _(side=side, k=k):
                    j = 0 if k == 1 else 2 * k - 3 + side

                    @pl.when(self.place.core == 0)
                    def _():
                        for i in range(4):
                            if k < far or i // 2 == side:
                                self.along_z(j, side, i, k).wait_send()

                    @pl.when(self.place.core == 1)
                    def _():
                        if k < far:
                            self.along_z(j, side, 0, k).wait_send()
                        else:
                            self.half_along_z(j, side).wait_send()


def prefill(
    patches, gain, up_t, up_bias, merge_down, down_bias, text, lengths, offsets, input_gain, qkv_weight, qkv_bias, freq,
    ny, nz, nx,
):
    patch_rows, vision = patches.shape
    units, joined = up_t.shape
    part = patch_rows // 4
    pad = -(-part // 16) * 16
    blocks = 2 * ny
    groups = nz * nx
    slots = groups * LMAX
    rows, width = text.shape
    half = rows // 2
    model = merge_down.shape[1]
    query_width = qkv_weight.shape[1] - HD
    heads = query_width // HD
    far = nz // 2

    def kernel(
        p_ref, g_ref, up_hbm, ub_ref, down_hbm, db_ref, text_ref, len_s, off_s, len_v, off_v, gain_ref, qkv_hbm, qb_ref,
        freq_ref, o_ref,
        buf, turned, up, hid, out, inn, down, w_q, w_kv, kv_bias, sib_out, sib_in, own, rel_out, rel_in, d_out, d_in,
        full, squares, normed, kv, q3, mx, den, acc,
        w_sem, c_send, c_recv, a_send, a_recv, p_send, p_recv, r_send, r_recv, d_send, d_recv,
        fns, fnr, ffs, ffr, fgs, fgr, bns, bnr, bfs, bfr, bgs, bgr,
        xs, xr, hs, hr, zs, zr, ss, sr,
    ):
        place = Place(ny, nz, nx)
        qkv_bias_row = qb_ref[...].reshape(1, query_width + HD)
        input_gain_row = gain_ref[...].reshape(1, model)
        e, s, core, z, x = place.e, place.s, place.core, place.z, place.x

        kv_at = pl.ds(pl.multiple_of(core * HD, HD), HD)
        other_at = pl.ds(pl.multiple_of((1 - core) * HD, HD), HD)
        query_at, rest_at = pl.ds(0, query_width), pl.ds(query_width, HD)
        loads = (
            pltpu.make_async_copy(up_hbm, turned, w_sem.at[0]),
            pltpu.make_async_copy(down_hbm, down, w_sem.at[1]),
            pltpu.make_async_copy(qkv_hbm.at[:, rest_at], w_kv.at[:, kv_at], w_sem.at[2]),
            pltpu.make_async_copy(qkv_hbm.at[:, query_at], w_q, w_sem.at[3]),
        )
        for load in loads:
            load.start()
        barrier = pltpu.get_barrier_semaphore()

        def greet(p, carry):
            pl.semaphore_signal(barrier, inc=1, device_id=(e, wrap(s + p, groups)), device_id_type=MESH)
            return carry

        lax.fori_loop(1, groups, greet, 0)
        for other in (*place.y_side, place.sibling):
            pl.semaphore_signal(barrier, inc=1, device_id=other, device_id_type=MESH)

        front = EncGather(place, buf, lambda block, h: block.at[pl.ds(2 * h, 2)], (fns, fnr, ffs, ffr, fgs, fgr))
        values = p_ref[...].astype(jnp.float32)
        mean_square = jnp.mean(values * values, axis=1, keepdims=True)
        vision_rows = (values * lax.rsqrt(mean_square + EPSILON) * g_ref[...].reshape(1, vision)).astype(jnp.bfloat16)
        to = lax.broadcasted_iota(jnp.int32, (4 * pad, patch_rows), 0)
        source = lax.broadcasted_iota(jnp.int32, (4 * pad, patch_rows), 1)
        moved = (source == 4 * (to % pad) + to // pad) & (to % pad < part)
        order = jnp.where(moved, 1.0, 0.0).astype(jnp.bfloat16)
        sorted_rows = jnp.dot(order, vision_rows, preferred_element_type=jnp.float32).astype(jnp.bfloat16)
        for q in range(4):
            buf[place.y, core, q] = sorted_rows[q * pad : (q + 1) * pad]
        pl.semaphore_wait(barrier, groups - 1 + 3)
        front.start(0)
        front.start(1)
        kv_columns = remote(
            qkv_hbm.at[:, rest_at], w_kv.at[:, kv_at], place.sibling, c_send.at[0], c_recv.at[0]
        )
        kv_columns.start()
        kv_bias[core] = qkv_bias_row[:, query_width:]
        bias_columns = remote(kv_bias.at[core], kv_bias.at[core], place.sibling, c_send.at[1], c_recv.at[1])
        bias_columns.start()

        loads[0].wait()
        def turn(i, carry):
            at = pl.ds(pl.multiple_of(i * 512, 512), 512)
            up[at, :] = turned[:, at].T
            return carry

        turns = joined // 512
        lax.fori_loop(0, turns // 2, turn, 0)
        front.relay()
        lax.fori_loop(turns // 2, turns, turn, 0)
        front.finish_near()

        lane = lax.broadcasted_iota(jnp.int32, (1, blocks * pad), 1)
        merged = jnp.where(lane % pad < part, lane // pad * part + lane % pad, -1)
        code = jnp.full((1, blocks * pad), -1, jnp.int32)
        begin = jnp.int32(0)
        for j in range(len_s.shape[0]):
            end = begin + len_s[j, s]
            inside = (merged >= begin) & (merged < end)
            code = jnp.where(inside, off_s[j, s] // rows * LMAX + merged - begin, code)
            begin = end
        slot = lax.broadcasted_iota(jnp.int32, (slots, blocks * pad), 0)
        pick = jnp.where(slot == code, 1.0, 0.0).astype(jnp.bfloat16)

        ours = off_v[...] // rows == s
        first = jnp.sum(jnp.where(ours, off_v[...] - s * rows, 0).astype(jnp.float32), axis=0, keepdims=True)
        count = jnp.sum(jnp.where(ours, len_v[...], 0).astype(jnp.float32), axis=0, keepdims=True)
        group = lax.broadcasted_iota(jnp.int32, (groups, slots), 0)
        position = lax.broadcasted_iota(jnp.int32, (groups, slots), 1)
        spread_groups = jnp.where(position // LMAX == group, 1.0, 0.0).astype(jnp.bfloat16)
        both = jnp.concatenate([jnp.broadcast_to(first, (8, groups)), jnp.broadcast_to(count, (8, groups))], axis=0)
        both = jnp.dot(both.astype(jnp.bfloat16), spread_groups, preferred_element_type=jnp.float32)
        index = (lax.broadcasted_iota(jnp.int32, (1, slots), 1) % LMAX).astype(jnp.float32)
        target = jnp.where(index < both[8:9], both[:1] + index, -1.0)
        token = lax.broadcasted_iota(jnp.int32, (rows, slots), 0).astype(jnp.float32)
        placing = jnp.where(token == target, 1.0, 0.0)
        covered = jnp.sum(placing, axis=1, keepdims=True) > 0.5

        def merge(*chips):
            grouped = jnp.concatenate(
                [
                    jnp.concatenate([buf[y, :, q].reshape(2 * pad, vision) for q in range(4)], axis=1)
                    for y in chips
                ],
                axis=0,
            )
            inner = jnp.dot(grouped, up[...], preferred_element_type=jnp.float32) + ub_ref[...].reshape(1, units)
            inner = (0.5 * inner * (1.0 + lax.erf(inner * math.sqrt(0.5)))).astype(jnp.bfloat16)
            for i, y in enumerate(chips):
                hid[y] = inner[i * 2 * pad : (i + 1) * 2 * pad]

        front.take(0)
        merge(place.ys[0])
        front.take(1)
        front.take(2)
        merge(place.ys[1], place.ys[2])
        front.finish_far()
        front.take(3)
        merge(place.ys[3])

        chosen = jnp.dot(pick, hid[...].reshape(blocks * pad, units), preferred_element_type=jnp.float32)
        out[...] = chosen.astype(jnp.bfloat16).reshape(groups, LMAX, units)

        def swap(p, at, arrives):
            return remote(out.at[at], inn.at[arrives], (e, at), a_send.at[p], a_recv.at[p])

        def begin_swap(p, carry):
            swap(p, wrap(s + p, groups), s).start()
            return carry

        lax.fori_loop(1, groups, begin_swap, 0)
        inn[s] = out[s]
        loads[1].wait()

        def end_swap(p, carry):
            swap(p, wrap(s + p, groups), wrap(s - p + groups, groups)).wait_recv()
            return carry

        lax.fori_loop(1, groups, end_swap, 0)
        placed = jnp.dot(
            placing.astype(jnp.bfloat16), inn[...].reshape(slots, units), preferred_element_type=jnp.float32
        ).astype(jnp.bfloat16)

        targets = (place.ys[3], place.ys[2], place.ys[1], place.y)

        def share(y_to, c_to):
            start = pl.multiple_of((y_to * 2 + c_to) * width, width)
            return jnp.dot(placed, down[:, pl.ds(start, width)], preferred_element_type=jnp.float32)

        def pair(i):
            return remote(sib_out.at[i], sib_in.at[i], place.sibling, p_send.at[i], p_recv.at[i])

        def relay(side):
            return remote(rel_out.at[side], rel_in.at[side], place.y_side[side], r_send.at[side], r_recv.at[side])

        def deliver(side, h):
            return remote(
                d_out.at[side, h], d_in.at[side, h], place.y_side[side], d_send.at[side, h], d_recv.at[side, h]
            )

        halves = (slice(0, half), slice(half, rows))
        for i in range(4):
            sib_out[i] = share(targets[i], 1 - core).astype(jnp.bfloat16)
            pair(i).start()
        for i in range(4):
            own[i] = share(targets[i], core)
        pair(0).wait_recv()
        for side in range(2):
            at = halves[side]
            rel_out[side] = (own[0, at] + sib_in[0, at].astype(jnp.float32)).astype(jnp.bfloat16)
            relay(side).start()
        for side in range(2):
            pair(1 + side).wait_recv()
            own[1 + side] = own[1 + side] + sib_in[1 + side].astype(jnp.float32)
            d_out[side, 1 - side] = own[1 + side, halves[1 - side]].astype(jnp.bfloat16)
            deliver(side, 1 - side).start()
        pair(3).wait_recv()
        own[3] = own[3] + sib_in[3].astype(jnp.float32) + db_ref[...].reshape(1, width)
        for side in range(2):
            relay(side).wait_recv()
            d_out[side, side] = (own[1 + side, halves[side]] + rel_in[side].astype(jnp.float32)).astype(jnp.bfloat16)
            deliver(side, side).start()

        token_id = lax.broadcasted_iota(jnp.int32, (rows, HD), 0) + s * rows
        sine, cosine = sine_cosine(token_id.astype(jnp.float32) * freq_ref[...])
        signed = jnp.where(lax.broadcasted_iota(jnp.int32, (rows, HD), 1) < HD // 2, -sine, sine)

        def rotate(block):
            return block * cosine + pltpu.roll(block, HD // 2, 1) * signed

        back = EncGather(place, full, lambda block, h: block.at[pl.ds(h * half, half)], (bns, bnr, bfs, bfr, bgs, bgr))
        for h in range(2):
            at = halves[h]
            total = own[3, at]
            for side in range(2):
                deliver(side, h).wait_recv()
                total = total + d_in[side, h].astype(jnp.float32)
            kept = jnp.where(covered[at], total, text_ref[at].astype(jnp.float32))
            full[place.y, core, at] = kept.astype(jnp.bfloat16)
            back.start(h)
        squares[...] = jnp.zeros(squares.shape, jnp.float32)

        def add_squares(y):
            for c in range(2):
                block = full[y, c].astype(jnp.float32)
                block = block * block
                for g in range(width // HD):
                    squares[...] += block[:, g * HD : (g + 1) * HD]

        back.take(0)
        add_squares(place.ys[0])
        back.relay()
        back.finish_near()
        for i in range(1, 3):
            back.take(i)
            add_squares(place.ys[i])
        back.finish_far()
        back.take(3)
        add_squares(place.ys[3])

        scale = lax.rsqrt(jnp.sum(squares[...], axis=1, keepdims=True) * (1.0 / model) + EPSILON)
        for block in range(blocks):
            at = slice(block * width, (block + 1) * width)
            normed[:, at] = (full[block // 2, block % 2].astype(jnp.float32) * scale * input_gain_row[:, at]).astype(
                jnp.bfloat16
            )
        loads[2].wait()
        remote(
            qkv_hbm.at[:, rest_at], w_kv.at[:, other_at], place.sibling, c_send.at[0], c_recv.at[0]
        ).wait_recv()
        remote(kv_bias.at[core], kv_bias.at[1 - core], place.sibling, c_send.at[1], c_recv.at[1]).wait_recv()
        both = jnp.dot(normed[...], w_kv[...], preferred_element_type=jnp.float32)
        key = rotate(both[:, :HD] + kv_bias[0]).T
        key_high = key.astype(jnp.bfloat16)
        key_low = (key - key_high.astype(jnp.float32)).astype(jnp.bfloat16)
        value = (both[:, HD:] + kv_bias[1]).astype(jnp.bfloat16)

        for c in range(2):
            @pl.when(core == c)
            def _(c=c):
                kv[z, c, x, :, :HD] = key_high[:, halves[c]]
                kv[z, c, x, :, HD : 2 * HD] = key_low[:, halves[c]]
                kv[z, c, x, :, 2 * HD :] = value[halves[c]]

        plane = PlaneAttention(place, kv, q3, mx, den, acc, (xs, xr, hs, hr, zs, zr, ss, sr), nz, nx)
        plane.start()

        loads[3].wait()
        scaling = HD ** (-0.5) * math.log2(math.e)
        for pair_of in range(heads // 2):
            at = slice(pair_of * 2 * HD, (pair_of + 1) * 2 * HD)
            query = jnp.dot(normed[...], w_q[:, at], preferred_element_type=jnp.float32) + qkv_bias_row[:, at]
            for i in range(2):
                rows_of = slice((pair_of * 2 + i) * rows, (pair_of * 2 + i + 1) * rows)
                turned_query = rotate(query[:, i * HD : (i + 1) * HD]) * scaling
                high = turned_query.astype(jnp.bfloat16)
                q3[rows_of, :HD] = high
                q3[rows_of, HD : 2 * HD] = high
                q3[rows_of, 2 * HD :] = (turned_query - high.astype(jnp.float32)).astype(jnp.bfloat16)

        plane.own_shard(key_high, key_low, value)
        plane.run()
        for h in range(heads):
            o_ref[:, h * HD : (h + 1) * HD] = plane.result(h).astype(o_ref.dtype)

        def sent_swap(p, carry):
            swap(p, wrap(s + p, groups), s).wait_send()
            return carry

        lax.fori_loop(1, groups, sent_swap, 0)
        front.drain()
        back.drain()
        kv_columns.wait_send()
        bias_columns.wait_send()
        for i in range(4):
            pair(i).wait_send()
        for side in range(2):
            relay(side).wait_send()
            for h in range(2):
                deliver(side, h).wait_send()
        plane.drain()

    dma = pltpu.SemaphoreType.DMA
    bf16, f32 = jnp.bfloat16, jnp.float32
    vmem = pl.BlockSpec(memory_space=pltpu.VMEM)
    smem = pl.BlockSpec(memory_space=pltpu.SMEM)
    any_space = pl.BlockSpec(memory_space=pl.ANY)
    enc_sems = [dma((2, 2)), dma((2, 2)), dma((2,)), dma((2,)), dma((4, 2)), dma((4, 2))]
    return pl.pallas_call(
        kernel,
        out_shape=jax.ShapeDtypeStruct((rows, query_width), bf16),
        in_specs=[
            vmem, vmem, any_space, vmem, any_space, vmem, vmem, smem, smem, vmem, vmem, vmem, any_space, vmem, vmem,
        ],
        out_specs=vmem,
        scratch_shapes=[
            pltpu.VMEM((ny, 2, 4, pad, vision), bf16),
            pltpu.VMEM((units, joined), bf16),
            pltpu.VMEM((joined, units), bf16),
            pltpu.VMEM((ny, 2 * pad, units), bf16),
            pltpu.VMEM((groups, LMAX, units), bf16),
            pltpu.VMEM((groups, LMAX, units), bf16),
            pltpu.VMEM(merge_down.shape, bf16),
            pltpu.VMEM((model, query_width), bf16),
            pltpu.VMEM((model, 2 * HD), bf16),
            pltpu.VMEM((2, 1, HD), f32),
            pltpu.VMEM((4, rows, width), bf16),
            pltpu.VMEM((4, rows, width), bf16),
            pltpu.VMEM((4, rows, width), f32),
            pltpu.VMEM((2, half, width), bf16),
            pltpu.VMEM((2, half, width), bf16),
            pltpu.VMEM((2, 2, half, width), bf16),
            pltpu.VMEM((2, 2, half, width), bf16),
            pltpu.VMEM((ny, 2, rows, width), bf16),
            pltpu.VMEM((rows, HD), f32),
            pltpu.VMEM((rows, model), bf16),
            pltpu.VMEM((nz, 2, nx, half, 3 * HD), bf16),
            pltpu.VMEM((heads * rows, 3 * HD), bf16),
            pltpu.VMEM((heads * rows, HD), f32),
            pltpu.VMEM((heads * rows, HD), f32),
            pltpu.VMEM((heads * rows, HD), f32),
            dma((4,)),
            dma((2,)),
            dma((2,)),
            dma((groups,)),
            dma((groups,)),
            dma((4,)),
            dma((4,)),
            dma((2,)),
            dma((2,)),
            dma((2, 2)),
            dma((2, 2)),
            *enc_sems,
            *enc_sems,
            dma((nz, 2)),
            dma((nz, 2)),
            dma((nz, 2)),
            dma((nz, 2)),
            dma((2, 4 * far)),
            dma((2, 4 * far)),
            dma((nz,)),
            dma((nz,)),
        ],
        compiler_params=pltpu.CompilerParams(
            collective_id=1, has_side_effects=True, vmem_limit_bytes=56 * 1024 * 1024
        ),
        name="prefill",
    )(
        patches, gain, up_t, up_bias, merge_down, down_bias, text, lengths, offsets, lengths, offsets, input_gain,
        qkv_weight, qkv_bias, freq,
    )


def local(
    patches, vision_gain, merge_up, merge_up_bias, merge_down, merge_down_bias, text_embed, image_lengths, image_offsets,
    input_gain, qkv_weight, qkv_bias,
):
    freq = np.exp(np.arange(HD // 2) * (-2.0 * np.log(THETA) / HD)).astype(np.float32)
    return prefill(
        patches[0], vision_gain, merge_up.T, merge_up_bias, merge_down, merge_down_bias, text_embed,
        image_lengths.T, image_offsets.T, input_gain, qkv_weight, qkv_bias,
        jnp.asarray(np.concatenate([freq, freq])[None]),
        lax.axis_size("enc") // 2, lax.axis_size("seq") // NX, NX,
    )


def solution(mesh):
    in_specs = (
        P("seq", "enc", None),
        P(),
        P(None, "enc"),
        P("enc"),
        P("enc", None),
        P("enc"),
        P("seq", "enc"),
        P(),
        P(),
        P(),
        P(None, "enc"),
        P("enc"),
    )
    out_specs = P("seq", "enc")
    return jax.shard_map(local, mesh=mesh, in_specs=in_specs, out_specs=out_specs, check_vma=False)
```

```python
import math

import jax
import jax.numpy as jnp
import numpy as np
from jax import lax
from jax.experimental import pallas as pl
from jax.experimental.pallas import tpu as pltpu
from jax.sharding import PartitionSpec as P

HD = 128
LMAX = 16
NX = 4
EPSILON = 1e-06
THETA = 1000000.0
NEG = -1e30
MESH = pl.DeviceIdType.MESH


def wrap(value, size):
    return lax.rem(value + 2 * size, size)


def remote(src, dst, to, send_sem, recv_sem):
    return pltpu.make_async_remote_copy(
        src_ref=src, dst_ref=dst, send_sem=send_sem, recv_sem=recv_sem, device_id=to, device_id_type=MESH
    )


def sine_cosine(angle):
    turns = jnp.floor(angle * (2.0 / math.pi) + 0.5)
    rest = ((angle - turns * 1.5703125) - turns * 4.837512969970703125e-4) - turns * 7.54978995489188216e-8
    square = rest * rest
    sine = ((-1.9515295891e-4 * square + 8.3321608736e-3) * square - 1.6666654611e-1) * square * rest + rest
    cosine = (
        ((2.443315711809948e-5 * square - 1.388731625493765e-3) * square + 4.166664568298827e-2) * square * square
        - 0.5 * square
        + 1.0
    )
    quadrant = turns - 4.0 * jnp.floor(turns * 0.25)
    odd = (quadrant == 1.0) | (quadrant == 3.0)
    sine, cosine = jnp.where(odd, cosine, sine), jnp.where(odd, sine, cosine)
    sine = jnp.where(quadrant >= 2.0, -sine, sine)
    cosine = jnp.where((quadrant == 1.0) | (quadrant == 2.0), -cosine, cosine)
    return sine, cosine


class EncGather:
    def __init__(self, place, half, sems, shared):
        self.place, self.half, self.shared = place, half, shared
        self.near_send, self.near_recv, self.far_send, self.far_recv, self.give_send, self.give_recv = sems

    def near(self, side, index, h):
        place = self.place
        slot = self.half(place.ys[index], place.core, h)
        return remote(slot, slot, place.y_side[side], self.near_send.at[side, h], self.near_recv.at[side, h])

    def far(self, side, index):
        place = self.place
        slot = self.half(place.ys[index], place.core, side)
        return remote(slot, slot, place.y_side[side], self.far_send.at[side], self.far_recv.at[side])

    def give(self, index, h, mine=True):
        place = self.place
        slot = self.half(place.ys[index], place.core if mine else 1 - place.core, h)
        return remote(slot, slot, place.sibling, self.give_send.at[index, h], self.give_recv.at[index, h])

    def take(self, index):
        for h in range(2):
            self.give(index, h, mine=False).wait_recv()

    def start(self, h):
        for side in range(2):
            self.near(side, 0, h).start()
        self.share(0, h)

    def share(self, index, h):
        if self.shared:
            self.give(index, h).start()

    def relay(self):
        for side in range(2):
            self.near(side, 1 + side, side).wait_recv()
            self.far(side, 1 + side).start()
            self.share(1 + side, side)

    def finish_near(self):
        for side in range(2):
            self.near(side, 1 + side, 1 - side).wait_recv()
            self.share(1 + side, 1 - side)

    def finish_far(self):
        for side in range(2):
            self.far(side, 3).wait_recv()
            self.share(3, side)

    def drain(self):
        for side in range(2):
            for h in range(2):
                self.near(side, 0, h).wait_send()
            self.far(side, 1 + side).wait_send()
        for index in range(4 if self.shared else 0):
            for h in range(2):
                self.give(index, h).wait_send()


class Place:
    def __init__(self, ny, nz, nx):
        e = lax.axis_index("enc")
        s = lax.axis_index("seq")
        self.e, self.s = e, s
        self.core, self.y = lax.rem(e, 2), lax.div(e, 2)
        self.z, self.x = lax.div(s, nx), lax.rem(s, nx)
        up, down = wrap(self.y + 1, ny), wrap(self.y - 1, ny)
        self.ys = (self.y, down, up, wrap(self.y + 2, ny))
        self.y_side = ((up * 2 + self.core, s), (down * 2 + self.core, s))
        self.sibling = (e + 1 - 2 * self.core, s)
        self.x_side = tuple((e, self.z * nx + wrap(self.x + d, nx)) for d in (1, -1))
        self.z_side = tuple((e, wrap(self.z + d, nz) * nx + self.x) for d in (1, -1))
        self.cols = (self.x, wrap(self.x - 1, nx), wrap(self.x + 1, nx), wrap(self.x + 2, nx))


class PlaneAttention:
    def __init__(self, place, kv, q3, mx, den, acc, sems, nz, nx):
        self.place, self.kv, self.q3, self.mx, self.den, self.acc, self.nz, self.nx = place, kv, q3, mx, den, acc, nz, nx
        self.xs, self.xr, self.hs, self.hr, self.zs, self.zr, self.ss, self.sr = sems
        self.far = nz // 2
        self.half = kv.shape[3]
        self.rows = 2 * self.half
        self.heads = q3.shape[0]
        self.together = min(2, self.heads)
        self.group = self.together * self.rows

    def along_x(self, j, side, i):
        place = self.place
        slot = self.kv.at[self.row_at(j), place.core, place.cols[i]]
        return remote(slot, slot, place.x_side[side], self.xs.at[j, side], self.xr.at[j, side])

    def half_on(self, j, side, i):
        place = self.place
        part = pl.ds(side * (self.half // 2), self.half // 2)
        slot = self.kv.at[self.row_at(j), place.core, place.cols[i], part]
        return remote(slot, slot, place.x_side[side], self.hs.at[j, side], self.hr.at[j, side])

    def along_z(self, j, side, i, k):
        place = self.place
        slot = self.kv.at[self.row_at(j), place.core, place.cols[i]]
        at = 4 * (k - 1) + i
        return remote(slot, slot, place.z_side[side], self.zs.at[side, at], self.zr.at[side, at])

    def half_along_z(self, j, side):
        place = self.place
        slot = self.kv.at[self.row_at(j), place.core, place.x, pl.ds(side * (self.half // 2), self.half // 2)]
        at = 4 * (self.far - 1)
        return remote(slot, slot, place.z_side[side], self.zs.at[side, at], self.zr.at[side, at])

    def give(self, j, mine=True):
        place = self.place
        slot = self.kv.at[self.row_at(j), place.core if mine else 1 - place.core]
        return remote(slot, slot, place.sibling, self.ss.at[j], self.sr.at[j])

    def row_at(self, j):
        k = (j + 1) // 2
        return wrap(self.place.z - k, self.nz) if j % 2 == 1 else wrap(self.place.z + k, self.nz)

    def ring_rows(self, k):
        far = self.far
        return [] if not 0 <= k <= far else [0] if k == 0 else [2 * k - 1] if k == far else [2 * k - 1, 2 * k]

    def comes(self, side, k):
        z = self.place.z
        return z >= k if side == 0 else wrap(z + k, self.nz) < self.far

    def goes(self, side, k):
        z = self.place.z
        if side == 0:
            return (z >= k - 1) & (z <= self.nz - 2)
        return wrap(z + k - 1, self.nz) < self.far

    def needed(self, j):
        k = (j + 1) // 2
        z = self.place.z
        return z >= k if j % 2 == 1 else z + k >= self.nz if j else z >= 0

    def start(self):
        for side in range(2):
            self.along_x(0, side, 0).start()

            @pl.when(self.goes(side, 1))
            def _(side=side):
                self.along_z(0, side, 0, 1).start()

    def attend(self, high, low, v, restrict, fresh=False):
        stacked = jnp.concatenate([high, low, high], axis=0)
        pieces = stacked.shape[1] // HD
        parts = [slice(i, i + self.group) for i in range(0, self.heads * self.rows, self.group)]
        queries = [
            self.q3[h : h + self.together].reshape(self.group, 3 * HD) for h in range(0, self.heads, self.together)
        ]
        scores = [jnp.dot(query, stacked, preferred_element_type=jnp.float32) for query in queries]
        for at, score in zip(parts, scores):
            if restrict is not None:
                score = jnp.concatenate([restrict(i, score[:, i * HD : (i + 1) * HD]) for i in range(pieces)], axis=1)
            top = jnp.max(score, axis=1, keepdims=True)
            new = jnp.broadcast_to(top, (self.group, HD)) if fresh else jnp.maximum(self.mx[at], top)
            weights = jnp.exp2(score - jnp.concatenate([new] * pieces, axis=1))
            summed = weights[:, :HD]
            for g in range(1, pieces):
                summed = summed + weights[:, g * HD : (g + 1) * HD]
            product = jnp.dot(weights.astype(jnp.bfloat16), v, preferred_element_type=jnp.float32)
            if fresh:
                self.den[at] = summed
                self.acc[at] = product
            else:
                factor = jnp.exp2(self.mx[at] - new)
                self.den[at] = self.den[at] * factor + summed
                self.acc[at] = self.acc[at] * factor + product
            self.mx[at] = new

    def compute(self, row, c, restrict=None, fresh=False):
        block = self.kv[row, c]
        high = jnp.concatenate([block[i, :, :HD] for i in range(self.nx)], axis=1)
        low = jnp.concatenate([block[i, :, HD : 2 * HD] for i in range(self.nx)], axis=1)
        self.attend(high, low, block[:, :, 2 * HD :].reshape(self.nx * self.half, HD), restrict, fresh)

    def own_row(self, c, fresh):
        x = self.place.x
        shape = (self.group, HD)
        token = lax.broadcasted_iota(jnp.int32, shape, 0) & (self.rows - 1)
        ahead = lax.broadcasted_iota(jnp.int32, shape, 1) - token

        def restrict(i, piece):
            limit = jnp.where(x > i, 2 * self.rows, jnp.where(x == i, 0, -2 * self.rows)) - c * self.half
            return jnp.where(ahead <= limit, piece, NEG)

        self.compute(self.place.z, c, restrict, fresh)

    def far_rows(self, k, c):
        def step(i, carry):
            row = wrap(self.place.z + k * (2 * i - 1), self.nz)

            @pl.when(row < self.place.z)
            def _():
                self.compute(row, c)

            return carry

        lax.fori_loop(0, len(self.ring_rows(k)), step, 0)

    def pass_rows(self, k, chosen):
        far = self.far
        if not 1 <= k <= far:
            return
        for side in range(2):
            j = min(2 * k - 1 + side, 2 * far - 1)
            mine = [i for i in chosen if k < far or i // 2 == side]
            onward = [i for i in chosen if k + 1 < far or (k + 1 == far and i // 2 == side)]

            @pl.when(self.comes(side, k))
            def _(side=side, j=j, mine=mine):
                for i in mine:
                    self.along_z(j, side, i, k).wait_recv()

            if onward:
                @pl.when(self.goes(side, k + 1))
                def _(side=side, j=j, onward=onward):
                    for i in onward:
                        self.along_z(j, side, i, k + 1).start()

    def early(self, t):
        far = self.far

        @pl.when(self.place.core == 0)
        def _():
            if t == 1:
                for side in range(2):
                    self.along_x(0, side, 1 + side).wait_recv()
                    self.half_on(0, side, 1 + side).start()
                    for direction in range(2):
                        @pl.when(self.goes(direction, 1))
                        def _(side=side, direction=direction):
                            self.along_z(0, direction, 1 + side, 1).start()
            self.pass_rows(t - 2, (0, 1))

        @pl.when(self.place.core == 1)
        def _():
            if 1 <= t <= far:
                for side in range(2):
                    j = min(2 * t - 1 + side, 2 * far - 1)

                    @pl.when(self.comes(side, t))
                    def _(side=side, j=j):
                        if t < far:
                            self.along_z(j, side, 0, t).wait_recv()
                        else:
                            self.half_along_z(j, side).wait_recv()

                    if t < far:
                        @pl.when(self.goes(side, t + 1))
                        def _(side=side, j=j):
                            if t + 1 < far:
                                self.along_z(j, side, 0, t + 1).start()
                            else:
                                self.half_along_z(j, side).start()
                for j in self.ring_rows(t):
                    @pl.when(self.needed(j))
                    def _(j=j):
                        for side in range(2):
                            self.along_x(j, side, 0).start()
            for j in self.ring_rows(t - 1):
                @pl.when(self.needed(j))
                def _(j=j):
                    for side in range(2):
                        self.along_x(j, side, 1 + side).wait_recv()
                        self.half_on(j, side, 1 + side).start()

    def from_sibling(self, k):
        for j in self.ring_rows(k):
            @pl.when(self.needed(j))
            def _(j=j):
                self.give(j, mine=False).wait_recv()

    def late(self, t):
        @pl.when(self.place.core == 0)
        def _():
            if t == 2:
                for side in range(2):
                    self.half_on(0, side, 3).wait_recv()
                for direction in range(2):
                    @pl.when(self.goes(direction, 1))
                    def _(direction=direction):
                        self.along_z(0, direction, 3, 1).start()
            self.pass_rows(t - 2, (2, 3))

        for j in self.ring_rows(t - 2):
            @pl.when(self.needed(j))
            def _(j=j):
                @pl.when(self.place.core == 1)
                def _():
                    for side in range(2):
                        self.half_on(j, side, 3).wait_recv()

                self.give(j).start()

    def run(self, queries_here):
        core, far = self.place.core, self.far
        for t in range(1, far + 4):
            self.early(t)
            if t > 3:
                self.from_sibling(t - 3)
                self.far_rows(t - 3, 1 - core)
            self.late(t)
            if t == 3:
                self.from_sibling(0)
                self.own_row(1 - core, False)
            if t == 2:
                queries_here()
                self.own_row(core, True)
            elif 3 <= t <= far + 2:
                self.far_rows(t - 2, core)

    def result(self, h):
        at = slice(h * self.rows, (h + 1) * self.rows)
        return self.acc[at] / jnp.sum(self.den[at], axis=1, keepdims=True)

    def drain(self):
        far = self.far
        for side in range(2):
            self.along_x(0, side, 0).wait_send()
            self.half_on(0, side, 1 + side).wait_send()
        for j in range(2 * far):
            @pl.when(self.needed(j))
            def _(j=j):
                self.give(j).wait_send()

                @pl.when((self.place.core == 1) & (j > 0))
                def _():
                    for side in range(2):
                        self.along_x(j, side, 0).wait_send()
                        self.half_on(j, side, 1 + side).wait_send()

        for side in range(2):
            for k in range(1, far + 1):
                @pl.when(self.goes(side, k))
                def _(side=side, k=k):
                    j = 0 if k == 1 else 2 * k - 3 + side

                    @pl.when(self.place.core == 0)
                    def _():
                        for i in range(4):
                            if k < far or i // 2 == side:
                                self.along_z(j, side, i, k).wait_send()

                    @pl.when(self.place.core == 1)
                    def _():
                        if k < far:
                            self.along_z(j, side, 0, k).wait_send()
                        else:
                            self.half_along_z(j, side).wait_send()


def prefill(
    patches, gain, up_t, up_bias, merge_down, down_bias, text, lengths, offsets, input_gain, qkv_weight, qkv_bias, freq,
    ny, nz, nx,
):
    patch_rows, vision = patches.shape
    units, joined = up_t.shape
    part = patch_rows // 4
    pad = -(-part // 16) * 16
    blocks = 2 * ny
    wide = 2 * text.shape[1]
    groups = nz * nx
    slots = groups * LMAX
    rows, width = text.shape
    half = rows // 2
    model = merge_down.shape[1]
    query_width = qkv_weight.shape[1] - HD
    heads = query_width // HD
    far = nz // 2

    def kernel(
        p_ref, g_ref, up_hbm, ub_ref, down_hbm, db_ref, text_ref, len_s, off_s, len_v, off_v, gain_ref, qkv_hbm, qb_ref,
        freq_ref, o_ref,
        buf, turned, up, hid, out, inn, down, w_q, w_kv, qkv_bias_of, down_bias_of, text_of, placed_out, placed_in,
        own, rel_out, rel_in, d_out, d_in, full, squares, normed, kv, q3, q_out, mx, den, acc,
        w_sem, c_send, c_recv, a_send, a_recv, r_send, r_recv, d_send, d_recv,
        fns, fnr, ffs, ffr, fgs, fgr, bns, bnr, bfs, bfr,
        xs, xr, hs, hr, zs, zr, ss, sr,
    ):
        place = Place(ny, nz, nx)
        e, s, core, z, x = place.e, place.s, place.core, place.z, place.x
        other = 1 - core

        query_at, rest_at = pl.ds(0, query_width), pl.ds(query_width, HD)

        def lanes(c, size):
            return pl.ds(pl.multiple_of(c * size, size), size)

        def tokens(c):
            return pl.ds(pl.multiple_of(c * half, half), half)

        loads = (
            pltpu.make_async_copy(up_hbm, turned, w_sem.at[0]),
            pltpu.make_async_copy(down_hbm, down.at[core], w_sem.at[1]),
            pltpu.make_async_copy(qkv_hbm.at[:, rest_at], w_kv.at[:, lanes(core, HD)], w_sem.at[2]),
            pltpu.make_async_copy(qkv_hbm.at[:, query_at], w_q.at[core], w_sem.at[3]),
        )
        for load in loads:
            load.start()

        def to_sibling(i, src, dst):
            return remote(src, dst, place.sibling, c_send.at[i], c_recv.at[i])

        def gift(i, c):
            return (
                lambda: to_sibling(0, qkv_bias_of.at[core], qkv_bias_of.at[c]),
                lambda: to_sibling(1, down_bias_of.at[core], down_bias_of.at[c]),
                lambda: to_sibling(2, text_ref.at[tokens(other)], text_of.at[:, lanes(c, width)]),
                lambda: to_sibling(3, qkv_hbm.at[:, rest_at], w_kv.at[:, lanes(c, HD)]),
                lambda: to_sibling(4, down_hbm, down.at[c]),
                lambda: to_sibling(5, qkv_hbm.at[:, query_at], w_q.at[c]),
                lambda: to_sibling(6, placed_out, placed_in),
                lambda: to_sibling(7, q_out, q3.at[:, c]),
            )[i]()

        barrier = pltpu.get_barrier_semaphore()

        def greet(p, carry):
            pl.semaphore_signal(barrier, inc=1, device_id=(e, wrap(s + p, groups)), device_id_type=MESH)
            return carry

        lax.fori_loop(1, groups, greet, 0)
        for to in (*place.y_side, place.sibling):
            pl.semaphore_signal(barrier, inc=1, device_id=to, device_id_type=MESH)

        front = EncGather(
            place, lambda y, c, h: buf.at[y, c, pl.ds(2 * h, 2)], (fns, fnr, ffs, ffr, fgs, fgr), shared=True
        )
        values = p_ref[...].astype(jnp.float32)
        mean_square = jnp.mean(values * values, axis=1, keepdims=True)
        vision_rows = (values * lax.rsqrt(mean_square + EPSILON) * g_ref[...].reshape(1, vision)).astype(jnp.bfloat16)
        to = lax.broadcasted_iota(jnp.int32, (4 * pad, patch_rows), 0)
        source = lax.broadcasted_iota(jnp.int32, (4 * pad, patch_rows), 1)
        moved = (source == 4 * (to % pad) + to // pad) & (to % pad < part)
        order = jnp.where(moved, 1.0, 0.0).astype(jnp.bfloat16)
        sorted_rows = jnp.dot(order, vision_rows, preferred_element_type=jnp.float32).astype(jnp.bfloat16)
        for q in range(4):
            buf[place.y, core, q] = sorted_rows[q * pad : (q + 1) * pad]
        pl.semaphore_wait(barrier, groups - 1 + 3)
        front.start(0)
        front.start(1)
        qkv_bias_of[core] = qb_ref[...].reshape(1, query_width + HD)
        down_bias_of[core] = db_ref[...].reshape(1, width)
        for i in range(4):
            gift(i, core).start()
        text_of[:, lanes(core, width)] = text_ref[tokens(core)]

        loads[0].wait()
        def turn(i, carry):
            at = pl.ds(pl.multiple_of(i * 512, 512), 512)
            up[at, :] = turned[:, at].T
            return carry

        turns = joined // 512
        lax.fori_loop(0, turns // 2, turn, 0)
        front.relay()
        lax.fori_loop(turns // 2, turns, turn, 0)
        front.finish_near()

        lane = lax.broadcasted_iota(jnp.int32, (1, blocks * pad), 1)
        merged = jnp.where(lane % pad < part, lane // pad * part + lane % pad, -1)
        code = jnp.full((1, blocks * pad), -1, jnp.int32)
        begin = jnp.int32(0)
        for j in range(len_s.shape[0]):
            end = begin + len_s[j, s]
            inside = (merged >= begin) & (merged < end)
            code = jnp.where(inside, off_s[j, s] // rows * LMAX + merged - begin, code)
            begin = end
        slot = lax.broadcasted_iota(jnp.int32, (slots, blocks * pad), 0)
        pick = jnp.where(slot == code, 1.0, 0.0).astype(jnp.bfloat16)

        ours = off_v[...] // rows == s
        first = jnp.sum(jnp.where(ours, off_v[...] - s * rows, 0).astype(jnp.float32), axis=0, keepdims=True)
        count = jnp.sum(jnp.where(ours, len_v[...], 0).astype(jnp.float32), axis=0, keepdims=True)
        group = lax.broadcasted_iota(jnp.int32, (groups, slots), 0)
        position = lax.broadcasted_iota(jnp.int32, (groups, slots), 1)
        spread_groups = jnp.where(position // LMAX == group, 1.0, 0.0).astype(jnp.bfloat16)
        both = jnp.concatenate([jnp.broadcast_to(first, (8, groups)), jnp.broadcast_to(count, (8, groups))], axis=0)
        both = jnp.dot(both.astype(jnp.bfloat16), spread_groups, preferred_element_type=jnp.float32)
        index = (lax.broadcasted_iota(jnp.int32, (1, slots), 1) % LMAX).astype(jnp.float32)
        target = jnp.where(index < both[8:9], both[:1] + index, -1.0)
        token = lax.broadcasted_iota(jnp.int32, (half, slots), 0)

        def placing(c):
            return jnp.where((token + c * half).astype(jnp.float32) == target, 1.0, 0.0)

        covered = jnp.sum(placing(core), axis=1, keepdims=True) > 0.5

        def merge(*chips):
            grouped = jnp.concatenate(
                [
                    jnp.concatenate([buf[y, :, q].reshape(2 * pad, vision) for q in range(4)], axis=1)
                    for y in chips
                ],
                axis=0,
            )
            inner = jnp.dot(grouped, up[...], preferred_element_type=jnp.float32) + ub_ref[...].reshape(1, units)
            inner = (0.5 * inner * (1.0 + lax.erf(inner * math.sqrt(0.5)))).astype(jnp.bfloat16)
            for i, y in enumerate(chips):
                hid[y] = inner[i * 2 * pad : (i + 1) * 2 * pad]

        front.take(0)
        merge(place.ys[0])
        front.take(1)
        front.take(2)
        merge(place.ys[1], place.ys[2])
        front.finish_far()
        for i in (4, 5):
            gift(i, core).start()
        front.take(3)
        merge(place.ys[3])

        chosen = jnp.dot(pick, hid[...].reshape(blocks * pad, units), preferred_element_type=jnp.float32)
        out[...] = chosen.astype(jnp.bfloat16).reshape(groups, LMAX, units)

        def swap(p, at, arrives):
            return remote(out.at[at], inn.at[arrives], (e, at), a_send.at[p], a_recv.at[p])

        def begin_swap(p, carry):
            swap(p, wrap(s + p, groups), s).start()
            return carry

        lax.fori_loop(1, groups, begin_swap, 0)
        inn[s] = out[s]
        def end_swap(p, carry):
            swap(p, wrap(s + p, groups), wrap(s - p + groups, groups)).wait_recv()
            return carry

        lax.fori_loop(1, groups, end_swap, 0)
        arrived = inn[...].reshape(slots, units)

        def place_tokens(c):
            return jnp.dot(
                placing(c).astype(jnp.bfloat16), arrived, preferred_element_type=jnp.float32
            ).astype(jnp.bfloat16)

        placed_out[...] = place_tokens(other)
        gift(6, core).start()
        placed = place_tokens(core)

        targets = (place.ys[3], place.ys[2], place.ys[1], place.y)

        def share(hidden_rows, c, y_to):
            return jnp.dot(hidden_rows, down[c, :, lanes(y_to, wide)], preferred_element_type=jnp.float32)

        def relay(side):
            return remote(rel_out.at[side], rel_in.at[side], place.y_side[side], r_send.at[side], r_recv.at[side])

        def deliver(side, h):
            return remote(
                d_out.at[side, h], d_in.at[side, h], place.y_side[side], d_send.at[side, h], d_recv.at[side, h]
            )

        halves = (slice(0, half // 2), slice(half // 2, half))
        loads[1].wait()
        for i in range(4):
            own[i] = share(placed, core, targets[i])
        gift(4, other).wait_recv()
        gift(6, other).wait_recv()
        for i in range(4):
            own[i] = own[i] + share(placed_in[...], other, targets[i])
            for side in range(2):
                if i == 0:
                    rel_out[side] = own[0, halves[side]].astype(jnp.bfloat16)
                    relay(side).start()
                if i == 1 + side:
                    d_out[side, 1 - side] = own[i, halves[1 - side]].astype(jnp.bfloat16)
                    deliver(side, 1 - side).start()
        gift(1, other).wait_recv()
        gift(2, other).wait_recv()
        own[3] = own[3] + jnp.concatenate([down_bias_of[0], down_bias_of[1]], axis=1)
        for side in range(2):
            relay(side).wait_recv()
            d_out[side, side] = (own[1 + side, halves[side]] + rel_in[side].astype(jnp.float32)).astype(jnp.bfloat16)
            deliver(side, side).start()

        token_id = lax.broadcasted_iota(jnp.int32, (half, HD), 0) + s * rows + core * half
        sine, cosine = sine_cosine(token_id.astype(jnp.float32) * freq_ref[...])
        signed = jnp.where(lax.broadcasted_iota(jnp.int32, (half, HD), 1) < HD // 2, -sine, sine)

        def rotate(block):
            return block * cosine + pltpu.roll(block, HD // 2, 1) * signed

        back = EncGather(
            place, lambda y, c, h: full.at[y, pl.ds(h * (half // 2), half // 2)], (bns, bnr, bfs, bfr, None, None), shared=False
        )
        for h in range(2):
            at = halves[h]
            total = own[3, at]
            for side in range(2):
                deliver(side, h).wait_recv()
                total = total + d_in[side, h].astype(jnp.float32)
            kept = jnp.where(covered[at], total, text_of[at].astype(jnp.float32))
            full[place.y, at] = kept.astype(jnp.bfloat16)
            back.start(h)
        squares[...] = jnp.zeros(squares.shape, jnp.float32)

        def add_squares(y):
            block = full[y].astype(jnp.float32)
            block = block * block
            summed = block[:, :HD]
            for g in range(1, wide // HD):
                summed = summed + block[:, g * HD : (g + 1) * HD]
            squares[...] += summed

        add_squares(place.ys[0])
        back.relay()
        back.finish_near()
        for i in range(1, 3):
            add_squares(place.ys[i])
        back.finish_far()
        add_squares(place.ys[3])

        scale = lax.rsqrt(jnp.sum(squares[...], axis=1, keepdims=True) * (1.0 / model) + EPSILON)
        input_gain_row = gain_ref[...].reshape(1, model)
        for y in range(ny):
            at = slice(y * wide, (y + 1) * wide)
            normed[:, at] = (full[y].astype(jnp.float32) * scale * input_gain_row[:, at]).astype(jnp.bfloat16)
        loads[2].wait()
        gift(0, other).wait_recv()
        gift(3, other).wait_recv()
        both = jnp.dot(normed[...], w_kv[...], preferred_element_type=jnp.float32)
        key = rotate(both[:, :HD] + qkv_bias_of[0, :, query_width:]).T
        key_high = key.astype(jnp.bfloat16)
        kv[z, core, x, :, :HD] = key_high
        kv[z, core, x, :, HD : 2 * HD] = (key - key_high.astype(jnp.float32)).astype(jnp.bfloat16)
        kv[z, core, x, :, 2 * HD :] = (both[:, HD:] + qkv_bias_of[1, :, query_width:]).astype(jnp.bfloat16)

        plane = PlaneAttention(place, kv, q3, mx, den, acc, (xs, xr, hs, hr, zs, zr, ss, sr), nz, nx)
        plane.start()

        scaling = HD ** (-0.5) * math.log2(math.e)

        def project(c, store):
            for first_head in range(0, heads, 2):
                at = slice(first_head * HD, (first_head + 2) * HD)
                query = jnp.dot(normed[...], w_q[c, :, at], preferred_element_type=jnp.float32) + qkv_bias_of[c, :, at]
                for i in range(2):
                    head = rotate(query[:, i * HD : (i + 1) * HD]) * scaling
                    high = head.astype(jnp.bfloat16)
                    low = (head - high.astype(jnp.float32)).astype(jnp.bfloat16)
                    store(first_head + i, jnp.concatenate([high, high, low], axis=1))

        def keep_out(h, value):
            q_out[h] = value

        def keep_here(h, value):
            q3[h, core] = value

        gift(5, other).wait_recv()
        project(other, keep_out)
        gift(7, core).start()
        loads[3].wait()
        project(core, keep_here)
        plane.run(lambda: gift(7, other).wait_recv())
        for h in range(heads):
            o_ref[:, h * HD : (h + 1) * HD] = plane.result(h).astype(o_ref.dtype)

        def sent_swap(p, carry):
            swap(p, wrap(s + p, groups), s).wait_send()
            return carry

        lax.fori_loop(1, groups, sent_swap, 0)
        front.drain()
        back.drain()
        for i in range(8):
            gift(i, core).wait_send()
        for side in range(2):
            relay(side).wait_send()
            for h in range(2):
                deliver(side, h).wait_send()
        plane.drain()

    dma = pltpu.SemaphoreType.DMA
    bf16, f32 = jnp.bfloat16, jnp.float32
    vmem = pl.BlockSpec(memory_space=pltpu.VMEM)
    smem = pl.BlockSpec(memory_space=pltpu.SMEM)
    any_space = pl.BlockSpec(memory_space=pl.ANY)
    enc_sems = [dma((2, 2)), dma((2, 2)), dma((2,)), dma((2,)), dma((4, 2)), dma((4, 2))]
    return pl.pallas_call(
        kernel,
        out_shape=jax.ShapeDtypeStruct((rows, query_width), bf16),
        in_specs=[
            vmem, vmem, any_space, vmem, any_space, vmem, vmem, smem, smem, vmem, vmem, vmem, any_space, vmem, vmem,
        ],
        out_specs=vmem,
        scratch_shapes=[
            pltpu.VMEM((ny, 2, 4, pad, vision), bf16),
            pltpu.VMEM((units, joined), bf16),
            pltpu.VMEM((joined, units), bf16),
            pltpu.VMEM((ny, 2 * pad, units), bf16),
            pltpu.VMEM((groups, LMAX, units), bf16),
            pltpu.VMEM((groups, LMAX, units), bf16),
            pltpu.VMEM((2, *merge_down.shape), bf16),
            pltpu.VMEM((2, model, query_width), bf16),
            pltpu.VMEM((model, 2 * HD), bf16),
            pltpu.VMEM((2, 1, query_width + HD), f32),
            pltpu.VMEM((2, 1, width), f32),
            pltpu.VMEM((half, wide), bf16),
            pltpu.VMEM((half, units), bf16),
            pltpu.VMEM((half, units), bf16),
            pltpu.VMEM((4, half, wide), f32),
            pltpu.VMEM((2, half // 2, wide), bf16),
            pltpu.VMEM((2, half // 2, wide), bf16),
            pltpu.VMEM((2, 2, half // 2, wide), bf16),
            pltpu.VMEM((2, 2, half // 2, wide), bf16),
            pltpu.VMEM((ny, half, wide), bf16),
            pltpu.VMEM((half, HD), f32),
            pltpu.VMEM((half, model), bf16),
            pltpu.VMEM((nz, 2, nx, half, 3 * HD), bf16),
            pltpu.VMEM((heads, 2, half, 3 * HD), bf16),
            pltpu.VMEM((heads, half, 3 * HD), bf16),
            pltpu.VMEM((heads * rows, HD), f32),
            pltpu.VMEM((heads * rows, HD), f32),
            pltpu.VMEM((heads * rows, HD), f32),
            dma((4,)),
            dma((8,)),
            dma((8,)),
            dma((groups,)),
            dma((groups,)),
            dma((2,)),
            dma((2,)),
            dma((2, 2)),
            dma((2, 2)),
            *enc_sems,
            *enc_sems[:4],
            dma((nz, 2)),
            dma((nz, 2)),
            dma((nz, 2)),
            dma((nz, 2)),
            dma((2, 4 * far)),
            dma((2, 4 * far)),
            dma((nz,)),
            dma((nz,)),
        ],
        compiler_params=pltpu.CompilerParams(
            collective_id=1, has_side_effects=True, vmem_limit_bytes=56 * 1024 * 1024
        ),
        name="prefill",
    )(
        patches, gain, up_t, up_bias, merge_down, down_bias, text, lengths, offsets, lengths, offsets, input_gain,
        qkv_weight, qkv_bias, freq,
    )


def local(
    patches, vision_gain, merge_up, merge_up_bias, merge_down, merge_down_bias, text_embed, image_lengths, image_offsets,
    input_gain, qkv_weight, qkv_bias,
):
    freq = np.exp(np.arange(HD // 2) * (-2.0 * np.log(THETA) / HD)).astype(np.float32)
    return prefill(
        patches[0], vision_gain, merge_up.T, merge_up_bias, merge_down, merge_down_bias, text_embed,
        image_lengths.T, image_offsets.T, input_gain, qkv_weight, qkv_bias,
        jnp.asarray(np.concatenate([freq, freq])[None]),
        lax.axis_size("enc") // 2, lax.axis_size("seq") // NX, NX,
    )


def solution(mesh):
    in_specs = (
        P("seq", "enc", None),
        P(),
        P(None, "enc"),
        P("enc"),
        P("enc", None),
        P("enc"),
        P("seq", "enc"),
        P(),
        P(),
        P(),
        P(None, "enc"),
        P("enc"),
    )
    out_specs = P("seq", "enc")
    return jax.shard_map(local, mesh=mesh, in_specs=in_specs, out_specs=out_specs, check_vma=False)
```

```python
import math

import jax
import jax.numpy as jnp
import numpy as np
from jax import lax
from jax.experimental import pallas as pl
from jax.experimental.pallas import tpu as pltpu
from jax.sharding import PartitionSpec as P

HD = 128
LMAX = 16
NX = 4
EPSILON = 1e-06
THETA = 1000000.0
NEG = -1e30
MESH = pl.DeviceIdType.MESH


def wrap(value, size):
    return lax.rem(value + 2 * size, size)


def remote(src, dst, to, send_sem, recv_sem):
    return pltpu.make_async_remote_copy(
        src_ref=src, dst_ref=dst, send_sem=send_sem, recv_sem=recv_sem, device_id=to, device_id_type=MESH
    )


def sine_cosine(angle):
    turns = jnp.floor(angle * (2.0 / math.pi) + 0.5)
    rest = ((angle - turns * 1.5703125) - turns * 4.837512969970703125e-4) - turns * 7.54978995489188216e-8
    square = rest * rest
    sine = ((-1.9515295891e-4 * square + 8.3321608736e-3) * square - 1.6666654611e-1) * square * rest + rest
    cosine = (
        ((2.443315711809948e-5 * square - 1.388731625493765e-3) * square + 4.166664568298827e-2) * square * square
        - 0.5 * square
        + 1.0
    )
    quadrant = turns - 4.0 * jnp.floor(turns * 0.25)
    odd = (quadrant == 1.0) | (quadrant == 3.0)
    sine, cosine = jnp.where(odd, cosine, sine), jnp.where(odd, sine, cosine)
    sine = jnp.where(quadrant >= 2.0, -sine, sine)
    cosine = jnp.where((quadrant == 1.0) | (quadrant == 2.0), -cosine, cosine)
    return sine, cosine


class EncGather:
    def __init__(self, place, half, sems, shared):
        self.place, self.half, self.shared = place, half, shared
        self.near_send, self.near_recv, self.far_send, self.far_recv, self.give_send, self.give_recv = sems

    def near(self, side, index, h):
        place = self.place
        slot = self.half(place.ys[index], place.core, h)
        return remote(slot, slot, place.y_side[side], self.near_send.at[side, h], self.near_recv.at[side, h])

    def far(self, side, index):
        place = self.place
        slot = self.half(place.ys[index], place.core, side)
        return remote(slot, slot, place.y_side[side], self.far_send.at[side], self.far_recv.at[side])

    def give(self, index, h, mine=True):
        place = self.place
        slot = self.half(place.ys[index], place.core if mine else 1 - place.core, h)
        return remote(slot, slot, place.sibling, self.give_send.at[index, h], self.give_recv.at[index, h])

    def take(self, index):
        for h in range(2):
            self.give(index, h, mine=False).wait_recv()

    def start(self, h):
        for side in range(2):
            self.near(side, 0, h).start()
        self.share(0, h)

    def share(self, index, h):
        if self.shared:
            self.give(index, h).start()

    def relay(self):
        for side in range(2):
            self.near(side, 1 + side, side).wait_recv()
            self.far(side, 1 + side).start()
            self.share(1 + side, side)

    def finish_near(self):
        for side in range(2):
            self.near(side, 1 + side, 1 - side).wait_recv()
            self.share(1 + side, 1 - side)

    def finish_far(self):
        for side in range(2):
            self.far(side, 3).wait_recv()
            self.share(3, side)

    def drain(self):
        for side in range(2):
            for h in range(2):
                self.near(side, 0, h).wait_send()
            self.far(side, 1 + side).wait_send()
        for index in range(4 if self.shared else 0):
            for h in range(2):
                self.give(index, h).wait_send()


class Place:
    def __init__(self, ny, nz, nx):
        e = lax.axis_index("enc")
        s = lax.axis_index("seq")
        self.e, self.s = e, s
        self.core, self.y = lax.rem(e, 2), lax.div(e, 2)
        self.z, self.x = lax.div(s, nx), lax.rem(s, nx)
        up, down = wrap(self.y + 1, ny), wrap(self.y - 1, ny)
        self.ys = (self.y, down, up, wrap(self.y + 2, ny))
        self.y_side = ((up * 2 + self.core, s), (down * 2 + self.core, s))
        self.sibling = (e + 1 - 2 * self.core, s)
        self.x_side = tuple((e, self.z * nx + wrap(self.x + d, nx)) for d in (1, -1))
        self.z_side = tuple((e, wrap(self.z + d, nz) * nx + self.x) for d in (1, -1))
        self.cols = (self.x, wrap(self.x - 1, nx), wrap(self.x + 1, nx), wrap(self.x + 2, nx))


class PlaneAttention:
    def __init__(self, place, kv, q3, mx, den, acc, sems, nz, nx):
        self.place, self.kv, self.q3, self.mx, self.den, self.acc, self.nz, self.nx = place, kv, q3, mx, den, acc, nz, nx
        self.xs, self.xr, self.hs, self.hr, self.zs, self.zr, self.ss, self.sr = sems
        self.far = nz // 2
        self.half = kv.shape[3]
        self.rows = 2 * self.half
        self.heads = q3.shape[0]
        self.together = min(2, self.heads)
        self.group = self.together * self.rows

    def along_x(self, j, side, i):
        place = self.place
        slot = self.kv.at[self.row_at(j), place.core, place.cols[i]]
        return remote(slot, slot, place.x_side[side], self.xs.at[j, side], self.xr.at[j, side])

    def half_on(self, j, side, i):
        place = self.place
        part = pl.ds(side * (self.half // 2), self.half // 2)
        slot = self.kv.at[self.row_at(j), place.core, place.cols[i], part]
        return remote(slot, slot, place.x_side[side], self.hs.at[j, side], self.hr.at[j, side])

    def along_z(self, j, side, i, k):
        place = self.place
        slot = self.kv.at[self.row_at(j), place.core, place.cols[i]]
        at = 4 * (k - 1) + i
        return remote(slot, slot, place.z_side[side], self.zs.at[side, at], self.zr.at[side, at])

    def half_along_z(self, j, side):
        place = self.place
        slot = self.kv.at[self.row_at(j), place.core, place.x, pl.ds(side * (self.half // 2), self.half // 2)]
        at = 4 * (self.far - 1)
        return remote(slot, slot, place.z_side[side], self.zs.at[side, at], self.zr.at[side, at])

    def give(self, j, mine=True):
        place = self.place
        slot = self.kv.at[self.row_at(j), place.core if mine else 1 - place.core]
        return remote(slot, slot, place.sibling, self.ss.at[j], self.sr.at[j])

    def row_at(self, j):
        k = (j + 1) // 2
        return wrap(self.place.z - k, self.nz) if j % 2 == 1 else wrap(self.place.z + k, self.nz)

    def ring_rows(self, k):
        far = self.far
        return [] if not 0 <= k <= far else [0] if k == 0 else [2 * k - 1] if k == far else [2 * k - 1, 2 * k]

    def comes(self, side, k):
        z = self.place.z
        return z >= k if side == 0 else wrap(z + k, self.nz) < self.far

    def goes(self, side, k):
        z = self.place.z
        if side == 0:
            return (z >= k - 1) & (z <= self.nz - 2)
        return wrap(z + k - 1, self.nz) < self.far

    def needed(self, j):
        k = (j + 1) // 2
        z = self.place.z
        return z >= k if j % 2 == 1 else z + k >= self.nz if j else z >= 0

    def start(self):
        for side in range(2):
            self.along_x(0, side, 0).start()

            @pl.when(self.goes(side, 1))
            def _(side=side):
                self.along_z(0, side, 0, 1).start()

    def compute(self, row, c, restrict=None):
        block = self.kv[row, c]
        high = jnp.concatenate([block[i, :, :HD] for i in range(self.nx)], axis=1)
        low = jnp.concatenate([block[i, :, HD : 2 * HD] for i in range(self.nx)], axis=1)
        v = block[:, :, 2 * HD :].reshape(self.nx * self.half, HD)
        stacked = jnp.concatenate([high, low, high], axis=0)
        queries = [
            self.q3[h : h + self.together].reshape(self.group, 3 * HD) for h in range(0, self.heads, self.together)
        ]
        scores = [jnp.dot(query, stacked, preferred_element_type=jnp.float32) for query in queries]
        for i, score in enumerate(scores):
            at = slice(i * self.group, (i + 1) * self.group)
            if restrict is not None:
                score = jnp.concatenate([restrict(n, score[:, n * HD : (n + 1) * HD]) for n in range(self.nx)], axis=1)
            new = jnp.maximum(self.mx[at], jnp.max(score, axis=1, keepdims=True))
            weights = jnp.exp2(score - jnp.concatenate([new] * self.nx, axis=1))
            summed = weights[:, :HD]
            for n in range(1, self.nx):
                summed = summed + weights[:, n * HD : (n + 1) * HD]
            product = jnp.dot(weights.astype(jnp.bfloat16), v, preferred_element_type=jnp.float32)
            factor = jnp.exp2(self.mx[at] - new)
            self.den[at] = self.den[at] * factor + summed
            self.acc[at] = self.acc[at] * factor + product
            self.mx[at] = new

    def own_row(self, c):
        x = self.place.x
        shape = (self.group, HD)
        token = lax.broadcasted_iota(jnp.int32, shape, 0) & (self.rows - 1)
        ahead = lax.broadcasted_iota(jnp.int32, shape, 1) - token

        def restrict(i, piece):
            limit = jnp.where(x > i, 2 * self.rows, jnp.where(x == i, 0, -2 * self.rows)) - c * self.half
            return jnp.where(ahead <= limit, piece, NEG)

        self.compute(self.place.z, c, restrict)

    def pass_rows(self, k, chosen):
        far = self.far
        if not 1 <= k <= far:
            return
        for side in range(2):
            j = min(2 * k - 1 + side, 2 * far - 1)
            mine = [i for i in chosen if k < far or i // 2 == side]
            onward = [i for i in chosen if k + 1 < far or (k + 1 == far and i // 2 == side)]

            @pl.when(self.comes(side, k))
            def _(side=side, j=j, mine=mine):
                for i in mine:
                    self.along_z(j, side, i, k).wait_recv()

            if onward:
                @pl.when(self.goes(side, k + 1))
                def _(side=side, j=j, onward=onward):
                    for i in onward:
                        self.along_z(j, side, i, k + 1).start()

    def early(self, t):
        far = self.far

        @pl.when(self.place.core == 0)
        def _():
            if t == 1:
                for side in range(2):
                    self.along_x(0, side, 1 + side).wait_recv()
                    self.half_on(0, side, 1 + side).start()
                    for direction in range(2):
                        @pl.when(self.goes(direction, 1))
                        def _(side=side, direction=direction):
                            self.along_z(0, direction, 1 + side, 1).start()
            self.pass_rows(t - 2, (0, 1))

        @pl.when(self.place.core == 1)
        def _():
            if 1 <= t <= far:
                for side in range(2):
                    j = min(2 * t - 1 + side, 2 * far - 1)

                    @pl.when(self.comes(side, t))
                    def _(side=side, j=j):
                        if t < far:
                            self.along_z(j, side, 0, t).wait_recv()
                        else:
                            self.half_along_z(j, side).wait_recv()

                    if t < far:
                        @pl.when(self.goes(side, t + 1))
                        def _(side=side, j=j):
                            if t + 1 < far:
                                self.along_z(j, side, 0, t + 1).start()
                            else:
                                self.half_along_z(j, side).start()
                for j in self.ring_rows(t):
                    @pl.when(self.needed(j))
                    def _(j=j):
                        for side in range(2):
                            self.along_x(j, side, 0).start()
            for j in self.ring_rows(t - 1):
                @pl.when(self.needed(j))
                def _(j=j):
                    for side in range(2):
                        self.along_x(j, side, 1 + side).wait_recv()
                        self.half_on(j, side, 1 + side).start()

    def from_sibling(self, k):
        for j in self.ring_rows(k):
            @pl.when(self.needed(j))
            def _(j=j):
                self.give(j, mine=False).wait_recv()

    def late(self, t):
        @pl.when(self.place.core == 0)
        def _():
            if t == 2:
                for side in range(2):
                    self.half_on(0, side, 3).wait_recv()
                for direction in range(2):
                    @pl.when(self.goes(direction, 1))
                    def _(direction=direction):
                        self.along_z(0, direction, 3, 1).start()
            self.pass_rows(t - 2, (2, 3))

        for j in self.ring_rows(t - 2):
            @pl.when(self.needed(j))
            def _(j=j):
                @pl.when(self.place.core == 1)
                def _():
                    for side in range(2):
                        self.half_on(j, side, 3).wait_recv()

                self.give(j).start()

    def run(self, queries_here):
        core, far, z, nz = self.place.core, self.far, self.place.z, self.nz
        self.mx[...] = jnp.full(self.mx.shape, NEG, jnp.float32)
        self.den[...] = jnp.zeros(self.den.shape, jnp.float32)
        self.acc[...] = jnp.zeros(self.acc.shape, jnp.float32)

        def phase(i, carry):
            for t in range(1, far + 4):
                @pl.when(i == 2 * t - 2)
                def _(t=t):
                    self.early(t)
                    if t > 3:
                        self.from_sibling(t - 3)

                @pl.when(i == 2 * t - 1)
                def _(t=t):
                    self.late(t)
                    if t == 2:
                        queries_here()
                    if t == 3:
                        self.from_sibling(0)

            @pl.when((i == 3) | (i == 5))
            def _():
                self.own_row(jnp.where(i == 3, core, 1 - core))

            odd = lax.rem(i, 2)
            k = lax.div(i, 2) - 2 + odd
            c = jnp.where(odd == 1, core, 1 - core)

            def attend(n, inner):
                row = wrap(z + k * (2 * n - 1), nz)

                @pl.when((k >= 1) & (k <= far) & (row < z) & ((k < far) | (n == 0)))
                def _():
                    self.compute(row, c)

                return inner

            lax.fori_loop(0, 2, attend, 0)
            return carry

        lax.fori_loop(0, 2 * (far + 3), phase, 0)

    def result(self, h):
        at = slice(h * self.rows, (h + 1) * self.rows)
        return self.acc[at] / jnp.sum(self.den[at], axis=1, keepdims=True)

    def drain(self):
        far = self.far
        for side in range(2):
            self.along_x(0, side, 0).wait_send()
            self.half_on(0, side, 1 + side).wait_send()
        for j in range(2 * far):
            @pl.when(self.needed(j))
            def _(j=j):
                self.give(j).wait_send()

                @pl.when((self.place.core == 1) & (j > 0))
                def _():
                    for side in range(2):
                        self.along_x(j, side, 0).wait_send()
                        self.half_on(j, side, 1 + side).wait_send()

        for side in range(2):
            for k in range(1, far + 1):
                @pl.when(self.goes(side, k))
                def _(side=side, k=k):
                    j = 0 if k == 1 else 2 * k - 3 + side

                    @pl.when(self.place.core == 0)
                    def _():
                        for i in range(4):
                            if k < far or i // 2 == side:
                                self.along_z(j, side, i, k).wait_send()

                    @pl.when(self.place.core == 1)
                    def _():
                        if k < far:
                            self.along_z(j, side, 0, k).wait_send()
                        else:
                            self.half_along_z(j, side).wait_send()


def prefill(
    patches, gain, up_t, up_bias, merge_down, down_bias, text, lengths, offsets, input_gain, qkv_weight, qkv_bias, freq,
    ny, nz, nx,
):
    patch_rows, vision = patches.shape
    units, joined = up_t.shape
    padded = -(-units // HD) * HD
    part = patch_rows // 4
    pad = -(-part // 16) * 16
    blocks = 2 * ny
    wide = 2 * text.shape[1]
    groups = nz * nx
    slots = groups * LMAX
    rows, width = text.shape
    half = rows // 2
    model = merge_down.shape[1]
    query_width = qkv_weight.shape[1] - HD
    heads = query_width // HD
    far = nz // 2

    def kernel(
        p_ref, g_ref, up_hbm, ub_ref, down_hbm, db_ref, text_ref, len_s, off_s, len_v, off_v, gain_ref, qkv_hbm, qb_ref,
        freq_ref, o_ref,
        buf, turned, up, hid, out, inn, down, w_q, w_kv, qkv_bias_of, down_bias_of, text_of, placed_out, placed_in, placed_mine,
        merged_sum, turn_cos, turn_sin, gain_row, own, rel_out, rel_in, d_out, d_in, full, squares, normed, kv, q3, mx, den, acc,
        w_sem, c_send, c_recv, a_send, a_recv, r_send, r_recv, d_send, d_recv,
        fns, fnr, ffs, ffr, fgs, fgr, bns, bnr, bfs, bfr,
        xs, xr, hs, hr, zs, zr, ss, sr,
    ):
        place = Place(ny, nz, nx)
        e, s, core, z, x = place.e, place.s, place.core, place.z, place.x
        other = 1 - core

        query_at, rest_at = pl.ds(0, query_width), pl.ds(query_width, HD)

        def lanes(c, size):
            return pl.ds(pl.multiple_of(c * size, size), size)

        def tokens(c):
            return pl.ds(pl.multiple_of(c * half, half), half)

        loads = (
            pltpu.make_async_copy(up_hbm, turned, w_sem.at[0]),
            pltpu.make_async_copy(down_hbm, down.at[core], w_sem.at[1]),
            pltpu.make_async_copy(qkv_hbm.at[:, rest_at], w_kv.at[:, lanes(core, HD)], w_sem.at[2]),
            pltpu.make_async_copy(qkv_hbm.at[:, query_at], w_q, w_sem.at[3]),
        )
        for load in loads:
            load.start()

        def to_sibling(i, src, dst):
            return remote(src, dst, place.sibling, c_send.at[i], c_recv.at[i])

        def gift(i, c):
            return (
                lambda: to_sibling(0, qkv_bias_of.at[core], qkv_bias_of.at[c]),
                lambda: to_sibling(1, down_bias_of.at[core], down_bias_of.at[c]),
                lambda: to_sibling(2, text_ref.at[tokens(other)], text_of.at[:, lanes(c, width)]),
                lambda: to_sibling(3, qkv_hbm.at[:, rest_at], w_kv.at[:, lanes(c, HD)]),
                lambda: to_sibling(4, down_hbm, down.at[c]),
                lambda: to_sibling(5, normed.at[core], normed.at[c]),
                lambda: to_sibling(6, placed_out, placed_in),
            )[i]()

        barrier = pltpu.get_barrier_semaphore()

        def greet(p, carry):
            pl.semaphore_signal(barrier, inc=1, device_id=(e, wrap(s + p, groups)), device_id_type=MESH)
            return carry

        lax.fori_loop(1, groups, greet, 0)
        for to in (*place.y_side, place.sibling):
            pl.semaphore_signal(barrier, inc=1, device_id=to, device_id_type=MESH)

        front = EncGather(
            place, lambda y, c, h: buf.at[y, c, pl.ds(2 * h, 2)], (fns, fnr, ffs, ffr, fgs, fgr), shared=True
        )
        values = p_ref[...].astype(jnp.float32)
        mean_square = jnp.mean(values * values, axis=1, keepdims=True)
        vision_rows = (values * lax.rsqrt(mean_square + EPSILON) * g_ref[...].reshape(1, vision)).astype(jnp.bfloat16)
        to = lax.broadcasted_iota(jnp.int32, (4 * pad, patch_rows), 0)
        source = lax.broadcasted_iota(jnp.int32, (4 * pad, patch_rows), 1)
        moved = (source == 4 * (to % pad) + to // pad) & (to % pad < part)
        order = jnp.where(moved, 1.0, 0.0).astype(jnp.bfloat16)
        sorted_rows = jnp.dot(order, vision_rows, preferred_element_type=jnp.float32).astype(jnp.bfloat16)
        for q in range(4):
            buf[place.y, core, q] = sorted_rows[q * pad : (q + 1) * pad]
        pl.semaphore_wait(barrier, groups - 1 + 3)
        front.start(0)
        front.start(1)
        qkv_bias_of[core] = qb_ref[...].reshape(1, query_width + HD)
        down_bias_of[core] = db_ref[...].reshape(1, width)
        for i in range(5):
            gift(i, core).start()
        text_of[:, lanes(core, width)] = text_ref[tokens(core)]

        loads[0].wait()
        def turn(i, carry):
            at = pl.ds(pl.multiple_of(i * 512, 512), 512)
            up[at, :] = turned[:, at].T
            return carry

        turns = joined // 512
        lax.fori_loop(0, turns // 2, turn, 0)
        front.relay()
        lax.fori_loop(turns // 2, turns, turn, 0)
        front.finish_near()

        lane = lax.broadcasted_iota(jnp.int32, (1, blocks * pad), 1)
        merged = jnp.where(lane % pad < part, lane // pad * part + lane % pad, -1)
        code = jnp.full((1, blocks * pad), -1, jnp.int32)
        begin = jnp.int32(0)
        for j in range(len_s.shape[0]):
            end = begin + len_s[j, s]
            inside = (merged >= begin) & (merged < end)
            code = jnp.where(inside, off_s[j, s] // rows * LMAX + merged - begin, code)
            begin = end
        slot = lax.broadcasted_iota(jnp.int32, (slots, blocks * pad), 0)
        pick = jnp.where(slot == code, 1.0, 0.0).astype(jnp.bfloat16)

        ours = off_v[...] // rows == s
        first = jnp.sum(jnp.where(ours, off_v[...] - s * rows, 0).astype(jnp.float32), axis=0, keepdims=True)
        count = jnp.sum(jnp.where(ours, len_v[...], 0).astype(jnp.float32), axis=0, keepdims=True)
        group = lax.broadcasted_iota(jnp.int32, (groups, slots), 0)
        position = lax.broadcasted_iota(jnp.int32, (groups, slots), 1)
        spread_groups = jnp.where(position // LMAX == group, 1.0, 0.0).astype(jnp.bfloat16)
        both = jnp.concatenate([jnp.broadcast_to(first, (8, groups)), jnp.broadcast_to(count, (8, groups))], axis=0)
        both = jnp.dot(both.astype(jnp.bfloat16), spread_groups, preferred_element_type=jnp.float32)
        index = (lax.broadcasted_iota(jnp.int32, (1, slots), 1) % LMAX).astype(jnp.float32)
        target = jnp.where(index < both[8:9], both[:1] + index, -1.0)
        token = lax.broadcasted_iota(jnp.int32, (half, slots), 0)

        def placing(c):
            return jnp.where((token + c * half).astype(jnp.float32) == target, 1.0, 0.0)

        covered = jnp.sum(placing(core), axis=1, keepdims=True) > 0.5

        out[...] = jnp.zeros(out.shape, jnp.bfloat16)

        def merge(*chips):
            count = len(chips) * 2 * pad
            merged_sum[:count] = jnp.broadcast_to(ub_ref[...].reshape(1, units), (count, units))

            def add_part(q, carry):
                grouped = jnp.concatenate([buf[y, :, q].reshape(2 * pad, vision) for y in chips], axis=0)
                weights = up[pl.ds(pl.multiple_of(q * vision, vision), vision), :]
                merged_sum[:count] += jnp.dot(grouped, weights, preferred_element_type=jnp.float32)
                return carry

            lax.fori_loop(0, 4, add_part, 0)
            inner = merged_sum[:count]
            inner = (0.5 * inner * (1.0 + lax.erf(inner * math.sqrt(0.5)))).astype(jnp.bfloat16)
            for i, y in enumerate(chips):
                hid[y] = inner[i * 2 * pad : (i + 1) * 2 * pad]

        front.take(0)
        merge(place.ys[0])
        front.take(1)
        front.take(2)
        merge(place.ys[1], place.ys[2])
        front.finish_far()
        front.take(3)
        merge(place.ys[3])

        chosen = jnp.dot(pick, hid[...].reshape(blocks * pad, units), preferred_element_type=jnp.float32)
        out[:, :, :units] = chosen.astype(jnp.bfloat16).reshape(groups, LMAX, units)

        def swap(p, at, arrives):
            return remote(out.at[at], inn.at[arrives], (e, at), a_send.at[p], a_recv.at[p])

        def begin_swap(p, carry):
            swap(p, wrap(s + p, groups), s).start()
            return carry

        lax.fori_loop(1, groups, begin_swap, 0)
        inn[s] = out[s]
        def end_swap(p, carry):
            swap(p, wrap(s + p, groups), wrap(s - p + groups, groups)).wait_recv()
            return carry

        lax.fori_loop(1, groups, end_swap, 0)
        arrived = inn[:, :, :units].reshape(slots, units)

        def place_tokens(c):
            return jnp.dot(
                placing(c).astype(jnp.bfloat16), arrived, preferred_element_type=jnp.float32
            ).astype(jnp.bfloat16)

        placed_out[...] = place_tokens(other)
        gift(6, core).start()
        placed_mine[...] = place_tokens(core)

        def share(hidden_rows, c, y_to):
            return jnp.dot(hidden_rows, down[c, :, lanes(y_to, wide)], preferred_element_type=jnp.float32)

        def relay(side):
            return remote(rel_out.at[side], rel_in.at[side], place.y_side[side], r_send.at[side], r_recv.at[side])

        def deliver(side, h):
            return remote(
                d_out.at[side, h], d_in.at[side, h], place.y_side[side], d_send.at[side, h], d_recv.at[side, h]
            )

        halves = (slice(0, half // 2), slice(half // 2, half))
        loads[1].wait()
        def target(i):
            return wrap(place.y + jnp.where(i == 0, 2, jnp.where(i == 1, 1, jnp.where(i == 2, -1, 0))), ny)

        def add_own(i, carry):
            own[i] = share(placed_mine[...], core, target(i))
            return carry

        def add_other(i, carry):
            own[i] += share(placed_in[...], other, target(i))
            return carry

        lax.fori_loop(0, 4, add_own, 0)
        gift(4, other).wait_recv()
        gift(6, other).wait_recv()
        for i in range(3):
            lax.fori_loop(i, i + 1 if i < 2 else 4, add_other, 0)
            for side in range(2):
                if i == 0:
                    rel_out[side] = own[0, halves[side]].astype(jnp.bfloat16)
                    relay(side).start()
                if i == 1 + side:
                    d_out[side, 1 - side] = own[i, halves[1 - side]].astype(jnp.bfloat16)
                    deliver(side, 1 - side).start()
        gift(1, other).wait_recv()
        gift(2, other).wait_recv()
        own[3] = own[3] + jnp.concatenate([down_bias_of[0], down_bias_of[1]], axis=1)
        for side in range(2):
            relay(side).wait_recv()
            d_out[side, side] = (own[1 + side, halves[side]] + rel_in[side].astype(jnp.float32)).astype(jnp.bfloat16)
            deliver(side, side).start()

        for c in range(2):
            token_id = lax.broadcasted_iota(jnp.int32, (half, HD), 0) + s * rows + c * half
            sine, cosine = sine_cosine(token_id.astype(jnp.float32) * freq_ref[...])
            turn_cos[c] = cosine
            turn_sin[c] = jnp.where(lax.broadcasted_iota(jnp.int32, (half, HD), 1) < HD // 2, -sine, sine)

        def rotate(block, c):
            return block * turn_cos[c] + pltpu.roll(block, HD // 2, 1) * turn_sin[c]

        back = EncGather(
            place, lambda y, c, h: full.at[y, pl.ds(h * (half // 2), half // 2)], (bns, bnr, bfs, bfr, None, None), shared=False
        )
        for h in range(2):
            at = halves[h]
            total = own[3, at]
            for side in range(2):
                deliver(side, h).wait_recv()
                total = total + d_in[side, h].astype(jnp.float32)
            kept = jnp.where(covered[at], total, text_of[at].astype(jnp.float32))
            full[place.y, at] = kept.astype(jnp.bfloat16)
            back.start(h)
        squares[...] = jnp.zeros(squares.shape, jnp.float32)

        def add_squares(y):
            block = full[y].astype(jnp.float32)
            block = block * block
            summed = block[:, :HD]
            for g in range(1, wide // HD):
                summed = summed + block[:, g * HD : (g + 1) * HD]
            squares[...] += summed

        add_squares(place.ys[0])
        back.relay()
        back.finish_near()
        for i in range(1, 3):
            add_squares(place.ys[i])
        back.finish_far()
        add_squares(place.ys[3])

        scale = lax.rsqrt(jnp.sum(squares[...], axis=1, keepdims=True) * (1.0 / model) + EPSILON)
        gain_row[...] = gain_ref[...].reshape(1, model)

        def norm_part(y, carry):
            at = lanes(y, wide)
            normed[core, :, at] = (full[y].astype(jnp.float32) * scale * gain_row[:, at]).astype(jnp.bfloat16)
            return carry

        lax.fori_loop(0, ny, norm_part, 0)
        gift(5, core).start()
        loads[2].wait()
        gift(0, other).wait_recv()
        gift(3, other).wait_recv()
        both = jnp.dot(normed[core], w_kv[...], preferred_element_type=jnp.float32)
        key = rotate(both[:, :HD] + qkv_bias_of[0, :, query_width:], core).T
        key_high = key.astype(jnp.bfloat16)
        kv[z, core, x, :, :HD] = key_high
        kv[z, core, x, :, HD : 2 * HD] = (key - key_high.astype(jnp.float32)).astype(jnp.bfloat16)
        kv[z, core, x, :, 2 * HD :] = (both[:, HD:] + qkv_bias_of[1, :, query_width:]).astype(jnp.bfloat16)

        plane = PlaneAttention(place, kv, q3, mx, den, acc, (xs, xr, hs, hr, zs, zr, ss, sr), nz, nx)
        plane.start()

        scaling = HD ** (-0.5) * math.log2(math.e)
        loads[3].wait()

        def project(i, carry):
            pairs = heads // 2
            c = jnp.where(i < pairs, core, other)
            first_head = 2 * lax.rem(i, pairs)

            @pl.when(i == pairs)
            def _():
                gift(5, other).wait_recv()

            at = pl.ds(pl.multiple_of(first_head * HD, 2 * HD), 2 * HD)
            query = jnp.dot(normed[c], w_q[:, at], preferred_element_type=jnp.float32) + qkv_bias_of[core, :, at]
            for n in range(2):
                head = rotate(query[:, n * HD : (n + 1) * HD], c) * scaling
                high = head.astype(jnp.bfloat16)
                low = (head - high.astype(jnp.float32)).astype(jnp.bfloat16)
                q3[first_head + n, c, :, :HD] = high
                q3[first_head + n, c, :, HD : 2 * HD] = high
                q3[first_head + n, c, :, 2 * HD :] = low
            return carry

        lax.fori_loop(0, heads, project, 0)
        plane.run(lambda: None)
        for h in range(heads):
            o_ref[:, h * HD : (h + 1) * HD] = plane.result(h).astype(o_ref.dtype)

        def sent_swap(p, carry):
            swap(p, wrap(s + p, groups), s).wait_send()
            return carry

        lax.fori_loop(1, groups, sent_swap, 0)
        front.drain()
        back.drain()
        for i in range(7):
            gift(i, core).wait_send()
        for side in range(2):
            relay(side).wait_send()
            for h in range(2):
                deliver(side, h).wait_send()
        plane.drain()

    dma = pltpu.SemaphoreType.DMA
    bf16, f32 = jnp.bfloat16, jnp.float32
    vmem = pl.BlockSpec(memory_space=pltpu.VMEM)
    smem = pl.BlockSpec(memory_space=pltpu.SMEM)
    any_space = pl.BlockSpec(memory_space=pl.ANY)
    enc_sems = [dma((2, 2)), dma((2, 2)), dma((2,)), dma((2,)), dma((4, 2)), dma((4, 2))]
    return pl.pallas_call(
        kernel,
        out_shape=jax.ShapeDtypeStruct((rows, query_width), bf16),
        in_specs=[
            vmem, vmem, any_space, vmem, any_space, vmem, vmem, smem, smem, vmem, vmem, vmem, any_space, vmem, vmem,
        ],
        out_specs=vmem,
        scratch_shapes=[
            pltpu.VMEM((ny, 2, 4, pad, vision), bf16),
            pltpu.VMEM((units, joined), bf16),
            pltpu.VMEM((joined, units), bf16),
            pltpu.VMEM((ny, 2 * pad, units), bf16),
            pltpu.VMEM((groups, LMAX, padded), bf16),
            pltpu.VMEM((groups, LMAX, padded), bf16),
            pltpu.VMEM((2, *merge_down.shape), bf16),
            pltpu.VMEM((model, query_width), bf16),
            pltpu.VMEM((model, 2 * HD), bf16),
            pltpu.VMEM((2, 1, query_width + HD), f32),
            pltpu.VMEM((2, 1, width), f32),
            pltpu.VMEM((half, wide), bf16),
            pltpu.VMEM((half, units), bf16),
            pltpu.VMEM((half, units), bf16),
            pltpu.VMEM((half, units), bf16),
            pltpu.VMEM((4 * pad, units), f32),
            pltpu.VMEM((2, half, HD), f32),
            pltpu.VMEM((2, half, HD), f32),
            pltpu.VMEM((1, model), f32),
            pltpu.VMEM((4, half, wide), f32),
            pltpu.VMEM((2, half // 2, wide), bf16),
            pltpu.VMEM((2, half // 2, wide), bf16),
            pltpu.VMEM((2, 2, half // 2, wide), bf16),
            pltpu.VMEM((2, 2, half // 2, wide), bf16),
            pltpu.VMEM((ny, half, wide), bf16),
            pltpu.VMEM((half, HD), f32),
            pltpu.VMEM((2, half, model), bf16),
            pltpu.VMEM((nz, 2, nx, half, 3 * HD), bf16),
            pltpu.VMEM((heads, 2, half, 3 * HD), bf16),
            pltpu.VMEM((heads * rows, HD), f32),
            pltpu.VMEM((heads * rows, HD), f32),
            pltpu.VMEM((heads * rows, HD), f32),
            dma((4,)),
            dma((7,)),
            dma((7,)),
            dma((groups,)),
            dma((groups,)),
            dma((2,)),
            dma((2,)),
            dma((2, 2)),
            dma((2, 2)),
            *enc_sems,
            *enc_sems[:4],
            dma((nz, 2)),
            dma((nz, 2)),
            dma((nz, 2)),
            dma((nz, 2)),
            dma((2, 4 * far)),
            dma((2, 4 * far)),
            dma((nz,)),
            dma((nz,)),
        ],
        compiler_params=pltpu.CompilerParams(
            collective_id=1, has_side_effects=True, vmem_limit_bytes=56 * 1024 * 1024
        ),
        name="prefill",
    )(
        patches, gain, up_t, up_bias, merge_down, down_bias, text, lengths, offsets, lengths, offsets, input_gain,
        qkv_weight, qkv_bias, freq,
    )


def local(
    patches, vision_gain, merge_up, merge_up_bias, merge_down, merge_down_bias, text_embed, image_lengths, image_offsets,
    input_gain, qkv_weight, qkv_bias,
):
    freq = np.exp(np.arange(HD // 2) * (-2.0 * np.log(THETA) / HD)).astype(np.float32)
    return prefill(
        patches[0], vision_gain, merge_up.T, merge_up_bias, merge_down, merge_down_bias, text_embed,
        image_lengths.T, image_offsets.T, input_gain, qkv_weight, qkv_bias,
        jnp.asarray(np.concatenate([freq, freq])[None]),
        lax.axis_size("enc") // 2, lax.axis_size("seq") // NX, NX,
    )


def solution(mesh):
    in_specs = (
        P("seq", "enc", None),
        P(),
        P(None, "enc"),
        P("enc"),
        P("enc", None),
        P("enc"),
        P("seq", "enc"),
        P(),
        P(),
        P(),
        P(None, "enc"),
        P("enc"),
    )
    out_specs = P("seq", "enc")
    return jax.shard_map(local, mesh=mesh, in_specs=in_specs, out_specs=out_specs, check_vma=False)
```

```python
import math

import jax
import jax.numpy as jnp
import numpy as np
from jax import lax
from jax.experimental import pallas as pl
from jax.experimental.pallas import tpu as pltpu
from jax.sharding import PartitionSpec as P

HD = 128
LMAX = 16
NX = 4
EPSILON = 1e-06
THETA = 1000000.0
NEG = -1e30
MESH = pl.DeviceIdType.MESH


def wrap(value, size):
    return lax.rem(value + 2 * size, size)


def remote(src, dst, to, send_sem, recv_sem):
    return pltpu.make_async_remote_copy(
        src_ref=src, dst_ref=dst, send_sem=send_sem, recv_sem=recv_sem, device_id=to, device_id_type=MESH
    )


def sine_cosine(angle):
    turns = jnp.floor(angle * (2.0 / math.pi) + 0.5)
    rest = ((angle - turns * 1.5703125) - turns * 4.837512969970703125e-4) - turns * 7.54978995489188216e-8
    square = rest * rest
    sine = ((-1.9515295891e-4 * square + 8.3321608736e-3) * square - 1.6666654611e-1) * square * rest + rest
    cosine = (
        ((2.443315711809948e-5 * square - 1.388731625493765e-3) * square + 4.166664568298827e-2) * square * square
        - 0.5 * square
        + 1.0
    )
    quadrant = turns - 4.0 * jnp.floor(turns * 0.25)
    odd = (quadrant == 1.0) | (quadrant == 3.0)
    sine, cosine = jnp.where(odd, cosine, sine), jnp.where(odd, sine, cosine)
    sine = jnp.where(quadrant >= 2.0, -sine, sine)
    cosine = jnp.where((quadrant == 1.0) | (quadrant == 2.0), -cosine, cosine)
    return sine, cosine


class EncGather:
    def __init__(self, place, half, sems, shared):
        self.place, self.half, self.shared = place, half, shared
        self.near_send, self.near_recv, self.far_send, self.far_recv, self.give_send, self.give_recv = sems

    def near(self, side, index, h):
        place = self.place
        slot = self.half(place.ys[index], place.core, h)
        return remote(slot, slot, place.y_side[side], self.near_send.at[side, h], self.near_recv.at[side, h])

    def far(self, side, index):
        place = self.place
        slot = self.half(place.ys[index], place.core, side)
        return remote(slot, slot, place.y_side[side], self.far_send.at[side], self.far_recv.at[side])

    def give(self, index, h, mine=True):
        place = self.place
        slot = self.half(place.ys[index], place.core if mine else 1 - place.core, h)
        return remote(slot, slot, place.sibling, self.give_send.at[index, h], self.give_recv.at[index, h])

    def take(self, index):
        for h in range(2):
            self.give(index, h, mine=False).wait_recv()

    def start(self, h):
        for side in range(2):
            self.near(side, 0, h).start()
        self.share(0, h)

    def share(self, index, h):
        if self.shared:
            self.give(index, h).start()

    def relay(self):
        for side in range(2):
            self.near(side, 1 + side, side).wait_recv()
            self.far(side, 1 + side).start()
            self.share(1 + side, side)

    def finish_near(self):
        for side in range(2):
            self.near(side, 1 + side, 1 - side).wait_recv()
            self.share(1 + side, 1 - side)

    def finish_far(self):
        for side in range(2):
            self.far(side, 3).wait_recv()
            self.share(3, side)

    def drain(self):
        for side in range(2):
            for h in range(2):
                self.near(side, 0, h).wait_send()
            self.far(side, 1 + side).wait_send()
        for index in range(4 if self.shared else 0):
            for h in range(2):
                self.give(index, h).wait_send()


class Place:
    def __init__(self, ny, nz, nx):
        e = lax.axis_index("enc")
        s = lax.axis_index("seq")
        self.e, self.s = e, s
        self.core, self.y = lax.rem(e, 2), lax.div(e, 2)
        self.z, self.x = lax.div(s, nx), lax.rem(s, nx)
        up, down = wrap(self.y + 1, ny), wrap(self.y - 1, ny)
        self.ys = (self.y, down, up, wrap(self.y + 2, ny))
        self.y_side = ((up * 2 + self.core, s), (down * 2 + self.core, s))
        self.sibling = (e + 1 - 2 * self.core, s)
        self.x_side = tuple((e, self.z * nx + wrap(self.x + d, nx)) for d in (1, -1))
        self.z_side = tuple((e, wrap(self.z + d, nz) * nx + self.x) for d in (1, -1))
        self.cols = (self.x, wrap(self.x - 1, nx), wrap(self.x + 1, nx), wrap(self.x + 2, nx))


class PlaneAttention:
    def __init__(self, place, kv, q3, mx, den, acc, sems, nz, nx):
        self.place, self.kv, self.q3, self.mx, self.den, self.acc, self.nz, self.nx = place, kv, q3, mx, den, acc, nz, nx
        self.xs, self.xr, self.hs, self.hr, self.zs, self.zr, self.ss, self.sr = sems
        self.far = nz // 2
        self.half = kv.shape[3]
        self.rows = 2 * self.half
        self.heads = q3.shape[0]
        self.together = min(2, self.heads)
        self.group = self.together * self.rows

    def along_x(self, j, side, i):
        place = self.place
        slot = self.kv.at[self.row_at(j), place.core, place.cols[i]]
        return remote(slot, slot, place.x_side[side], self.xs.at[j, side], self.xr.at[j, side])

    def half_on(self, j, side, i):
        place = self.place
        part = pl.ds(side * (self.half // 2), self.half // 2)
        slot = self.kv.at[self.row_at(j), place.core, place.cols[i], part]
        return remote(slot, slot, place.x_side[side], self.hs.at[j, side], self.hr.at[j, side])

    def along_z(self, j, side, i, k):
        place = self.place
        slot = self.kv.at[self.row_at(j), place.core, place.cols[i]]
        at = 4 * (k - 1) + i
        return remote(slot, slot, place.z_side[side], self.zs.at[side, at], self.zr.at[side, at])

    def half_along_z(self, j, side):
        place = self.place
        slot = self.kv.at[self.row_at(j), place.core, place.x, pl.ds(side * (self.half // 2), self.half // 2)]
        at = 4 * (self.far - 1)
        return remote(slot, slot, place.z_side[side], self.zs.at[side, at], self.zr.at[side, at])

    def give(self, j, mine=True):
        place = self.place
        slot = self.kv.at[self.row_at(j), place.core if mine else 1 - place.core]
        return remote(slot, slot, place.sibling, self.ss.at[j], self.sr.at[j])

    def row_at(self, j):
        k = (j + 1) // 2
        return wrap(self.place.z - k, self.nz) if j % 2 == 1 else wrap(self.place.z + k, self.nz)

    def ring_rows(self, k):
        far = self.far
        return [] if not 0 <= k <= far else [0] if k == 0 else [2 * k - 1] if k == far else [2 * k - 1, 2 * k]

    def comes(self, side, k):
        z = self.place.z
        return z >= k if side == 0 else wrap(z + k, self.nz) < self.far

    def goes(self, side, k):
        z = self.place.z
        if side == 0:
            return (z >= k - 1) & (z <= self.nz - 2)
        return wrap(z + k - 1, self.nz) < self.far

    def needed(self, j):
        k = (j + 1) // 2
        z = self.place.z
        return z >= k if j % 2 == 1 else z + k >= self.nz if j else z >= 0

    def start(self):
        for side in range(2):
            self.along_x(0, side, 0).start()

            @pl.when(self.goes(side, 1))
            def _(side=side):
                self.along_z(0, side, 0, 1).start()

    def compute(self, row, c, restrict=None):
        block = self.kv[row, c]
        high = jnp.concatenate([block[i, :, :HD] for i in range(self.nx)], axis=1)
        low = jnp.concatenate([block[i, :, HD : 2 * HD] for i in range(self.nx)], axis=1)
        v = block[:, :, 2 * HD :].reshape(self.nx * self.half, HD)
        stacked = jnp.concatenate([high, low, high], axis=0)
        queries = [
            self.q3[h : h + self.together].reshape(self.group, 3 * HD) for h in range(0, self.heads, self.together)
        ]
        scores = [jnp.dot(query, stacked, preferred_element_type=jnp.float32) for query in queries]
        for i, score in enumerate(scores):
            at = slice(i * self.group, (i + 1) * self.group)
            if restrict is not None:
                score = jnp.concatenate([restrict(n, score[:, n * HD : (n + 1) * HD]) for n in range(self.nx)], axis=1)
            new = jnp.maximum(self.mx[at], jnp.max(score, axis=1, keepdims=True))
            weights = jnp.exp2(score - jnp.concatenate([new] * self.nx, axis=1))
            summed = weights[:, :HD]
            for n in range(1, self.nx):
                summed = summed + weights[:, n * HD : (n + 1) * HD]
            product = jnp.dot(weights.astype(jnp.bfloat16), v, preferred_element_type=jnp.float32)
            factor = jnp.exp2(self.mx[at] - new)
            self.den[at] = self.den[at] * factor + summed
            self.acc[at] = self.acc[at] * factor + product
            self.mx[at] = new

    def own_row(self, c):
        x = self.place.x
        shape = (self.group, HD)
        token = lax.broadcasted_iota(jnp.int32, shape, 0) & (self.rows - 1)
        ahead = lax.broadcasted_iota(jnp.int32, shape, 1) - token

        def restrict(i, piece):
            limit = jnp.where(x > i, 2 * self.rows, jnp.where(x == i, 0, -2 * self.rows)) - c * self.half
            return jnp.where(ahead <= limit, piece, NEG)

        self.compute(self.place.z, c, restrict)

    def pass_rows(self, k, chosen):
        far = self.far
        if not 1 <= k <= far:
            return
        for side in range(2):
            j = min(2 * k - 1 + side, 2 * far - 1)
            mine = [i for i in chosen if k < far or i // 2 == side]
            onward = [i for i in chosen if k + 1 < far or (k + 1 == far and i // 2 == side)]

            @pl.when(self.comes(side, k))
            def _(side=side, j=j, mine=mine):
                for i in mine:
                    self.along_z(j, side, i, k).wait_recv()

            if onward:
                @pl.when(self.goes(side, k + 1))
                def _(side=side, j=j, onward=onward):
                    for i in onward:
                        self.along_z(j, side, i, k + 1).start()

    def early(self, t):
        far = self.far

        @pl.when(self.place.core == 0)
        def _():
            if t == 1:
                for side in range(2):
                    self.along_x(0, side, 1 + side).wait_recv()
                    self.half_on(0, side, 1 + side).start()
                    for direction in range(2):
                        @pl.when(self.goes(direction, 1))
                        def _(side=side, direction=direction):
                            self.along_z(0, direction, 1 + side, 1).start()
            self.pass_rows(t - 2, (1,))
            self.pass_rows(t - 1, (0,))

        @pl.when(self.place.core == 1)
        def _():
            if 1 <= t <= far:
                for side in range(2):
                    j = min(2 * t - 1 + side, 2 * far - 1)

                    @pl.when(self.comes(side, t))
                    def _(side=side, j=j):
                        if t < far:
                            self.along_z(j, side, 0, t).wait_recv()
                        else:
                            self.half_along_z(j, side).wait_recv()

                    if t < far:
                        @pl.when(self.goes(side, t + 1))
                        def _(side=side, j=j):
                            if t + 1 < far:
                                self.along_z(j, side, 0, t + 1).start()
                            else:
                                self.half_along_z(j, side).start()
                for j in self.ring_rows(t):
                    @pl.when(self.needed(j))
                    def _(j=j):
                        for side in range(2):
                            self.along_x(j, side, 0).start()
            for j in self.ring_rows(t - 1):
                @pl.when(self.needed(j))
                def _(j=j):
                    for side in range(2):
                        self.along_x(j, side, 1 + side).wait_recv()
                        self.half_on(j, side, 1 + side).start()

    def from_sibling(self, k):
        for j in self.ring_rows(k):
            @pl.when(self.needed(j))
            def _(j=j):
                self.give(j, mine=False).wait_recv()

    def late(self, t):
        @pl.when(self.place.core == 0)
        def _():
            if t == 2:
                for side in range(2):
                    self.half_on(0, side, 3).wait_recv()
                for direction in range(2):
                    @pl.when(self.goes(direction, 1))
                    def _(direction=direction):
                        self.along_z(0, direction, 3, 1).start()
            self.pass_rows(t - 2, (2, 3))

        for j in self.ring_rows(t - 2):
            @pl.when(self.needed(j))
            def _(j=j):
                @pl.when(self.place.core == 1)
                def _():
                    for side in range(2):
                        self.half_on(j, side, 3).wait_recv()

                self.give(j).start()

    def run(self, queries_here):
        core, far, z, nz = self.place.core, self.far, self.place.z, self.nz
        self.mx[...] = jnp.full(self.mx.shape, NEG, jnp.float32)
        self.den[...] = jnp.zeros(self.den.shape, jnp.float32)
        self.acc[...] = jnp.zeros(self.acc.shape, jnp.float32)

        def phase(i, carry):
            for t in range(1, far + 4):
                @pl.when(i == 2 * t - 2)
                def _(t=t):
                    self.early(t)
                    if t > 3:
                        self.from_sibling(t - 3)

                @pl.when(i == 2 * t - 1)
                def _(t=t):
                    self.late(t)
                    if t == 1:
                        queries_here()
                    if t == 3:
                        self.from_sibling(0)

            @pl.when((i == 3) | (i == 5))
            def _():
                self.own_row(jnp.where(i == 3, core, 1 - core))

            odd = lax.rem(i, 2)
            k = lax.div(i, 2) - 2 + odd
            c = jnp.where(odd == 1, core, 1 - core)

            def attend(n, inner):
                row = wrap(z + k * (2 * n - 1), nz)

                @pl.when((k >= 1) & (k <= far) & (row < z) & ((k < far) | (n == 0)))
                def _():
                    self.compute(row, c)

                return inner

            lax.fori_loop(0, 2, attend, 0)
            return carry

        lax.fori_loop(0, 2 * (far + 3), phase, 0)

    def result(self, h):
        at = slice(h * self.rows, (h + 1) * self.rows)
        return self.acc[at] / jnp.sum(self.den[at], axis=1, keepdims=True)

    def drain(self):
        far = self.far
        for side in range(2):
            self.along_x(0, side, 0).wait_send()
            self.half_on(0, side, 1 + side).wait_send()
        for j in range(2 * far):
            @pl.when(self.needed(j))
            def _(j=j):
                self.give(j).wait_send()

                @pl.when((self.place.core == 1) & (j > 0))
                def _():
                    for side in range(2):
                        self.along_x(j, side, 0).wait_send()
                        self.half_on(j, side, 1 + side).wait_send()

        for side in range(2):
            for k in range(1, far + 1):
                @pl.when(self.goes(side, k))
                def _(side=side, k=k):
                    j = 0 if k == 1 else 2 * k - 3 + side

                    @pl.when(self.place.core == 0)
                    def _():
                        for i in range(4):
                            if k < far or i // 2 == side:
                                self.along_z(j, side, i, k).wait_send()

                    @pl.when(self.place.core == 1)
                    def _():
                        if k < far:
                            self.along_z(j, side, 0, k).wait_send()
                        else:
                            self.half_along_z(j, side).wait_send()


def prefill(
    patches, gain, up_t, up_bias, merge_down, down_bias, text, lengths, offsets, input_gain, qkv_weight, qkv_bias, freq,
    ny, nz, nx,
):
    patch_rows, vision = patches.shape
    units, joined = up_t.shape
    part = patch_rows // 4
    pad = -(-part // 16) * 16
    cut = -(-patch_rows // 32) * 16
    blocks = 2 * ny
    wide = 2 * text.shape[1]
    groups = nz * nx
    slots = groups * LMAX
    rows, width = text.shape
    half = rows // 2
    model = merge_down.shape[1]
    query_width = qkv_weight.shape[1] - HD
    heads = query_width // HD
    far = nz // 2

    def kernel(
        p_ref, g_ref, up_hbm, ub_ref, down_hbm, db_ref, text_ref, len_s, off_s, len_v, off_v, gain_ref, qkv_hbm, qb_ref,
        freq_ref, o_ref,
        buf, order, ordered, turned, up, hid, out, inn, down, w_q, w_kv, qkv_bias_of, down_bias_of, text_of, placed_out, placed_in, placed_mine,
        merged_sum, turn_cos, turn_sin, gain_row, own, rel_out, rel_in, d_out, d_in, full, squares, normed, kv, q3, mx, den, acc,
        w_sem, c_send, c_recv, a_send, a_recv, r_send, r_recv, d_send, d_recv,
        fns, fnr, ffs, ffr, fgs, fgr, bns, bnr, bfs, bfr,
        xs, xr, hs, hr, zs, zr, ss, sr,
    ):
        place = Place(ny, nz, nx)
        e, s, core, z, x = place.e, place.s, place.core, place.z, place.x
        other = 1 - core

        query_at, rest_at = pl.ds(0, query_width), pl.ds(query_width, HD)

        def lanes(c, size):
            return pl.ds(pl.multiple_of(c * size, size), size)

        def tokens(c):
            return pl.ds(pl.multiple_of(c * half, half), half)

        loads = (
            pltpu.make_async_copy(up_hbm, turned, w_sem.at[0]),
            pltpu.make_async_copy(down_hbm, down.at[core], w_sem.at[1]),
            pltpu.make_async_copy(qkv_hbm.at[:, rest_at], w_kv.at[:, lanes(core, HD)], w_sem.at[2]),
            pltpu.make_async_copy(qkv_hbm.at[:, query_at], w_q, w_sem.at[3]),
        )
        for load in loads:
            load.start()

        def to_sibling(i, src, dst):
            return remote(src, dst, place.sibling, c_send.at[i], c_recv.at[i])

        def gift(i, c):
            return (
                lambda: to_sibling(0, qkv_bias_of.at[core], qkv_bias_of.at[c]),
                lambda: to_sibling(1, down_bias_of.at[core], down_bias_of.at[c]),
                lambda: to_sibling(2, text_ref.at[tokens(other)], text_of.at[:, lanes(c, width)]),
                lambda: to_sibling(3, qkv_hbm.at[:, rest_at], w_kv.at[:, lanes(c, HD)]),
                lambda: to_sibling(4, down_hbm, down.at[c]),
                lambda: to_sibling(5, normed.at[core], normed.at[c]),
                lambda: to_sibling(6, placed_out, placed_in),
            )[i]()

        barrier = pltpu.get_barrier_semaphore()

        def greet(p, carry):
            pl.semaphore_signal(barrier, inc=1, device_id=(e, wrap(s + p, groups)), device_id_type=MESH)
            return carry

        lax.fori_loop(1, groups, greet, 0)
        for to in (*place.y_side, place.sibling):
            pl.semaphore_signal(barrier, inc=1, device_id=to, device_id_type=MESH)

        front = EncGather(
            place, lambda y, c, h: buf.at[y, c, pl.ds(h * cut, patch_rows - cut if h else cut)], (fns, fnr, ffs, ffr, fgs, fgr), shared=True
        )
        values = p_ref[...].astype(jnp.float32)
        mean_square = jnp.mean(values * values, axis=1, keepdims=True)
        buf[place.y, core] = (
            values * lax.rsqrt(mean_square + EPSILON) * g_ref[...].reshape(1, vision)
        ).astype(jnp.bfloat16)
        pl.semaphore_wait(barrier, groups - 1 + 3)
        front.start(0)
        front.start(1)
        qkv_bias_of[core] = qb_ref[...].reshape(1, query_width + HD)
        down_bias_of[core] = db_ref[...].reshape(1, width)
        for i in range(5):
            gift(i, core).start()
        text_of[:, lanes(core, width)] = text_ref[tokens(core)]

        loads[0].wait()
        def turn(i, carry):
            at = pl.ds(pl.multiple_of(i * 512, 512), 512)
            up[at, :] = turned[:, at].T
            return carry

        turns = joined // 512
        lax.fori_loop(0, turns // 2, turn, 0)
        front.relay()
        lax.fori_loop(turns // 2, turns, turn, 0)
        front.finish_near()

        to = lax.broadcasted_iota(jnp.int32, (4 * pad, patch_rows), 0)
        source = lax.broadcasted_iota(jnp.int32, (4 * pad, patch_rows), 1)
        moved = (source == 4 * (to % pad) + to // pad) & (to % pad < part)
        order[...] = jnp.where(moved, 1.0, 0.0).astype(jnp.bfloat16)

        lane = lax.broadcasted_iota(jnp.int32, (1, blocks * pad), 1)
        merged = jnp.where(lane % pad < part, lane // pad * part + lane % pad, -1)
        code = jnp.full((1, blocks * pad), -1, jnp.int32)
        begin = jnp.int32(0)
        for j in range(len_s.shape[0]):
            end = begin + len_s[j, s]
            inside = (merged >= begin) & (merged < end)
            code = jnp.where(inside, off_s[j, s] // rows * LMAX + merged - begin, code)
            begin = end
        slot = lax.broadcasted_iota(jnp.int32, (slots, blocks * pad), 0)
        pick = jnp.where(slot == code, 1.0, 0.0).astype(jnp.bfloat16)

        ours = off_v[...] // rows == s
        first = jnp.sum(jnp.where(ours, off_v[...] - s * rows, 0).astype(jnp.float32), axis=0, keepdims=True)
        count = jnp.sum(jnp.where(ours, len_v[...], 0).astype(jnp.float32), axis=0, keepdims=True)
        group = lax.broadcasted_iota(jnp.int32, (groups, slots), 0)
        position = lax.broadcasted_iota(jnp.int32, (groups, slots), 1)
        spread_groups = jnp.where(position // LMAX == group, 1.0, 0.0).astype(jnp.bfloat16)
        both = jnp.concatenate([jnp.broadcast_to(first, (8, groups)), jnp.broadcast_to(count, (8, groups))], axis=0)
        both = jnp.dot(both.astype(jnp.bfloat16), spread_groups, preferred_element_type=jnp.float32)
        index = (lax.broadcasted_iota(jnp.int32, (1, slots), 1) % LMAX).astype(jnp.float32)
        target = jnp.where(index < both[8:9], both[:1] + index, -1.0)
        token = lax.broadcasted_iota(jnp.int32, (half, slots), 0)

        def placing(c):
            return jnp.where((token + c * half).astype(jnp.float32) == target, 1.0, 0.0)

        covered = jnp.sum(placing(core), axis=1, keepdims=True) > 0.5

        def merge(*chips):
            count = len(chips) * 2 * pad

            def sort(c, carry):
                for i, y in enumerate(chips):
                    rows_of = jnp.dot(order[...], buf[y, c], preferred_element_type=jnp.float32)
                    ordered[:, i, c] = rows_of.astype(jnp.bfloat16).reshape(4, pad, vision)
                return carry

            lax.fori_loop(0, 2, sort, 0)
            merged_sum[:count] = jnp.broadcast_to(ub_ref[...].reshape(1, units), (count, units))

            def add_part(q, carry):
                grouped = ordered[q, : len(chips)].reshape(count, vision)
                weights = up[pl.ds(pl.multiple_of(q * vision, vision), vision), :]
                merged_sum[:count] += jnp.dot(grouped, weights, preferred_element_type=jnp.float32)
                return carry

            lax.fori_loop(0, 4, add_part, 0)
            inner = merged_sum[:count]
            inner = (0.5 * inner * (1.0 + lax.erf(inner * math.sqrt(0.5)))).astype(jnp.bfloat16)
            for i, y in enumerate(chips):
                hid[y] = inner[i * 2 * pad : (i + 1) * 2 * pad]

        front.take(0)
        merge(place.ys[0])
        front.take(1)
        front.take(2)
        merge(place.ys[1], place.ys[2])
        front.finish_far()
        front.take(3)
        merge(place.ys[3])

        chosen = jnp.dot(pick, hid[...].reshape(blocks * pad, units), preferred_element_type=jnp.float32)
        out[...] = chosen.astype(jnp.bfloat16).reshape(groups, LMAX, units)

        def swap(p, at, arrives):
            return remote(out.at[at], inn.at[arrives], (e, at), a_send.at[p], a_recv.at[p])

        def begin_swap(p, carry):
            swap(p, wrap(s + p, groups), s).start()
            return carry

        lax.fori_loop(1, groups, begin_swap, 0)
        inn[s] = out[s]
        def end_swap(p, carry):
            swap(p, wrap(s + p, groups), wrap(s - p + groups, groups)).wait_recv()
            return carry

        lax.fori_loop(1, groups, end_swap, 0)
        arrived = inn[...].reshape(slots, units)

        def place_tokens(c):
            return jnp.dot(
                placing(c).astype(jnp.bfloat16), arrived, preferred_element_type=jnp.float32
            ).astype(jnp.bfloat16)

        placed_out[...] = place_tokens(other)
        gift(6, core).start()
        placed_mine[...] = place_tokens(core)

        def share(hidden_rows, c, y_to):
            return jnp.dot(hidden_rows, down[c, :, lanes(y_to, wide)], preferred_element_type=jnp.float32)

        def relay(side):
            return remote(rel_out.at[side], rel_in.at[side], place.y_side[side], r_send.at[side], r_recv.at[side])

        def deliver(side, h):
            return remote(
                d_out.at[side, h], d_in.at[side, h], place.y_side[side], d_send.at[side, h], d_recv.at[side, h]
            )

        halves = (slice(0, half // 2), slice(half // 2, half))
        loads[1].wait()
        def target(i):
            return wrap(place.y + jnp.where(i == 0, 2, jnp.where(i == 1, 1, jnp.where(i == 2, -1, 0))), ny)

        def add_own(i, carry):
            own[i] = share(placed_mine[...], core, target(i))
            return carry

        def add_other(i, carry):
            own[i] += share(placed_in[...], other, target(i))
            return carry

        lax.fori_loop(0, 4, add_own, 0)
        gift(4, other).wait_recv()
        gift(6, other).wait_recv()
        for i in range(3):
            lax.fori_loop(i, i + 1 if i < 2 else 4, add_other, 0)
            for side in range(2):
                if i == 0:
                    rel_out[side] = own[0, halves[side]].astype(jnp.bfloat16)
                    relay(side).start()
                if i == 1 + side:
                    d_out[side, 1 - side] = own[i, halves[1 - side]].astype(jnp.bfloat16)
                    deliver(side, 1 - side).start()
        gift(1, other).wait_recv()
        gift(2, other).wait_recv()
        own[3] = own[3] + jnp.concatenate([down_bias_of[0], down_bias_of[1]], axis=1)
        for side in range(2):
            relay(side).wait_recv()
            d_out[side, side] = (own[1 + side, halves[side]] + rel_in[side].astype(jnp.float32)).astype(jnp.bfloat16)
            deliver(side, side).start()

        for c in range(2):
            token_id = lax.broadcasted_iota(jnp.int32, (half, HD), 0) + s * rows + c * half
            sine, cosine = sine_cosine(token_id.astype(jnp.float32) * freq_ref[...])
            turn_cos[c] = cosine
            turn_sin[c] = jnp.where(lax.broadcasted_iota(jnp.int32, (half, HD), 1) < HD // 2, -sine, sine)

        def rotate(block, c):
            return block * turn_cos[c] + pltpu.roll(block, HD // 2, 1) * turn_sin[c]

        back = EncGather(
            place, lambda y, c, h: full.at[y, pl.ds(h * (half // 2), half // 2)], (bns, bnr, bfs, bfr, None, None), shared=False
        )
        for h in range(2):
            at = halves[h]
            total = own[3, at]
            for side in range(2):
                deliver(side, h).wait_recv()
                total = total + d_in[side, h].astype(jnp.float32)
            kept = jnp.where(covered[at], total, text_of[at].astype(jnp.float32))
            full[place.y, at] = kept.astype(jnp.bfloat16)
            back.start(h)
        squares[...] = jnp.zeros(squares.shape, jnp.float32)

        def add_squares(y):
            block = full[y].astype(jnp.float32)
            block = block * block
            summed = block[:, :HD]
            for g in range(1, wide // HD):
                summed = summed + block[:, g * HD : (g + 1) * HD]
            squares[...] += summed

        add_squares(place.ys[0])
        back.relay()
        back.finish_near()
        for i in range(1, 3):
            add_squares(place.ys[i])
        back.finish_far()
        add_squares(place.ys[3])

        scale = lax.rsqrt(jnp.sum(squares[...], axis=1, keepdims=True) * (1.0 / model) + EPSILON)
        gain_row[...] = gain_ref[...].reshape(1, model)

        def norm_part(y, carry):
            at = lanes(y, wide)
            normed[core, :, at] = (full[y].astype(jnp.float32) * scale * gain_row[:, at]).astype(jnp.bfloat16)
            return carry

        lax.fori_loop(0, ny, norm_part, 0)
        gift(5, core).start()
        loads[2].wait()
        gift(0, other).wait_recv()
        gift(3, other).wait_recv()
        both = jnp.dot(normed[core], w_kv[...], preferred_element_type=jnp.float32)
        key = rotate(both[:, :HD] + qkv_bias_of[0, :, query_width:], core).T
        key_high = key.astype(jnp.bfloat16)
        kv[z, core, x, :, :HD] = key_high
        kv[z, core, x, :, HD : 2 * HD] = (key - key_high.astype(jnp.float32)).astype(jnp.bfloat16)
        kv[z, core, x, :, 2 * HD :] = (both[:, HD:] + qkv_bias_of[1, :, query_width:]).astype(jnp.bfloat16)

        plane = PlaneAttention(place, kv, q3, mx, den, acc, (xs, xr, hs, hr, zs, zr, ss, sr), nz, nx)
        plane.start()

        scaling = HD ** (-0.5) * math.log2(math.e)
        loads[3].wait()

        def project(i, carry):
            pairs = heads // 2
            c = jnp.where(i < pairs, core, other)
            first_head = 2 * lax.rem(i, pairs)

            at = pl.ds(pl.multiple_of(first_head * HD, 2 * HD), 2 * HD)
            query = jnp.dot(normed[c], w_q[:, at], preferred_element_type=jnp.float32) + qkv_bias_of[core, :, at]
            for n in range(2):
                head = rotate(query[:, n * HD : (n + 1) * HD], c) * scaling
                high = head.astype(jnp.bfloat16)
                low = (head - high.astype(jnp.float32)).astype(jnp.bfloat16)
                q3[first_head + n, c, :, :HD] = high
                q3[first_head + n, c, :, HD : 2 * HD] = high
                q3[first_head + n, c, :, 2 * HD :] = low
            return carry

        def sibling_tokens():
            gift(5, other).wait_recv()
            lax.fori_loop(heads // 2, heads, project, 0)

        lax.fori_loop(0, heads // 2, project, 0)
        plane.run(sibling_tokens)
        for h in range(heads):
            o_ref[:, h * HD : (h + 1) * HD] = plane.result(h).astype(o_ref.dtype)

        def sent_swap(p, carry):
            swap(p, wrap(s + p, groups), s).wait_send()
            return carry

        lax.fori_loop(1, groups, sent_swap, 0)
        front.drain()
        back.drain()
        for i in range(7):
            gift(i, core).wait_send()
        for side in range(2):
            relay(side).wait_send()
            for h in range(2):
                deliver(side, h).wait_send()
        plane.drain()

    dma = pltpu.SemaphoreType.DMA
    bf16, f32 = jnp.bfloat16, jnp.float32
    vmem = pl.BlockSpec(memory_space=pltpu.VMEM)
    smem = pl.BlockSpec(memory_space=pltpu.SMEM)
    any_space = pl.BlockSpec(memory_space=pl.ANY)
    enc_sems = [dma((2, 2)), dma((2, 2)), dma((2,)), dma((2,)), dma((4, 2)), dma((4, 2))]
    return pl.pallas_call(
        kernel,
        out_shape=jax.ShapeDtypeStruct((rows, query_width), bf16),
        in_specs=[
            vmem, vmem, any_space, vmem, any_space, vmem, vmem, smem, smem, vmem, vmem, vmem, any_space, vmem, vmem,
        ],
        out_specs=vmem,
        scratch_shapes=[
            pltpu.VMEM((ny, 2, patch_rows, vision), bf16),
            pltpu.VMEM((4 * pad, patch_rows), bf16),
            pltpu.VMEM((4, 2, 2, pad, vision), bf16),
            pltpu.VMEM((units, joined), bf16),
            pltpu.VMEM((joined, units), bf16),
            pltpu.VMEM((ny, 2 * pad, units), bf16),
            pltpu.VMEM((groups, LMAX, units), bf16),
            pltpu.VMEM((groups, LMAX, units), bf16),
            pltpu.VMEM((2, *merge_down.shape), bf16),
            pltpu.VMEM((model, query_width), bf16),
            pltpu.VMEM((model, 2 * HD), bf16),
            pltpu.VMEM((2, 1, query_width + HD), f32),
            pltpu.VMEM((2, 1, width), f32),
            pltpu.VMEM((half, wide), bf16),
            pltpu.VMEM((half, units), bf16),
            pltpu.VMEM((half, units), bf16),
            pltpu.VMEM((half, units), bf16),
            pltpu.VMEM((4 * pad, units), f32),
            pltpu.VMEM((2, half, HD), f32),
            pltpu.VMEM((2, half, HD), f32),
            pltpu.VMEM((1, model), f32),
            pltpu.VMEM((4, half, wide), f32),
            pltpu.VMEM((2, half // 2, wide), bf16),
            pltpu.VMEM((2, half // 2, wide), bf16),
            pltpu.VMEM((2, 2, half // 2, wide), bf16),
            pltpu.VMEM((2, 2, half // 2, wide), bf16),
            pltpu.VMEM((ny, half, wide), bf16),
            pltpu.VMEM((half, HD), f32),
            pltpu.VMEM((2, half, model), bf16),
            pltpu.VMEM((nz, 2, nx, half, 3 * HD), bf16),
            pltpu.VMEM((heads, 2, half, 3 * HD), bf16),
            pltpu.VMEM((heads * rows, HD), f32),
            pltpu.VMEM((heads * rows, HD), f32),
            pltpu.VMEM((heads * rows, HD), f32),
            dma((4,)),
            dma((7,)),
            dma((7,)),
            dma((groups,)),
            dma((groups,)),
            dma((2,)),
            dma((2,)),
            dma((2, 2)),
            dma((2, 2)),
            *enc_sems,
            *enc_sems[:4],
            dma((nz, 2)),
            dma((nz, 2)),
            dma((nz, 2)),
            dma((nz, 2)),
            dma((2, 4 * far)),
            dma((2, 4 * far)),
            dma((nz,)),
            dma((nz,)),
        ],
        compiler_params=pltpu.CompilerParams(
            collective_id=1, has_side_effects=True, vmem_limit_bytes=56 * 1024 * 1024
        ),
        name="prefill",
    )(
        patches, gain, up_t, up_bias, merge_down, down_bias, text, lengths, offsets, lengths, offsets, input_gain,
        qkv_weight, qkv_bias, freq,
    )


def local(
    patches, vision_gain, merge_up, merge_up_bias, merge_down, merge_down_bias, text_embed, image_lengths, image_offsets,
    input_gain, qkv_weight, qkv_bias,
):
    freq = np.exp(np.arange(HD // 2) * (-2.0 * np.log(THETA) / HD)).astype(np.float32)
    return prefill(
        patches[0], vision_gain, merge_up.T, merge_up_bias, merge_down, merge_down_bias, text_embed,
        image_lengths.T, image_offsets.T, input_gain, qkv_weight, qkv_bias,
        jnp.asarray(np.concatenate([freq, freq])[None]),
        lax.axis_size("enc") // 2, lax.axis_size("seq") // NX, NX,
    )


def solution(mesh):
    in_specs = (
        P("seq", "enc", None),
        P(),
        P(None, "enc"),
        P("enc"),
        P("enc", None),
        P("enc"),
        P("seq", "enc"),
        P(),
        P(),
        P(),
        P(None, "enc"),
        P("enc"),
    )
    out_specs = P("seq", "enc")
    return jax.shard_map(local, mesh=mesh, in_specs=in_specs, out_specs=out_specs, check_vma=False)
```

```python
import math

import jax
import jax.numpy as jnp
import numpy as np
from jax import lax
from jax.experimental import pallas as pl
from jax.experimental.pallas import tpu as pltpu
from jax.sharding import PartitionSpec as P

HD = 128
LMAX = 16
NX = 4
EPSILON = 1e-06
THETA = 1000000.0
NEG = -1e30
MESH = pl.DeviceIdType.MESH


def wrap(value, size):
    return lax.rem(value + 2 * size, size)


def remote(src, dst, to, send_sem, recv_sem):
    return pltpu.make_async_remote_copy(
        src_ref=src, dst_ref=dst, send_sem=send_sem, recv_sem=recv_sem, device_id=to, device_id_type=MESH
    )


def sine_cosine(angle):
    turns = jnp.floor(angle * (2.0 / math.pi) + 0.5)
    rest = ((angle - turns * 1.5703125) - turns * 4.837512969970703125e-4) - turns * 7.54978995489188216e-8
    square = rest * rest
    sine = ((-1.9515295891e-4 * square + 8.3321608736e-3) * square - 1.6666654611e-1) * square * rest + rest
    cosine = (
        ((2.443315711809948e-5 * square - 1.388731625493765e-3) * square + 4.166664568298827e-2) * square * square
        - 0.5 * square
        + 1.0
    )
    quadrant = turns - 4.0 * jnp.floor(turns * 0.25)
    odd = (quadrant == 1.0) | (quadrant == 3.0)
    sine, cosine = jnp.where(odd, cosine, sine), jnp.where(odd, sine, cosine)
    sine = jnp.where(quadrant >= 2.0, -sine, sine)
    cosine = jnp.where((quadrant == 1.0) | (quadrant == 2.0), -cosine, cosine)
    return sine, cosine


class EncGather:
    def __init__(self, place, half, sems, shared):
        self.place, self.half, self.shared = place, half, shared
        self.near_send, self.near_recv, self.far_send, self.far_recv, self.give_send, self.give_recv = sems

    def near(self, side, index, h):
        place = self.place
        slot = self.half(place.ys[index], place.core, h)
        return remote(slot, slot, place.y_side[side], self.near_send.at[side, h], self.near_recv.at[side, h])

    def far(self, side, index):
        place = self.place
        slot = self.half(place.ys[index], place.core, side)
        return remote(slot, slot, place.y_side[side], self.far_send.at[side], self.far_recv.at[side])

    def give(self, index, h, mine=True):
        place = self.place
        slot = self.half(place.ys[index], place.core if mine else 1 - place.core, h)
        return remote(slot, slot, place.sibling, self.give_send.at[index, h], self.give_recv.at[index, h])

    def take(self, index):
        for h in range(2):
            self.give(index, h, mine=False).wait_recv()

    def start(self, h):
        for side in range(2):
            self.near(side, 0, h).start()
        self.share(0, h)

    def share(self, index, h):
        if self.shared:
            self.give(index, h).start()

    def relay(self):
        for side in range(2):
            self.near(side, 1 + side, side).wait_recv()
            self.far(side, 1 + side).start()
            self.share(1 + side, side)

    def finish_near(self):
        for side in range(2):
            self.near(side, 1 + side, 1 - side).wait_recv()
            self.share(1 + side, 1 - side)

    def finish_far(self):
        for side in range(2):
            self.far(side, 3).wait_recv()
            self.share(3, side)

    def drain(self):
        for side in range(2):
            for h in range(2):
                self.near(side, 0, h).wait_send()
            self.far(side, 1 + side).wait_send()
        for index in range(4 if self.shared else 0):
            for h in range(2):
                self.give(index, h).wait_send()


class Place:
    def __init__(self, ny, nz, nx):
        e = lax.axis_index("enc")
        s = lax.axis_index("seq")
        self.e, self.s = e, s
        self.core, self.y = lax.rem(e, 2), lax.div(e, 2)
        self.z, self.x = lax.div(s, nx), lax.rem(s, nx)
        up, down = wrap(self.y + 1, ny), wrap(self.y - 1, ny)
        self.ys = (self.y, down, up, wrap(self.y + 2, ny))
        self.y_side = ((up * 2 + self.core, s), (down * 2 + self.core, s))
        self.sibling = (e + 1 - 2 * self.core, s)
        self.x_side = tuple((e, self.z * nx + wrap(self.x + d, nx)) for d in (1, -1))
        self.z_side = tuple((e, wrap(self.z + d, nz) * nx + self.x) for d in (1, -1))
        self.cols = (self.x, wrap(self.x - 1, nx), wrap(self.x + 1, nx), wrap(self.x + 2, nx))


class PlaneAttention:
    def __init__(self, place, kv, q3, mx, den, acc, sems, nz, nx):
        self.place, self.kv, self.q3, self.mx, self.den, self.acc, self.nz, self.nx = place, kv, q3, mx, den, acc, nz, nx
        self.xs, self.xr, self.hs, self.hr, self.zs, self.zr, self.ss, self.sr = sems
        self.far = nz // 2
        self.half = kv.shape[3]
        self.rows = 2 * self.half
        self.heads = q3.shape[0]
        self.together = min(2, self.heads)
        self.group = self.together * self.rows

    def along_x(self, j, side, i):
        place = self.place
        slot = self.kv.at[self.row_at(j), place.core, place.cols[i]]
        return remote(slot, slot, place.x_side[side], self.xs.at[j, side], self.xr.at[j, side])

    def half_on(self, j, side, i):
        place = self.place
        part = pl.ds(side * (self.half // 2), self.half // 2)
        slot = self.kv.at[self.row_at(j), place.core, place.cols[i], part]
        return remote(slot, slot, place.x_side[side], self.hs.at[j, side], self.hr.at[j, side])

    def along_z(self, j, side, i, k):
        place = self.place
        slot = self.kv.at[self.row_at(j), place.core, place.cols[i]]
        at = 4 * (k - 1) + i
        return remote(slot, slot, place.z_side[side], self.zs.at[side, at], self.zr.at[side, at])

    def half_along_z(self, j, side):
        place = self.place
        slot = self.kv.at[self.row_at(j), place.core, place.x, pl.ds(side * (self.half // 2), self.half // 2)]
        at = 4 * (self.far - 1)
        return remote(slot, slot, place.z_side[side], self.zs.at[side, at], self.zr.at[side, at])

    def give(self, j, mine=True):
        place = self.place
        slot = self.kv.at[self.row_at(j), place.core if mine else 1 - place.core]
        return remote(slot, slot, place.sibling, self.ss.at[j], self.sr.at[j])

    def row_at(self, j):
        k = (j + 1) // 2
        return wrap(self.place.z - k, self.nz) if j % 2 == 1 else wrap(self.place.z + k, self.nz)

    def ring_rows(self, k):
        far = self.far
        return [] if not 0 <= k <= far else [0] if k == 0 else [2 * k - 1] if k == far else [2 * k - 1, 2 * k]

    def comes(self, side, k):
        z = self.place.z
        return z >= k if side == 0 else wrap(z + k, self.nz) < self.far

    def goes(self, side, k):
        z = self.place.z
        if side == 0:
            return (z >= k - 1) & (z <= self.nz - 2)
        return wrap(z + k - 1, self.nz) < self.far

    def needed(self, j):
        k = (j + 1) // 2
        z = self.place.z
        return z >= k if j % 2 == 1 else z + k >= self.nz if j else z >= 0

    def start(self):
        for side in range(2):
            self.along_x(0, side, 0).start()

            @pl.when(self.goes(side, 1))
            def _(side=side):
                self.along_z(0, side, 0, 1).start()

    def compute(self, row, c, restrict=None):
        block = self.kv[row, c]
        high = jnp.concatenate([block[i, :, :HD] for i in range(self.nx)], axis=1)
        low = jnp.concatenate([block[i, :, HD : 2 * HD] for i in range(self.nx)], axis=1)
        v = block[:, :, 2 * HD :].reshape(self.nx * self.half, HD)
        stacked = jnp.concatenate([high, low, high], axis=0)
        queries = [
            self.q3[h : h + self.together].reshape(self.group, 3 * HD) for h in range(0, self.heads, self.together)
        ]
        scores = [jnp.dot(query, stacked, preferred_element_type=jnp.float32) for query in queries]
        for i, score in enumerate(scores):
            at = slice(i * self.group, (i + 1) * self.group)
            if restrict is not None:
                score = jnp.concatenate([restrict(n, score[:, n * HD : (n + 1) * HD]) for n in range(self.nx)], axis=1)
            new = jnp.maximum(self.mx[at], jnp.max(score, axis=1, keepdims=True))
            weights = jnp.exp2(score - jnp.concatenate([new] * self.nx, axis=1))
            summed = weights[:, :HD]
            for n in range(1, self.nx):
                summed = summed + weights[:, n * HD : (n + 1) * HD]
            product = jnp.dot(weights.astype(jnp.bfloat16), v, preferred_element_type=jnp.float32)
            factor = jnp.exp2(self.mx[at] - new)
            self.den[at] = self.den[at] * factor + summed
            self.acc[at] = self.acc[at] * factor + product
            self.mx[at] = new

    def own_row(self, c):
        x = self.place.x
        shape = (self.group, HD)
        token = lax.broadcasted_iota(jnp.int32, shape, 0) & (self.rows - 1)
        ahead = lax.broadcasted_iota(jnp.int32, shape, 1) - token

        def restrict(i, piece):
            limit = jnp.where(x > i, 2 * self.rows, jnp.where(x == i, 0, -2 * self.rows)) - c * self.half
            return jnp.where(ahead <= limit, piece, NEG)

        self.compute(self.place.z, c, restrict)

    def pass_rows(self, k, chosen):
        if not 1 <= k < self.far:
            return
        for side in range(2):
            j = 2 * k - 1 + side

            @pl.when(self.comes(side, k))
            def _(side=side, j=j):
                for i in chosen:
                    self.along_z(j, side, i, k).wait_recv()

            if k + 1 < self.far:
                @pl.when(self.goes(side, k + 1))
                def _(side=side, j=j):
                    for i in chosen:
                        self.along_z(j, side, i, k + 1).start()

    def spreads(self, j):
        everyone = j in (0, 2 * self.far - 1)
        return self.needed(j) if everyone else self.needed(j) & (self.place.core == 1)

    def early(self, t):
        far = self.far
        if 1 <= t <= far:
            for side in range(2):
                j = min(2 * t - 1 + side, 2 * far - 1)

                @pl.when(self.comes(side, t))
                def _(side=side, j=j):
                    if t < far:
                        self.along_z(j, side, 0, t).wait_recv()
                    else:
                        self.half_along_z(j, side).wait_recv()

                if t < far:
                    @pl.when(self.goes(side, t + 1))
                    def _(side=side, j=j):
                        if t + 1 < far:
                            self.along_z(j, side, 0, t + 1).start()
                        else:
                            self.half_along_z(j, side).start()
            for j in self.ring_rows(t):
                @pl.when(self.spreads(j))
                def _(j=j):
                    for side in range(2):
                        self.along_x(j, side, 0).start()
        for j in self.ring_rows(t - 1):
            @pl.when(self.spreads(j))
            def _(j=j):
                for side in range(2):
                    self.along_x(j, side, 1 + side).wait_recv()
                    self.half_on(j, side, 1 + side).start()

        @pl.when(self.place.core == 0)
        def _():
            if t == 1:
                for direction in range(2):
                    @pl.when(self.goes(direction, 1))
                    def _(direction=direction):
                        for i in (1, 2):
                            self.along_z(0, direction, i, 1).start()
            self.pass_rows(t - 2, (1,))

    def from_sibling(self, k):
        for j in self.ring_rows(k):
            @pl.when(self.needed(j))
            def _(j=j):
                self.give(j, mine=False).wait_recv()

    def late(self, t):
        for j in self.ring_rows(t - 2):
            @pl.when(self.spreads(j))
            def _(j=j):
                for side in range(2):
                    self.half_on(j, side, 3).wait_recv()

        @pl.when(self.place.core == 0)
        def _():
            if t == 2:
                for direction in range(2):
                    @pl.when(self.goes(direction, 1))
                    def _(direction=direction):
                        self.along_z(0, direction, 3, 1).start()
            self.pass_rows(t - 2, (2, 3))

        for j in self.ring_rows(t - 2):
            @pl.when(self.needed(j))
            def _(j=j):
                self.give(j).start()

    def run(self, queries_here):
        core, far, z, nz = self.place.core, self.far, self.place.z, self.nz
        self.mx[...] = jnp.full(self.mx.shape, NEG, jnp.float32)
        self.den[...] = jnp.zeros(self.den.shape, jnp.float32)
        self.acc[...] = jnp.zeros(self.acc.shape, jnp.float32)

        def phase(i, carry):
            for t in range(1, far + 4):
                @pl.when(i == 2 * t - 2)
                def _(t=t):
                    self.early(t)
                    if t > 3:
                        self.from_sibling(t - 3)

                @pl.when(i == 2 * t - 1)
                def _(t=t):
                    self.late(t)
                    if t == 1:
                        queries_here()
                    if t == 3:
                        self.from_sibling(0)

            @pl.when((i == 3) | (i == 5))
            def _():
                self.own_row(jnp.where(i == 3, core, 1 - core))

            odd = lax.rem(i, 2)
            k = lax.div(i, 2) - 2 + odd
            c = jnp.where(odd == 1, core, 1 - core)

            def attend(n, inner):
                row = wrap(z + k * (2 * n - 1), nz)

                @pl.when((k >= 1) & (k <= far) & (row < z) & ((k < far) | (n == 0)))
                def _():
                    self.compute(row, c)

                return inner

            lax.fori_loop(0, 2, attend, 0)
            return carry

        lax.fori_loop(0, 2 * (far + 3), phase, 0)

    def result(self, h):
        at = slice(h * self.rows, (h + 1) * self.rows)
        return self.acc[at] / jnp.sum(self.den[at], axis=1, keepdims=True)

    def drain(self):
        far = self.far
        for j in range(2 * far):
            @pl.when(self.needed(j))
            def _(j=j):
                self.give(j).wait_send()

            @pl.when(self.spreads(j))
            def _(j=j):
                for side in range(2):
                    self.along_x(j, side, 0).wait_send()
                    self.half_on(j, side, 1 + side).wait_send()

        for side in range(2):
            for k in range(1, far + 1):
                @pl.when(self.goes(side, k))
                def _(side=side, k=k):
                    j = 0 if k == 1 else 2 * k - 3 + side
                    if k == far:
                        self.half_along_z(j, side).wait_send()
                    else:
                        self.along_z(j, side, 0, k).wait_send()

                        @pl.when(self.place.core == 0)
                        def _():
                            for i in range(1, 4):
                                self.along_z(j, side, i, k).wait_send()


def prefill(
    patches, gain, up_t, up_bias, merge_down, down_bias, text, lengths, offsets, input_gain, qkv_weight, qkv_bias, freq,
    ny, nz, nx,
):
    patch_rows, vision = patches.shape
    units, joined = up_t.shape
    part = patch_rows // 4
    pad = -(-part // 16) * 16
    cut = -(-patch_rows // 32) * 16
    blocks = 2 * ny
    wide = 2 * text.shape[1]
    groups = nz * nx
    slots = groups * LMAX
    rows, width = text.shape
    half = rows // 2
    model = merge_down.shape[1]
    query_width = qkv_weight.shape[1] - HD
    heads = query_width // HD
    far = nz // 2

    def kernel(
        p_ref, g_ref, up_hbm, ub_ref, down_hbm, db_ref, text_ref, len_s, off_s, len_v, off_v, gain_ref, qkv_hbm, qb_ref,
        freq_ref, o_ref,
        buf, order, ordered, turned, up, hid, out, inn, down, w_q, w_kv, qkv_bias_of, down_bias_of, text_of, placed_out, placed_in, placed_mine,
        merged_sum, turn_cos, turn_sin, gain_row, own, rel_out, rel_in, d_out, d_in, full, squares, normed, kv, q3, mx, den, acc,
        w_sem, c_send, c_recv, a_send, a_recv, r_send, r_recv, d_send, d_recv,
        fns, fnr, ffs, ffr, fgs, fgr, bns, bnr, bfs, bfr,
        xs, xr, hs, hr, zs, zr, ss, sr,
    ):
        place = Place(ny, nz, nx)
        e, s, core, z, x = place.e, place.s, place.core, place.z, place.x
        other = 1 - core

        query_at, rest_at = pl.ds(0, query_width), pl.ds(query_width, HD)

        def lanes(c, size):
            return pl.ds(pl.multiple_of(c * size, size), size)

        def tokens(c):
            return pl.ds(pl.multiple_of(c * half, half), half)

        loads = (
            pltpu.make_async_copy(up_hbm, turned, w_sem.at[0]),
            pltpu.make_async_copy(down_hbm, down.at[core], w_sem.at[1]),
            pltpu.make_async_copy(qkv_hbm.at[:, rest_at], w_kv.at[:, lanes(core, HD)], w_sem.at[2]),
            pltpu.make_async_copy(qkv_hbm.at[:, query_at], w_q, w_sem.at[3]),
        )
        for load in loads:
            load.start()

        def to_sibling(i, src, dst):
            return remote(src, dst, place.sibling, c_send.at[i], c_recv.at[i])

        def gift(i, c):
            return (
                lambda: to_sibling(0, qkv_bias_of.at[core], qkv_bias_of.at[c]),
                lambda: to_sibling(1, down_bias_of.at[core], down_bias_of.at[c]),
                lambda: to_sibling(2, text_ref.at[tokens(other)], text_of.at[:, lanes(c, width)]),
                lambda: to_sibling(3, qkv_hbm.at[:, rest_at], w_kv.at[:, lanes(c, HD)]),
                lambda: to_sibling(4, down_hbm, down.at[c]),
                lambda: to_sibling(5, normed.at[core], normed.at[c]),
                lambda: to_sibling(6, placed_out, placed_in),
            )[i]()

        barrier = pltpu.get_barrier_semaphore()

        def greet(p, carry):
            pl.semaphore_signal(barrier, inc=1, device_id=(e, wrap(s + p, groups)), device_id_type=MESH)
            return carry

        lax.fori_loop(1, groups, greet, 0)
        for to in (*place.y_side, place.sibling):
            pl.semaphore_signal(barrier, inc=1, device_id=to, device_id_type=MESH)

        front = EncGather(
            place, lambda y, c, h: buf.at[y, c, pl.ds(h * cut, patch_rows - cut if h else cut)], (fns, fnr, ffs, ffr, fgs, fgr), shared=True
        )
        values = p_ref[...].astype(jnp.float32)
        mean_square = jnp.mean(values * values, axis=1, keepdims=True)
        buf[place.y, core] = (
            values * lax.rsqrt(mean_square + EPSILON) * g_ref[...].reshape(1, vision)
        ).astype(jnp.bfloat16)
        pl.semaphore_wait(barrier, groups - 1 + 3)
        front.start(0)
        front.start(1)
        qkv_bias_of[core] = qb_ref[...].reshape(1, query_width + HD)
        down_bias_of[core] = db_ref[...].reshape(1, width)
        for i in range(5):
            gift(i, core).start()
        text_of[:, lanes(core, width)] = text_ref[tokens(core)]

        loads[0].wait()
        def turn(i, carry):
            at = pl.ds(pl.multiple_of(i * 512, 512), 512)
            up[at, :] = turned[:, at].T
            return carry

        turns = joined // 512
        lax.fori_loop(0, turns // 2, turn, 0)
        front.relay()
        lax.fori_loop(turns // 2, turns, turn, 0)
        front.finish_near()

        to = lax.broadcasted_iota(jnp.int32, (4 * pad, patch_rows), 0)
        source = lax.broadcasted_iota(jnp.int32, (4 * pad, patch_rows), 1)
        moved = (source == 4 * (to % pad) + to // pad) & (to % pad < part)
        order[...] = jnp.where(moved, 1.0, 0.0).astype(jnp.bfloat16)

        lane = lax.broadcasted_iota(jnp.int32, (1, blocks * pad), 1)
        merged = jnp.where(lane % pad < part, lane // pad * part + lane % pad, -1)
        code = jnp.full((1, blocks * pad), -1, jnp.int32)
        begin = jnp.int32(0)
        for j in range(len_s.shape[0]):
            end = begin + len_s[j, s]
            inside = (merged >= begin) & (merged < end)
            code = jnp.where(inside, off_s[j, s] // rows * LMAX + merged - begin, code)
            begin = end
        slot = lax.broadcasted_iota(jnp.int32, (slots, blocks * pad), 0)
        pick = jnp.where(slot == code, 1.0, 0.0).astype(jnp.bfloat16)

        ours = off_v[...] // rows == s
        first = jnp.sum(jnp.where(ours, off_v[...] - s * rows, 0).astype(jnp.float32), axis=0, keepdims=True)
        count = jnp.sum(jnp.where(ours, len_v[...], 0).astype(jnp.float32), axis=0, keepdims=True)
        group = lax.broadcasted_iota(jnp.int32, (groups, slots), 0)
        position = lax.broadcasted_iota(jnp.int32, (groups, slots), 1)
        spread_groups = jnp.where(position // LMAX == group, 1.0, 0.0).astype(jnp.bfloat16)
        both = jnp.concatenate([jnp.broadcast_to(first, (8, groups)), jnp.broadcast_to(count, (8, groups))], axis=0)
        both = jnp.dot(both.astype(jnp.bfloat16), spread_groups, preferred_element_type=jnp.float32)
        index = (lax.broadcasted_iota(jnp.int32, (1, slots), 1) % LMAX).astype(jnp.float32)
        target = jnp.where(index < both[8:9], both[:1] + index, -1.0)
        token = lax.broadcasted_iota(jnp.int32, (half, slots), 0)

        def placing(c):
            return jnp.where((token + c * half).astype(jnp.float32) == target, 1.0, 0.0)

        covered = jnp.sum(placing(core), axis=1, keepdims=True) > 0.5

        def merge(*chips):
            count = len(chips) * 2 * pad

            def sort(c, carry):
                for i, y in enumerate(chips):
                    rows_of = jnp.dot(order[...], buf[y, c], preferred_element_type=jnp.float32)
                    ordered[:, i, c] = rows_of.astype(jnp.bfloat16).reshape(4, pad, vision)
                return carry

            lax.fori_loop(0, 2, sort, 0)
            merged_sum[:count] = jnp.broadcast_to(ub_ref[...].reshape(1, units), (count, units))

            def add_part(q, carry):
                grouped = ordered[q, : len(chips)].reshape(count, vision)
                weights = up[pl.ds(pl.multiple_of(q * vision, vision), vision), :]
                merged_sum[:count] += jnp.dot(grouped, weights, preferred_element_type=jnp.float32)
                return carry

            lax.fori_loop(0, 4, add_part, 0)
            inner = merged_sum[:count]
            inner = (0.5 * inner * (1.0 + lax.erf(inner * math.sqrt(0.5)))).astype(jnp.bfloat16)
            for i, y in enumerate(chips):
                hid[y] = inner[i * 2 * pad : (i + 1) * 2 * pad]

        front.take(0)
        merge(place.ys[0])
        front.take(1)
        front.take(2)
        merge(place.ys[1], place.ys[2])
        front.finish_far()
        front.take(3)
        merge(place.ys[3])

        chosen = jnp.dot(pick, hid[...].reshape(blocks * pad, units), preferred_element_type=jnp.float32)
        out[...] = chosen.astype(jnp.bfloat16).reshape(groups, LMAX, units)

        def swap(p, at, arrives):
            return remote(out.at[at], inn.at[arrives], (e, at), a_send.at[p], a_recv.at[p])

        def begin_swap(p, carry):
            swap(p, wrap(s + p, groups), s).start()
            return carry

        lax.fori_loop(1, groups, begin_swap, 0)
        inn[s] = out[s]
        def end_swap(p, carry):
            swap(p, wrap(s + p, groups), wrap(s - p + groups, groups)).wait_recv()
            return carry

        lax.fori_loop(1, groups, end_swap, 0)
        arrived = inn[...].reshape(slots, units)

        def place_tokens(c):
            return jnp.dot(
                placing(c).astype(jnp.bfloat16), arrived, preferred_element_type=jnp.float32
            ).astype(jnp.bfloat16)

        placed_out[...] = place_tokens(other)
        gift(6, core).start()
        placed_mine[...] = place_tokens(core)

        def share(hidden_rows, c, y_to):
            return jnp.dot(hidden_rows, down[c, :, lanes(y_to, wide)], preferred_element_type=jnp.float32)

        def relay(side):
            return remote(rel_out.at[side], rel_in.at[side], place.y_side[side], r_send.at[side], r_recv.at[side])

        def deliver(side, h):
            return remote(
                d_out.at[side, h], d_in.at[side, h], place.y_side[side], d_send.at[side, h], d_recv.at[side, h]
            )

        halves = (slice(0, half // 2), slice(half // 2, half))
        loads[1].wait()
        def target(i):
            return wrap(place.y + jnp.where(i == 0, 2, jnp.where(i == 1, 1, jnp.where(i == 2, -1, 0))), ny)

        def add_own(i, carry):
            own[i] = share(placed_mine[...], core, target(i))
            return carry

        def add_other(i, carry):
            own[i] += share(placed_in[...], other, target(i))
            return carry

        lax.fori_loop(0, 4, add_own, 0)
        gift(4, other).wait_recv()
        gift(6, other).wait_recv()
        for i in range(3):
            lax.fori_loop(i, i + 1 if i < 2 else 4, add_other, 0)
            for side in range(2):
                if i == 0:
                    rel_out[side] = own[0, halves[side]].astype(jnp.bfloat16)
                    relay(side).start()
                if i == 1 + side:
                    d_out[side, 1 - side] = own[i, halves[1 - side]].astype(jnp.bfloat16)
                    deliver(side, 1 - side).start()
        gift(1, other).wait_recv()
        gift(2, other).wait_recv()
        own[3] = own[3] + jnp.concatenate([down_bias_of[0], down_bias_of[1]], axis=1)
        for side in range(2):
            relay(side).wait_recv()
            d_out[side, side] = (own[1 + side, halves[side]] + rel_in[side].astype(jnp.float32)).astype(jnp.bfloat16)
            deliver(side, side).start()

        for c in range(2):
            token_id = lax.broadcasted_iota(jnp.int32, (half, HD), 0) + s * rows + c * half
            sine, cosine = sine_cosine(token_id.astype(jnp.float32) * freq_ref[...])
            turn_cos[c] = cosine
            turn_sin[c] = jnp.where(lax.broadcasted_iota(jnp.int32, (half, HD), 1) < HD // 2, -sine, sine)

        def rotate(block, c):
            return block * turn_cos[c] + pltpu.roll(block, HD // 2, 1) * turn_sin[c]

        back = EncGather(
            place, lambda y, c, h: full.at[y, pl.ds(h * (half // 2), half // 2)], (bns, bnr, bfs, bfr, None, None), shared=False
        )
        for h in range(2):
            at = halves[h]
            total = own[3, at]
            for side in range(2):
                deliver(side, h).wait_recv()
                total = total + d_in[side, h].astype(jnp.float32)
            kept = jnp.where(covered[at], total, text_of[at].astype(jnp.float32))
            full[place.y, at] = kept.astype(jnp.bfloat16)
            back.start(h)
        squares[...] = jnp.zeros(squares.shape, jnp.float32)

        def add_squares(y):
            block = full[y].astype(jnp.float32)
            block = block * block
            summed = block[:, :HD]
            for g in range(1, wide // HD):
                summed = summed + block[:, g * HD : (g + 1) * HD]
            squares[...] += summed

        add_squares(place.ys[0])
        back.relay()
        back.finish_near()
        for i in range(1, 3):
            add_squares(place.ys[i])
        back.finish_far()
        add_squares(place.ys[3])

        scale = lax.rsqrt(jnp.sum(squares[...], axis=1, keepdims=True) * (1.0 / model) + EPSILON)
        gain_row[...] = gain_ref[...].reshape(1, model)

        def norm_part(y, carry):
            at = lanes(y, wide)
            normed[core, :, at] = (full[y].astype(jnp.float32) * scale * gain_row[:, at]).astype(jnp.bfloat16)
            return carry

        lax.fori_loop(0, ny, norm_part, 0)
        gift(5, core).start()
        loads[2].wait()
        gift(0, other).wait_recv()
        gift(3, other).wait_recv()
        both = jnp.dot(normed[core], w_kv[...], preferred_element_type=jnp.float32)
        key = rotate(both[:, :HD] + qkv_bias_of[0, :, query_width:], core).T
        key_high = key.astype(jnp.bfloat16)
        kv[z, core, x, :, :HD] = key_high
        kv[z, core, x, :, HD : 2 * HD] = (key - key_high.astype(jnp.float32)).astype(jnp.bfloat16)
        kv[z, core, x, :, 2 * HD :] = (both[:, HD:] + qkv_bias_of[1, :, query_width:]).astype(jnp.bfloat16)

        plane = PlaneAttention(place, kv, q3, mx, den, acc, (xs, xr, hs, hr, zs, zr, ss, sr), nz, nx)
        plane.start()

        scaling = HD ** (-0.5) * math.log2(math.e)
        loads[3].wait()

        def project(i, carry):
            pairs = heads // 2
            c = jnp.where(i < pairs, core, other)
            first_head = 2 * lax.rem(i, pairs)

            at = pl.ds(pl.multiple_of(first_head * HD, 2 * HD), 2 * HD)
            query = jnp.dot(normed[c], w_q[:, at], preferred_element_type=jnp.float32) + qkv_bias_of[core, :, at]
            for n in range(2):
                head = rotate(query[:, n * HD : (n + 1) * HD], c) * scaling
                high = head.astype(jnp.bfloat16)
                low = (head - high.astype(jnp.float32)).astype(jnp.bfloat16)
                q3[first_head + n, c, :, :HD] = high
                q3[first_head + n, c, :, HD : 2 * HD] = high
                q3[first_head + n, c, :, 2 * HD :] = low
            return carry

        def sibling_tokens():
            gift(5, other).wait_recv()
            lax.fori_loop(heads // 2, heads, project, 0)

        lax.fori_loop(0, heads // 2, project, 0)
        plane.run(sibling_tokens)
        for h in range(heads):
            o_ref[:, h * HD : (h + 1) * HD] = plane.result(h).astype(o_ref.dtype)

        def sent_swap(p, carry):
            swap(p, wrap(s + p, groups), s).wait_send()
            return carry

        lax.fori_loop(1, groups, sent_swap, 0)
        front.drain()
        back.drain()
        for i in range(7):
            gift(i, core).wait_send()
        for side in range(2):
            relay(side).wait_send()
            for h in range(2):
                deliver(side, h).wait_send()
        plane.drain()

    dma = pltpu.SemaphoreType.DMA
    bf16, f32 = jnp.bfloat16, jnp.float32
    vmem = pl.BlockSpec(memory_space=pltpu.VMEM)
    smem = pl.BlockSpec(memory_space=pltpu.SMEM)
    any_space = pl.BlockSpec(memory_space=pl.ANY)
    enc_sems = [dma((2, 2)), dma((2, 2)), dma((2,)), dma((2,)), dma((4, 2)), dma((4, 2))]
    return pl.pallas_call(
        kernel,
        out_shape=jax.ShapeDtypeStruct((rows, query_width), bf16),
        in_specs=[
            vmem, vmem, any_space, vmem, any_space, vmem, vmem, smem, smem, vmem, vmem, vmem, any_space, vmem, vmem,
        ],
        out_specs=vmem,
        scratch_shapes=[
            pltpu.VMEM((ny, 2, patch_rows, vision), bf16),
            pltpu.VMEM((4 * pad, patch_rows), bf16),
            pltpu.VMEM((4, 2, 2, pad, vision), bf16),
            pltpu.VMEM((units, joined), bf16),
            pltpu.VMEM((joined, units), bf16),
            pltpu.VMEM((ny, 2 * pad, units), bf16),
            pltpu.VMEM((groups, LMAX, units), bf16),
            pltpu.VMEM((groups, LMAX, units), bf16),
            pltpu.VMEM((2, *merge_down.shape), bf16),
            pltpu.VMEM((model, query_width), bf16),
            pltpu.VMEM((model, 2 * HD), bf16),
            pltpu.VMEM((2, 1, query_width + HD), f32),
            pltpu.VMEM((2, 1, width), f32),
            pltpu.VMEM((half, wide), bf16),
            pltpu.VMEM((half, units), bf16),
            pltpu.VMEM((half, units), bf16),
            pltpu.VMEM((half, units), bf16),
            pltpu.VMEM((4 * pad, units), f32),
            pltpu.VMEM((2, half, HD), f32),
            pltpu.VMEM((2, half, HD), f32),
            pltpu.VMEM((1, model), f32),
            pltpu.VMEM((4, half, wide), f32),
            pltpu.VMEM((2, half // 2, wide), bf16),
            pltpu.VMEM((2, half // 2, wide), bf16),
            pltpu.VMEM((2, 2, half // 2, wide), bf16),
            pltpu.VMEM((2, 2, half // 2, wide), bf16),
            pltpu.VMEM((ny, half, wide), bf16),
            pltpu.VMEM((half, HD), f32),
            pltpu.VMEM((2, half, model), bf16),
            pltpu.VMEM((nz, 2, nx, half, 3 * HD), bf16),
            pltpu.VMEM((heads, 2, half, 3 * HD), bf16),
            pltpu.VMEM((heads * rows, HD), f32),
            pltpu.VMEM((heads * rows, HD), f32),
            pltpu.VMEM((heads * rows, HD), f32),
            dma((4,)),
            dma((7,)),
            dma((7,)),
            dma((groups,)),
            dma((groups,)),
            dma((2,)),
            dma((2,)),
            dma((2, 2)),
            dma((2, 2)),
            *enc_sems,
            *enc_sems[:4],
            dma((nz, 2)),
            dma((nz, 2)),
            dma((nz, 2)),
            dma((nz, 2)),
            dma((2, 4 * far)),
            dma((2, 4 * far)),
            dma((nz,)),
            dma((nz,)),
        ],
        compiler_params=pltpu.CompilerParams(
            collective_id=1, has_side_effects=True, vmem_limit_bytes=56 * 1024 * 1024
        ),
        name="prefill",
    )(
        patches, gain, up_t, up_bias, merge_down, down_bias, text, lengths, offsets, lengths, offsets, input_gain,
        qkv_weight, qkv_bias, freq,
    )


def local(
    patches, vision_gain, merge_up, merge_up_bias, merge_down, merge_down_bias, text_embed, image_lengths, image_offsets,
    input_gain, qkv_weight, qkv_bias,
):
    freq = np.exp(np.arange(HD // 2) * (-2.0 * np.log(THETA) / HD)).astype(np.float32)
    return prefill(
        patches[0], vision_gain, merge_up.T, merge_up_bias, merge_down, merge_down_bias, text_embed,
        image_lengths.T, image_offsets.T, input_gain, qkv_weight, qkv_bias,
        jnp.asarray(np.concatenate([freq, freq])[None]),
        lax.axis_size("enc") // 2, lax.axis_size("seq") // NX, NX,
    )


def solution(mesh):
    in_specs = (
        P("seq", "enc", None),
        P(),
        P(None, "enc"),
        P("enc"),
        P("enc", None),
        P("enc"),
        P("seq", "enc"),
        P(),
        P(),
        P(),
        P(None, "enc"),
        P("enc"),
    )
    out_specs = P("seq", "enc")
    return jax.shard_map(local, mesh=mesh, in_specs=in_specs, out_specs=out_specs, check_vma=False)
```

```python
import math

import jax
import jax.numpy as jnp
import numpy as np
from jax import lax
from jax.experimental import pallas as pl
from jax.experimental.pallas import tpu as pltpu
from jax.sharding import PartitionSpec as P

HD = 128
LMAX = 16
NX = 4
EPSILON = 1e-06
THETA = 1000000.0
NEG = -1e30
MESH = pl.DeviceIdType.MESH


def wrap(value, size):
    return lax.rem(value + 2 * size, size)


def remote(src, dst, to, send_sem, recv_sem):
    return pltpu.make_async_remote_copy(
        src_ref=src, dst_ref=dst, send_sem=send_sem, recv_sem=recv_sem, device_id=to, device_id_type=MESH
    )


def sine_cosine(angle):
    turns = jnp.floor(angle * (2.0 / math.pi) + 0.5)
    rest = ((angle - turns * 1.5703125) - turns * 4.837512969970703125e-4) - turns * 7.54978995489188216e-8
    square = rest * rest
    sine = ((-1.9515295891e-4 * square + 8.3321608736e-3) * square - 1.6666654611e-1) * square * rest + rest
    cosine = (
        ((2.443315711809948e-5 * square - 1.388731625493765e-3) * square + 4.166664568298827e-2) * square * square
        - 0.5 * square
        + 1.0
    )
    quadrant = turns - 4.0 * jnp.floor(turns * 0.25)
    odd = (quadrant == 1.0) | (quadrant == 3.0)
    sine, cosine = jnp.where(odd, cosine, sine), jnp.where(odd, sine, cosine)
    sine = jnp.where(quadrant >= 2.0, -sine, sine)
    cosine = jnp.where((quadrant == 1.0) | (quadrant == 2.0), -cosine, cosine)
    return sine, cosine


class EncGather:
    def __init__(self, place, half, sems, shared):
        self.place, self.half, self.shared = place, half, shared
        self.near_send, self.near_recv, self.far_send, self.far_recv, self.give_send, self.give_recv = sems

    def near(self, side, index, h):
        place = self.place
        slot = self.half(place.ys[index], place.core, h)
        return remote(slot, slot, place.y_side[side], self.near_send.at[side, h], self.near_recv.at[side, h])

    def far(self, side, index):
        place = self.place
        slot = self.half(place.ys[index], place.core, side)
        return remote(slot, slot, place.y_side[side], self.far_send.at[side], self.far_recv.at[side])

    def give(self, index, h, mine=True):
        place = self.place
        slot = self.half(place.ys[index], place.core if mine else 1 - place.core, h)
        return remote(slot, slot, place.sibling, self.give_send.at[index, h], self.give_recv.at[index, h])

    def take(self, index):
        for h in range(2):
            self.give(index, h, mine=False).wait_recv()

    def start(self, h):
        for side in range(2):
            self.near(side, 0, h).start()
        self.share(0, h)

    def share(self, index, h):
        if self.shared:
            self.give(index, h).start()

    def relay(self):
        for side in range(2):
            self.near(side, 1 + side, side).wait_recv()
            self.far(side, 1 + side).start()
            self.share(1 + side, side)

    def finish_near(self):
        for side in range(2):
            self.near(side, 1 + side, 1 - side).wait_recv()
            self.share(1 + side, 1 - side)

    def finish_far(self):
        for side in range(2):
            self.far(side, 3).wait_recv()
            self.share(3, side)

    def drain(self):
        for side in range(2):
            for h in range(2):
                self.near(side, 0, h).wait_send()
            self.far(side, 1 + side).wait_send()
        for index in range(4 if self.shared else 0):
            for h in range(2):
                self.give(index, h).wait_send()


class Place:
    def __init__(self, ny, nz, nx):
        e = lax.axis_index("enc")
        s = lax.axis_index("seq")
        self.e, self.s = e, s
        self.core, self.y = lax.rem(e, 2), lax.div(e, 2)
        self.z, self.x = lax.div(s, nx), lax.rem(s, nx)
        up, down = wrap(self.y + 1, ny), wrap(self.y - 1, ny)
        self.ys = (self.y, down, up, wrap(self.y + 2, ny))
        self.y_side = ((up * 2 + self.core, s), (down * 2 + self.core, s))
        self.sibling = (e + 1 - 2 * self.core, s)
        self.x_side = tuple((e, self.z * nx + wrap(self.x + d, nx)) for d in (1, -1))
        self.z_side = tuple((e, wrap(self.z + d, nz) * nx + self.x) for d in (1, -1))
        self.cols = (self.x, wrap(self.x - 1, nx), wrap(self.x + 1, nx), wrap(self.x + 2, nx))


class PlaneAttention:
    def __init__(self, place, kv, q3, mx, den, acc, sems, nz, nx):
        self.place, self.kv, self.q3, self.mx, self.den, self.acc, self.nz, self.nx = place, kv, q3, mx, den, acc, nz, nx
        self.xs, self.xr, self.hs, self.hr, self.zs, self.zr, self.ss, self.sr = sems
        self.far = nz // 2
        self.half = kv.shape[3]
        self.rows = 2 * self.half
        self.heads = q3.shape[0]
        self.together = 1
        self.group = self.together * self.rows

    def along_x(self, j, side, i):
        place = self.place
        slot = self.kv.at[self.row_at(j), place.core, place.cols[i]]
        return remote(slot, slot, place.x_side[side], self.xs.at[j, side], self.xr.at[j, side])

    def half_on(self, j, side, i):
        place = self.place
        part = pl.ds(side * (self.half // 2), self.half // 2)
        slot = self.kv.at[self.row_at(j), place.core, place.cols[i], part]
        return remote(slot, slot, place.x_side[side], self.hs.at[j, side], self.hr.at[j, side])

    def along_z(self, j, side, i, k):
        place = self.place
        slot = self.kv.at[self.row_at(j), place.core, place.cols[i]]
        at = 4 * (k - 1) + i
        return remote(slot, slot, place.z_side[side], self.zs.at[side, at], self.zr.at[side, at])

    def half_along_z(self, j, side):
        place = self.place
        slot = self.kv.at[self.row_at(j), place.core, place.x, pl.ds(side * (self.half // 2), self.half // 2)]
        at = 4 * (self.far - 1)
        return remote(slot, slot, place.z_side[side], self.zs.at[side, at], self.zr.at[side, at])

    def give(self, j, mine=True):
        place = self.place
        slot = self.kv.at[self.row_at(j), place.core if mine else 1 - place.core]
        return remote(slot, slot, place.sibling, self.ss.at[j], self.sr.at[j])

    def row_at(self, j):
        k = (j + 1) // 2
        return wrap(self.place.z - k, self.nz) if j % 2 == 1 else wrap(self.place.z + k, self.nz)

    def ring_rows(self, k):
        far = self.far
        return [] if not 0 <= k <= far else [0] if k == 0 else [2 * k - 1] if k == far else [2 * k - 1, 2 * k]

    def comes(self, side, k):
        z = self.place.z
        return z >= k if side == 0 else wrap(z + k, self.nz) < self.far

    def goes(self, side, k):
        z = self.place.z
        if side == 0:
            return (z >= k - 1) & (z <= self.nz - 2)
        return wrap(z + k - 1, self.nz) < self.far

    def needed(self, j):
        k = (j + 1) // 2
        z = self.place.z
        return z >= k if j % 2 == 1 else z + k >= self.nz if j else z >= 0

    def start(self):
        for side in range(2):
            self.along_x(0, side, 0).start()

            @pl.when(self.goes(side, 1))
            def _(side=side):
                self.along_z(0, side, 0, 1).start()

    def compute(self, row, c, restrict=None):
        block = self.kv[row, c]
        high = jnp.concatenate([block[i, :, :HD] for i in range(self.nx)], axis=1)
        low = jnp.concatenate([block[i, :, HD : 2 * HD] for i in range(self.nx)], axis=1)
        v = block[:, :, 2 * HD :].reshape(self.nx * self.half, HD)
        stacked = jnp.concatenate([high, low, high], axis=0)
        queries = [
            self.q3[h : h + self.together].reshape(self.group, 3 * HD) for h in range(0, self.heads, self.together)
        ]
        scores = [jnp.dot(query, stacked, preferred_element_type=jnp.float32) for query in queries]
        for i, score in enumerate(scores):
            at = slice(i * self.group, (i + 1) * self.group)
            if restrict is not None:
                score = jnp.concatenate([restrict(n, score[:, n * HD : (n + 1) * HD]) for n in range(self.nx)], axis=1)
            new = jnp.maximum(self.mx[at], jnp.max(score, axis=1, keepdims=True))
            weights = jnp.exp2(score - jnp.concatenate([new] * self.nx, axis=1))
            summed = weights[:, :HD]
            for n in range(1, self.nx):
                summed = summed + weights[:, n * HD : (n + 1) * HD]
            product = jnp.dot(weights.astype(jnp.bfloat16), v, preferred_element_type=jnp.float32)
            factor = jnp.exp2(self.mx[at] - new)
            self.den[at] = self.den[at] * factor + summed
            self.acc[at] = self.acc[at] * factor + product
            self.mx[at] = new

    def own_row(self, c):
        x = self.place.x
        shape = (self.group, HD)
        token = lax.broadcasted_iota(jnp.int32, shape, 0) & (self.rows - 1)
        ahead = lax.broadcasted_iota(jnp.int32, shape, 1) - token

        def restrict(i, piece):
            limit = jnp.where(x > i, 2 * self.rows, jnp.where(x == i, 0, -2 * self.rows)) - c * self.half
            return jnp.where(ahead <= limit, piece, NEG)

        self.compute(self.place.z, c, restrict)

    def pass_rows(self, k, chosen):
        if not 1 <= k < self.far:
            return
        for side in range(2):
            j = 2 * k - 1 + side

            @pl.when(self.comes(side, k))
            def _(side=side, j=j):
                for i in chosen:
                    self.along_z(j, side, i, k).wait_recv()

            if k + 1 < self.far:
                @pl.when(self.goes(side, k + 1))
                def _(side=side, j=j):
                    for i in chosen:
                        self.along_z(j, side, i, k + 1).start()

    def spreads(self, j):
        everyone = j in (0, 2 * self.far - 1)
        return self.needed(j) if everyone else self.needed(j) & (self.place.core == 1)

    def early(self, t):
        far = self.far
        if 1 <= t <= far:
            for side in range(2):
                j = min(2 * t - 1 + side, 2 * far - 1)

                @pl.when(self.comes(side, t))
                def _(side=side, j=j):
                    if t < far:
                        self.along_z(j, side, 0, t).wait_recv()
                    else:
                        self.half_along_z(j, side).wait_recv()

                if t < far:
                    @pl.when(self.goes(side, t + 1))
                    def _(side=side, j=j):
                        if t + 1 < far:
                            self.along_z(j, side, 0, t + 1).start()
                        else:
                            self.half_along_z(j, side).start()
            for j in self.ring_rows(t):
                @pl.when(self.spreads(j))
                def _(j=j):
                    for side in range(2):
                        self.along_x(j, side, 0).start()
        for j in self.ring_rows(t - 1):
            @pl.when(self.spreads(j))
            def _(j=j):
                for side in range(2):
                    self.along_x(j, side, 1 + side).wait_recv()
                    self.half_on(j, side, 1 + side).start()

        @pl.when(self.place.core == 0)
        def _():
            if t == 1:
                for direction in range(2):
                    @pl.when(self.goes(direction, 1))
                    def _(direction=direction):
                        for i in (1, 2):
                            self.along_z(0, direction, i, 1).start()
            self.pass_rows(t - 2, (1,))

    def from_sibling(self, k):
        for j in self.ring_rows(k):
            @pl.when(self.needed(j))
            def _(j=j):
                self.give(j, mine=False).wait_recv()

    def late(self, t):
        for j in self.ring_rows(t - 2):
            @pl.when(self.spreads(j))
            def _(j=j):
                for side in range(2):
                    self.half_on(j, side, 3).wait_recv()

        @pl.when(self.place.core == 0)
        def _():
            if t == 2:
                for direction in range(2):
                    @pl.when(self.goes(direction, 1))
                    def _(direction=direction):
                        self.along_z(0, direction, 3, 1).start()
            self.pass_rows(t - 2, (2, 3))

        for j in self.ring_rows(t - 2):
            @pl.when(self.needed(j))
            def _(j=j):
                self.give(j).start()

    def run(self, queries_here):
        core, far, z, nz = self.place.core, self.far, self.place.z, self.nz
        self.mx[...] = jnp.full(self.mx.shape, NEG, jnp.float32)
        self.den[...] = jnp.zeros(self.den.shape, jnp.float32)
        self.acc[...] = jnp.zeros(self.acc.shape, jnp.float32)

        def phase(i, carry):
            for t in range(1, far + 4):
                @pl.when(i == 2 * t - 2)
                def _(t=t):
                    self.early(t)
                    if t > 3:
                        self.from_sibling(t - 3)

                @pl.when(i == 2 * t - 1)
                def _(t=t):
                    self.late(t)
                    if t == 1:
                        queries_here()
                    if t == 3:
                        self.from_sibling(0)

            @pl.when((i == 3) | (i == 5))
            def _():
                self.own_row(jnp.where(i == 3, core, 1 - core))

            odd = lax.rem(i, 2)
            k = lax.div(i, 2) - 2 + odd
            c = jnp.where(odd == 1, core, 1 - core)

            def attend(n, inner):
                row = wrap(z + k * (2 * n - 1), nz)

                @pl.when((k >= 1) & (k <= far) & (row < z) & ((k < far) | (n == 0)))
                def _():
                    self.compute(row, c)

                return inner

            lax.fori_loop(0, 2, attend, 0)
            return carry

        lax.fori_loop(0, 2 * (far + 3), phase, 0)

    def result(self, h):
        at = slice(h * self.rows, (h + 1) * self.rows)
        return self.acc[at] / jnp.sum(self.den[at], axis=1, keepdims=True)

    def drain(self):
        far = self.far
        for j in range(2 * far):
            @pl.when(self.needed(j))
            def _(j=j):
                self.give(j).wait_send()

            @pl.when(self.spreads(j))
            def _(j=j):
                for side in range(2):
                    self.along_x(j, side, 0).wait_send()
                    self.half_on(j, side, 1 + side).wait_send()

        for side in range(2):
            for k in range(1, far + 1):
                @pl.when(self.goes(side, k))
                def _(side=side, k=k):
                    j = 0 if k == 1 else 2 * k - 3 + side
                    if k == far:
                        self.half_along_z(j, side).wait_send()
                    else:
                        self.along_z(j, side, 0, k).wait_send()

                        @pl.when(self.place.core == 0)
                        def _():
                            for i in range(1, 4):
                                self.along_z(j, side, i, k).wait_send()


def prefill(
    patches, gain, up_t, up_bias, merge_down, down_bias, text, lengths, offsets, input_gain, qkv_weight, qkv_bias, freq,
    ny, nz, nx,
):
    patch_rows, vision = patches.shape
    units, joined = up_t.shape
    part = patch_rows // 4
    pad = -(-part // 16) * 16
    cut = -(-patch_rows // 32) * 16
    blocks = 2 * ny
    wide = 2 * text.shape[1]
    groups = nz * nx
    slots = groups * LMAX
    rows, width = text.shape
    half = rows // 2
    model = merge_down.shape[1]
    query_width = qkv_weight.shape[1] - HD
    heads = query_width // HD
    far = nz // 2

    def kernel(
        p_ref, g_ref, up_hbm, ub_ref, down_hbm, db_ref, text_ref, len_s, off_s, len_v, off_v, gain_ref, qkv_hbm, qb_ref,
        freq_ref, o_ref,
        buf, order, ordered, turned, up, hid, out, inn, down, w_q, w_kv, qkv_bias_of, down_bias_of, text_of, placed_out, placed_in, placed_mine,
        merged_sum, turn_cos, turn_sin, gain_row, own, rel_out, rel_in, d_out, d_in, full, squares, normed, kv, q3, mx, den, acc,
        w_sem, c_send, c_recv, a_send, a_recv, r_send, r_recv, d_send, d_recv,
        fns, fnr, ffs, ffr, fgs, fgr, bns, bnr, bfs, bfr,
        xs, xr, hs, hr, zs, zr, ss, sr,
    ):
        place = Place(ny, nz, nx)
        e, s, core, z, x = place.e, place.s, place.core, place.z, place.x
        other = 1 - core

        query_at, rest_at = pl.ds(0, query_width), pl.ds(query_width, HD)

        def lanes(c, size):
            return pl.ds(pl.multiple_of(c * size, size), size)

        def tokens(c):
            return pl.ds(pl.multiple_of(c * half, half), half)

        loads = (
            pltpu.make_async_copy(up_hbm, turned, w_sem.at[0]),
            pltpu.make_async_copy(down_hbm, down.at[core], w_sem.at[1]),
            pltpu.make_async_copy(qkv_hbm.at[:, rest_at], w_kv.at[:, lanes(core, HD)], w_sem.at[2]),
            pltpu.make_async_copy(qkv_hbm.at[:, query_at], w_q, w_sem.at[3]),
        )
        for load in loads:
            load.start()

        def to_sibling(i, src, dst):
            return remote(src, dst, place.sibling, c_send.at[i], c_recv.at[i])

        def gift(i, c):
            return (
                lambda: to_sibling(0, qkv_bias_of.at[core], qkv_bias_of.at[c]),
                lambda: to_sibling(1, down_bias_of.at[core], down_bias_of.at[c]),
                lambda: to_sibling(2, text_ref.at[tokens(other)], text_of.at[:, lanes(c, width)]),
                lambda: to_sibling(3, qkv_hbm.at[:, rest_at], w_kv.at[:, lanes(c, HD)]),
                lambda: to_sibling(4, down_hbm, down.at[c]),
                lambda: to_sibling(5, normed.at[core], normed.at[c]),
                lambda: to_sibling(6, placed_out, placed_in),
            )[i]()

        barrier = pltpu.get_barrier_semaphore()

        def greet(p, carry):
            pl.semaphore_signal(barrier, inc=1, device_id=(e, wrap(s + p, groups)), device_id_type=MESH)
            return carry

        lax.fori_loop(1, groups, greet, 0)
        for to in (*place.y_side, place.sibling):
            pl.semaphore_signal(barrier, inc=1, device_id=to, device_id_type=MESH)

        front = EncGather(
            place, lambda y, c, h: buf.at[y, c, pl.ds(h * cut, patch_rows - cut if h else cut)], (fns, fnr, ffs, ffr, fgs, fgr), shared=True
        )
        values = p_ref[...].astype(jnp.float32)
        mean_square = jnp.mean(values * values, axis=1, keepdims=True)
        buf[place.y, core] = (
            values * lax.rsqrt(mean_square + EPSILON) * g_ref[...].reshape(1, vision)
        ).astype(jnp.bfloat16)
        pl.semaphore_wait(barrier, groups - 1 + 3)
        front.start(0)
        front.start(1)
        qkv_bias_of[core] = qb_ref[...].reshape(1, query_width + HD)
        down_bias_of[core] = db_ref[...].reshape(1, width)
        for i in range(5):
            gift(i, core).start()
        text_of[:, lanes(core, width)] = text_ref[tokens(core)]

        loads[0].wait()
        def turn(i, carry):
            at = pl.ds(pl.multiple_of(i * 512, 512), 512)
            up[at, :] = turned[:, at].T
            return carry

        turns = joined // 512
        lax.fori_loop(0, turns // 2, turn, 0)
        front.relay()
        lax.fori_loop(turns // 2, turns, turn, 0)
        front.finish_near()

        to = lax.broadcasted_iota(jnp.int32, (4 * pad, patch_rows), 0)
        source = lax.broadcasted_iota(jnp.int32, (4 * pad, patch_rows), 1)
        moved = (source == 4 * (to % pad) + to // pad) & (to % pad < part)
        order[...] = jnp.where(moved, 1.0, 0.0).astype(jnp.bfloat16)

        lane = lax.broadcasted_iota(jnp.int32, (1, blocks * pad), 1)
        merged = jnp.where(lane % pad < part, lane // pad * part + lane % pad, -1)
        code = jnp.full((1, blocks * pad), -1, jnp.int32)
        begin = jnp.int32(0)
        for j in range(len_s.shape[0]):
            end = begin + len_s[j, s]
            inside = (merged >= begin) & (merged < end)
            code = jnp.where(inside, off_s[j, s] // rows * LMAX + merged - begin, code)
            begin = end
        slot = lax.broadcasted_iota(jnp.int32, (slots, blocks * pad), 0)
        pick = jnp.where(slot == code, 1.0, 0.0).astype(jnp.bfloat16)

        ours = off_v[...] // rows == s
        first = jnp.sum(jnp.where(ours, off_v[...] - s * rows, 0).astype(jnp.float32), axis=0, keepdims=True)
        count = jnp.sum(jnp.where(ours, len_v[...], 0).astype(jnp.float32), axis=0, keepdims=True)
        group = lax.broadcasted_iota(jnp.int32, (groups, slots), 0)
        position = lax.broadcasted_iota(jnp.int32, (groups, slots), 1)
        spread_groups = jnp.where(position // LMAX == group, 1.0, 0.0).astype(jnp.bfloat16)
        both = jnp.concatenate([jnp.broadcast_to(first, (8, groups)), jnp.broadcast_to(count, (8, groups))], axis=0)
        both = jnp.dot(both.astype(jnp.bfloat16), spread_groups, preferred_element_type=jnp.float32)
        index = (lax.broadcasted_iota(jnp.int32, (1, slots), 1) % LMAX).astype(jnp.float32)
        target = jnp.where(index < both[8:9], both[:1] + index, -1.0)
        token = lax.broadcasted_iota(jnp.int32, (half, slots), 0)

        def placing(c):
            return jnp.where((token + c * half).astype(jnp.float32) == target, 1.0, 0.0)

        covered = jnp.sum(placing(core), axis=1, keepdims=True) > 0.5

        def merge(*chips):
            count = len(chips) * 2 * pad

            def sort(c, carry):
                for i, y in enumerate(chips):
                    rows_of = jnp.dot(order[...], buf[y, c], preferred_element_type=jnp.float32)
                    ordered[:, i, c] = rows_of.astype(jnp.bfloat16).reshape(4, pad, vision)
                return carry

            lax.fori_loop(0, 2, sort, 0)
            merged_sum[:count] = jnp.broadcast_to(ub_ref[...].reshape(1, units), (count, units))

            def add_part(q, carry):
                grouped = ordered[q, : len(chips)].reshape(count, vision)
                weights = up[pl.ds(pl.multiple_of(q * vision, vision), vision), :]
                merged_sum[:count] += jnp.dot(grouped, weights, preferred_element_type=jnp.float32)
                return carry

            lax.fori_loop(0, 4, add_part, 0)
            inner = merged_sum[:count]
            inner = (0.5 * inner * (1.0 + lax.erf(inner * math.sqrt(0.5)))).astype(jnp.bfloat16)
            for i, y in enumerate(chips):
                hid[y] = inner[i * 2 * pad : (i + 1) * 2 * pad]

        front.take(0)
        merge(place.ys[0])
        front.take(1)
        front.take(2)
        merge(place.ys[1], place.ys[2])
        front.finish_far()
        front.take(3)
        merge(place.ys[3])

        chosen = jnp.dot(pick, hid[...].reshape(blocks * pad, units), preferred_element_type=jnp.float32)
        out[...] = chosen.astype(jnp.bfloat16).reshape(groups, LMAX, units)

        def swap(p, at, arrives):
            return remote(out.at[at], inn.at[arrives], (e, at), a_send.at[p], a_recv.at[p])

        def begin_swap(p, carry):
            swap(p, wrap(s + p, groups), s).start()
            return carry

        lax.fori_loop(1, groups, begin_swap, 0)
        inn[s] = out[s]
        def end_swap(p, carry):
            swap(p, wrap(s + p, groups), wrap(s - p + groups, groups)).wait_recv()
            return carry

        lax.fori_loop(1, groups, end_swap, 0)
        arrived = inn[...].reshape(slots, units)

        def place_tokens(c):
            return jnp.dot(
                placing(c).astype(jnp.bfloat16), arrived, preferred_element_type=jnp.float32
            ).astype(jnp.bfloat16)

        placed_out[...] = place_tokens(other)
        gift(6, core).start()
        placed_mine[...] = place_tokens(core)

        def share(hidden_rows, c, y_to):
            return jnp.dot(hidden_rows, down[c, :, lanes(y_to, wide)], preferred_element_type=jnp.float32)

        def relay(side):
            return remote(rel_out.at[side], rel_in.at[side], place.y_side[side], r_send.at[side], r_recv.at[side])

        def deliver(side, h):
            return remote(
                d_out.at[side, h], d_in.at[side, h], place.y_side[side], d_send.at[side, h], d_recv.at[side, h]
            )

        halves = (slice(0, half // 2), slice(half // 2, half))
        loads[1].wait()
        def target(i):
            return wrap(place.y + jnp.where(i == 0, 2, jnp.where(i == 1, 1, jnp.where(i == 2, -1, 0))), ny)

        def add_own(i, carry):
            own[i] = share(placed_mine[...], core, target(i))
            return carry

        def add_other(i, carry):
            own[i] += share(placed_in[...], other, target(i))
            return carry

        lax.fori_loop(0, 4, add_own, 0)
        gift(4, other).wait_recv()
        gift(6, other).wait_recv()
        for i in range(3):
            lax.fori_loop(i, i + 1 if i < 2 else 4, add_other, 0)
            for side in range(2):
                if i == 0:
                    rel_out[side] = own[0, halves[side]].astype(jnp.bfloat16)
                    relay(side).start()
                if i == 1 + side:
                    d_out[side, 1 - side] = own[i, halves[1 - side]].astype(jnp.bfloat16)
                    deliver(side, 1 - side).start()
        gift(1, other).wait_recv()
        gift(2, other).wait_recv()
        own[3] = own[3] + jnp.concatenate([down_bias_of[0], down_bias_of[1]], axis=1)
        for side in range(2):
            relay(side).wait_recv()
            d_out[side, side] = (own[1 + side, halves[side]] + rel_in[side].astype(jnp.float32)).astype(jnp.bfloat16)
            deliver(side, side).start()

        for c in range(2):
            token_id = lax.broadcasted_iota(jnp.int32, (half, HD), 0) + s * rows + c * half
            sine, cosine = sine_cosine(token_id.astype(jnp.float32) * freq_ref[...])
            turn_cos[c] = cosine
            turn_sin[c] = jnp.where(lax.broadcasted_iota(jnp.int32, (half, HD), 1) < HD // 2, -sine, sine)

        def rotate(block, c):
            return block * turn_cos[c] + pltpu.roll(block, HD // 2, 1) * turn_sin[c]

        back = EncGather(
            place, lambda y, c, h: full.at[y, pl.ds(h * (half // 2), half // 2)], (bns, bnr, bfs, bfr, None, None), shared=False
        )
        for h in range(2):
            at = halves[h]
            total = own[3, at]
            for side in range(2):
                deliver(side, h).wait_recv()
                total = total + d_in[side, h].astype(jnp.float32)
            kept = jnp.where(covered[at], total, text_of[at].astype(jnp.float32))
            full[place.y, at] = kept.astype(jnp.bfloat16)
            back.start(h)
        squares[...] = jnp.zeros(squares.shape, jnp.float32)

        def add_squares(y):
            block = full[y].astype(jnp.float32)
            block = block * block
            summed = block[:, :HD]
            for g in range(1, wide // HD):
                summed = summed + block[:, g * HD : (g + 1) * HD]
            squares[...] += summed

        add_squares(place.ys[0])
        back.relay()
        back.finish_near()
        for i in range(1, 3):
            add_squares(place.ys[i])
        back.finish_far()
        add_squares(place.ys[3])

        scale = lax.rsqrt(jnp.sum(squares[...], axis=1, keepdims=True) * (1.0 / model) + EPSILON)
        gain_row[...] = gain_ref[...].reshape(1, model)

        def norm_part(y, carry):
            at = lanes(y, wide)
            normed[core, :, at] = (full[y].astype(jnp.float32) * scale * gain_row[:, at]).astype(jnp.bfloat16)
            return carry

        lax.fori_loop(0, ny, norm_part, 0)
        gift(5, core).start()
        loads[2].wait()
        gift(0, other).wait_recv()
        gift(3, other).wait_recv()
        both = jnp.dot(normed[core], w_kv[...], preferred_element_type=jnp.float32)
        key = rotate(both[:, :HD] + qkv_bias_of[0, :, query_width:], core).T
        key_high = key.astype(jnp.bfloat16)
        kv[z, core, x, :, :HD] = key_high
        kv[z, core, x, :, HD : 2 * HD] = (key - key_high.astype(jnp.float32)).astype(jnp.bfloat16)
        kv[z, core, x, :, 2 * HD :] = (both[:, HD:] + qkv_bias_of[1, :, query_width:]).astype(jnp.bfloat16)

        plane = PlaneAttention(place, kv, q3, mx, den, acc, (xs, xr, hs, hr, zs, zr, ss, sr), nz, nx)
        plane.start()

        scaling = HD ** (-0.5) * math.log2(math.e)
        loads[3].wait()

        def project(i, carry):
            pairs = heads // 2
            c = jnp.where(i < pairs, core, other)
            first_head = 2 * lax.rem(i, pairs)

            at = pl.ds(pl.multiple_of(first_head * HD, 2 * HD), 2 * HD)
            query = jnp.dot(normed[c], w_q[:, at], preferred_element_type=jnp.float32) + qkv_bias_of[core, :, at]
            for n in range(2):
                head = rotate(query[:, n * HD : (n + 1) * HD], c) * scaling
                high = head.astype(jnp.bfloat16)
                low = (head - high.astype(jnp.float32)).astype(jnp.bfloat16)
                q3[first_head + n, c, :, :HD] = high
                q3[first_head + n, c, :, HD : 2 * HD] = high
                q3[first_head + n, c, :, 2 * HD :] = low
            return carry

        def sibling_tokens():
            gift(5, other).wait_recv()
            lax.fori_loop(heads // 2, heads, project, 0)

        lax.fori_loop(0, heads // 2, project, 0)
        plane.run(sibling_tokens)
        for h in range(heads):
            o_ref[:, h * HD : (h + 1) * HD] = plane.result(h).astype(o_ref.dtype)

        def sent_swap(p, carry):
            swap(p, wrap(s + p, groups), s).wait_send()
            return carry

        lax.fori_loop(1, groups, sent_swap, 0)
        front.drain()
        back.drain()
        for i in range(7):
            gift(i, core).wait_send()
        for side in range(2):
            relay(side).wait_send()
            for h in range(2):
                deliver(side, h).wait_send()
        plane.drain()

    dma = pltpu.SemaphoreType.DMA
    bf16, f32 = jnp.bfloat16, jnp.float32
    vmem = pl.BlockSpec(memory_space=pltpu.VMEM)
    smem = pl.BlockSpec(memory_space=pltpu.SMEM)
    any_space = pl.BlockSpec(memory_space=pl.ANY)
    enc_sems = [dma((2, 2)), dma((2, 2)), dma((2,)), dma((2,)), dma((4, 2)), dma((4, 2))]
    return pl.pallas_call(
        kernel,
        out_shape=jax.ShapeDtypeStruct((rows, query_width), bf16),
        in_specs=[
            vmem, vmem, any_space, vmem, any_space, vmem, vmem, smem, smem, vmem, vmem, vmem, any_space, vmem, vmem,
        ],
        out_specs=vmem,
        scratch_shapes=[
            pltpu.VMEM((ny, 2, patch_rows, vision), bf16),
            pltpu.VMEM((4 * pad, patch_rows), bf16),
            pltpu.VMEM((4, 2, 2, pad, vision), bf16),
            pltpu.VMEM((units, joined), bf16),
            pltpu.VMEM((joined, units), bf16),
            pltpu.VMEM((ny, 2 * pad, units), bf16),
            pltpu.VMEM((groups, LMAX, units), bf16),
            pltpu.VMEM((groups, LMAX, units), bf16),
            pltpu.VMEM((2, *merge_down.shape), bf16),
            pltpu.VMEM((model, query_width), bf16),
            pltpu.VMEM((model, 2 * HD), bf16),
            pltpu.VMEM((2, 1, query_width + HD), f32),
            pltpu.VMEM((2, 1, width), f32),
            pltpu.VMEM((half, wide), bf16),
            pltpu.VMEM((half, units), bf16),
            pltpu.VMEM((half, units), bf16),
            pltpu.VMEM((half, units), bf16),
            pltpu.VMEM((4 * pad, units), f32),
            pltpu.VMEM((2, half, HD), f32),
            pltpu.VMEM((2, half, HD), f32),
            pltpu.VMEM((1, model), f32),
            pltpu.VMEM((4, half, wide), f32),
            pltpu.VMEM((2, half // 2, wide), bf16),
            pltpu.VMEM((2, half // 2, wide), bf16),
            pltpu.VMEM((2, 2, half // 2, wide), bf16),
            pltpu.VMEM((2, 2, half // 2, wide), bf16),
            pltpu.VMEM((ny, half, wide), bf16),
            pltpu.VMEM((half, HD), f32),
            pltpu.VMEM((2, half, model), bf16),
            pltpu.VMEM((nz, 2, nx, half, 3 * HD), bf16),
            pltpu.VMEM((heads, 2, half, 3 * HD), bf16),
            pltpu.VMEM((heads * rows, HD), f32),
            pltpu.VMEM((heads * rows, HD), f32),
            pltpu.VMEM((heads * rows, HD), f32),
            dma((4,)),
            dma((7,)),
            dma((7,)),
            dma((groups,)),
            dma((groups,)),
            dma((2,)),
            dma((2,)),
            dma((2, 2)),
            dma((2, 2)),
            *enc_sems,
            *enc_sems[:4],
            dma((nz, 2)),
            dma((nz, 2)),
            dma((nz, 2)),
            dma((nz, 2)),
            dma((2, 4 * far)),
            dma((2, 4 * far)),
            dma((nz,)),
            dma((nz,)),
        ],
        compiler_params=pltpu.CompilerParams(
            collective_id=1, has_side_effects=True, vmem_limit_bytes=56 * 1024 * 1024
        ),
        name="prefill",
    )(
        patches, gain, up_t, up_bias, merge_down, down_bias, text, lengths, offsets, lengths, offsets, input_gain,
        qkv_weight, qkv_bias, freq,
    )


def local(
    patches, vision_gain, merge_up, merge_up_bias, merge_down, merge_down_bias, text_embed, image_lengths, image_offsets,
    input_gain, qkv_weight, qkv_bias,
):
    freq = np.exp(np.arange(HD // 2) * (-2.0 * np.log(THETA) / HD)).astype(np.float32)
    return prefill(
        patches[0], vision_gain, merge_up.T, merge_up_bias, merge_down, merge_down_bias, text_embed,
        image_lengths.T, image_offsets.T, input_gain, qkv_weight, qkv_bias,
        jnp.asarray(np.concatenate([freq, freq])[None]),
        lax.axis_size("enc") // 2, lax.axis_size("seq") // NX, NX,
    )


def solution(mesh):
    in_specs = (
        P("seq", "enc", None),
        P(),
        P(None, "enc"),
        P("enc"),
        P("enc", None),
        P("enc"),
        P("seq", "enc"),
        P(),
        P(),
        P(),
        P(None, "enc"),
        P("enc"),
    )
    out_specs = P("seq", "enc")
    return jax.shard_map(local, mesh=mesh, in_specs=in_specs, out_specs=out_specs, check_vma=False)
```

```python
import math

import jax
import jax.numpy as jnp
import numpy as np
from jax import lax
from jax.experimental import pallas as pl
from jax.experimental.pallas import tpu as pltpu
from jax.sharding import PartitionSpec as P

HD = 128
LMAX = 16
NX = 4
EPSILON = 1e-06
THETA = 1000000.0
NEG = -1e30
MESH = pl.DeviceIdType.MESH


def wrap(value, size):
    return lax.rem(value + 2 * size, size)


def remote(src, dst, to, send_sem, recv_sem):
    return pltpu.make_async_remote_copy(
        src_ref=src, dst_ref=dst, send_sem=send_sem, recv_sem=recv_sem, device_id=to, device_id_type=MESH
    )


def sine_cosine(angle):
    turns = jnp.floor(angle * (2.0 / math.pi) + 0.5)
    rest = ((angle - turns * 1.5703125) - turns * 4.837512969970703125e-4) - turns * 7.54978995489188216e-8
    square = rest * rest
    sine = ((-1.9515295891e-4 * square + 8.3321608736e-3) * square - 1.6666654611e-1) * square * rest + rest
    cosine = (
        ((2.443315711809948e-5 * square - 1.388731625493765e-3) * square + 4.166664568298827e-2) * square * square
        - 0.5 * square
        + 1.0
    )
    quadrant = turns - 4.0 * jnp.floor(turns * 0.25)
    odd = (quadrant == 1.0) | (quadrant == 3.0)
    sine, cosine = jnp.where(odd, cosine, sine), jnp.where(odd, sine, cosine)
    sine = jnp.where(quadrant >= 2.0, -sine, sine)
    cosine = jnp.where((quadrant == 1.0) | (quadrant == 2.0), -cosine, cosine)
    return sine, cosine


class EncGather:
    def __init__(self, place, half, sems, shared):
        self.place, self.half, self.shared = place, half, shared
        self.near_send, self.near_recv, self.far_send, self.far_recv, self.give_send, self.give_recv = sems

    def near(self, side, index, h):
        place = self.place
        slot = self.half(place.ys[index], place.core, h)
        return remote(slot, slot, place.y_side[side], self.near_send.at[side, h], self.near_recv.at[side, h])

    def far(self, side, index):
        place = self.place
        slot = self.half(place.ys[index], place.core, side)
        return remote(slot, slot, place.y_side[side], self.far_send.at[side], self.far_recv.at[side])

    def give(self, index, h, mine=True):
        place = self.place
        slot = self.half(place.ys[index], place.core if mine else 1 - place.core, h)
        return remote(slot, slot, place.sibling, self.give_send.at[index, h], self.give_recv.at[index, h])

    def take(self, index):
        for h in range(2):
            self.give(index, h, mine=False).wait_recv()

    def start(self, h):
        for side in range(2):
            self.near(side, 0, h).start()
        self.share(0, h)

    def share(self, index, h):
        if self.shared:
            self.give(index, h).start()

    def relay(self):
        for side in range(2):
            self.near(side, 1 + side, side).wait_recv()
            self.far(side, 1 + side).start()
            self.share(1 + side, side)

    def finish_near(self):
        for side in range(2):
            self.near(side, 1 + side, 1 - side).wait_recv()
            self.share(1 + side, 1 - side)

    def finish_far(self):
        for side in range(2):
            self.far(side, 3).wait_recv()
            self.share(3, side)

    def drain(self):
        for side in range(2):
            for h in range(2):
                self.near(side, 0, h).wait_send()
            self.far(side, 1 + side).wait_send()
        for index in range(4 if self.shared else 0):
            for h in range(2):
                self.give(index, h).wait_send()


class Place:
    def __init__(self, ny, nz, nx):
        e = lax.axis_index("enc")
        s = lax.axis_index("seq")
        self.e, self.s = e, s
        self.core, self.y = lax.rem(e, 2), lax.div(e, 2)
        self.z, self.x = lax.div(s, nx), lax.rem(s, nx)
        up, down = wrap(self.y + 1, ny), wrap(self.y - 1, ny)
        self.ys = (self.y, down, up, wrap(self.y + 2, ny))
        self.y_side = ((up * 2 + self.core, s), (down * 2 + self.core, s))
        self.sibling = (e + 1 - 2 * self.core, s)
        self.x_side = tuple((e, self.z * nx + wrap(self.x + d, nx)) for d in (1, -1))
        self.z_side = tuple((e, wrap(self.z + d, nz) * nx + self.x) for d in (1, -1))
        self.cols = (self.x, wrap(self.x - 1, nx), wrap(self.x + 1, nx), wrap(self.x + 2, nx))


class PlaneAttention:
    def __init__(self, place, kv, q3, mx, den, acc, sems, nz, nx):
        self.place, self.kv, self.q3, self.mx, self.den, self.acc, self.nz, self.nx = place, kv, q3, mx, den, acc, nz, nx
        self.xs, self.xr, self.hs, self.hr, self.zs, self.zr, self.ss, self.sr = sems
        self.far = nz // 2
        self.half = kv.shape[3]
        self.rows = 2 * self.half
        self.heads = q3.shape[0]
        self.together = min(2, self.heads)
        self.group = self.together * self.rows

    def along_x(self, j, side, i):
        place = self.place
        slot = self.kv.at[self.row_at(j), place.core, place.cols[i]]
        return remote(slot, slot, place.x_side[side], self.xs.at[j, side], self.xr.at[j, side])

    def half_on(self, j, side, i):
        place = self.place
        part = pl.ds(side * (self.half // 2), self.half // 2)
        slot = self.kv.at[self.row_at(j), place.core, place.cols[i], part]
        return remote(slot, slot, place.x_side[side], self.hs.at[j, side], self.hr.at[j, side])

    def along_z(self, j, side, i, k):
        place = self.place
        slot = self.kv.at[self.row_at(j), place.core, place.cols[i]]
        at = 4 * (k - 1) + i
        return remote(slot, slot, place.z_side[side], self.zs.at[side, at], self.zr.at[side, at])

    def half_along_z(self, j, side):
        place = self.place
        slot = self.kv.at[self.row_at(j), place.core, place.x, pl.ds(side * (self.half // 2), self.half // 2)]
        at = 4 * (self.far - 1)
        return remote(slot, slot, place.z_side[side], self.zs.at[side, at], self.zr.at[side, at])

    def give(self, j, mine=True):
        place = self.place
        slot = self.kv.at[self.row_at(j), place.core if mine else 1 - place.core]
        return remote(slot, slot, place.sibling, self.ss.at[j], self.sr.at[j])

    def row_at(self, j):
        k = (j + 1) // 2
        return wrap(self.place.z - k, self.nz) if j % 2 == 1 else wrap(self.place.z + k, self.nz)

    def ring_rows(self, k):
        far = self.far
        return [] if not 0 <= k <= far else [0] if k == 0 else [2 * k - 1] if k == far else [2 * k - 1, 2 * k]

    def comes(self, side, k):
        z = self.place.z
        return z >= k if side == 0 else wrap(z + k, self.nz) < self.far

    def goes(self, side, k):
        z = self.place.z
        if side == 0:
            return (z >= k - 1) & (z <= self.nz - 2)
        return wrap(z + k - 1, self.nz) < self.far

    def needed(self, j):
        k = (j + 1) // 2
        z = self.place.z
        return z >= k if j % 2 == 1 else z + k >= self.nz if j else z >= 0

    def start(self):
        for side in range(2):
            self.along_x(0, side, 0).start()

            @pl.when(self.goes(side, 1))
            def _(side=side):
                self.along_z(0, side, 0, 1).start()

    def compute(self, rows, c, restrict=None):
        blocks = [self.kv[row, c] for row in rows]
        pieces = len(rows) * self.nx
        high = jnp.concatenate([block[i, :, :HD] for block in blocks for i in range(self.nx)], axis=1)
        low = jnp.concatenate([block[i, :, HD : 2 * HD] for block in blocks for i in range(self.nx)], axis=1)
        v = jnp.concatenate([block[:, :, 2 * HD :].reshape(self.nx * self.half, HD) for block in blocks], axis=0)
        stacked = jnp.concatenate([high, low, high], axis=0)
        queries = [
            self.q3[h : h + self.together].reshape(self.group, 3 * HD) for h in range(0, self.heads, self.together)
        ]
        scores = [jnp.dot(query, stacked, preferred_element_type=jnp.float32) for query in queries]
        for i, score in enumerate(scores):
            at = slice(i * self.group, (i + 1) * self.group)
            if restrict is not None:
                score = jnp.concatenate([restrict(n, score[:, n * HD : (n + 1) * HD]) for n in range(pieces)], axis=1)
            new = jnp.maximum(self.mx[at], jnp.max(score, axis=1, keepdims=True))
            weights = jnp.exp2(score - jnp.concatenate([new] * pieces, axis=1))
            summed = weights[:, :HD]
            for n in range(1, pieces):
                summed = summed + weights[:, n * HD : (n + 1) * HD]
            product = jnp.dot(weights.astype(jnp.bfloat16), v, preferred_element_type=jnp.float32)
            factor = jnp.exp2(self.mx[at] - new)
            self.den[at] = self.den[at] * factor + summed
            self.acc[at] = self.acc[at] * factor + product
            self.mx[at] = new

    def own_row(self, c):
        x = self.place.x
        shape = (self.group, HD)
        token = lax.broadcasted_iota(jnp.int32, shape, 0) & (self.rows - 1)
        ahead = lax.broadcasted_iota(jnp.int32, shape, 1) - token

        def restrict(i, piece):
            limit = jnp.where(x > i, 2 * self.rows, jnp.where(x == i, 0, -2 * self.rows)) - c * self.half
            return jnp.where(ahead <= limit, piece, NEG)

        self.compute([self.place.z], c, restrict)

    def pass_rows(self, k, chosen):
        if not 1 <= k < self.far:
            return
        for side in range(2):
            j = 2 * k - 1 + side

            @pl.when(self.comes(side, k))
            def _(side=side, j=j):
                for i in chosen:
                    self.along_z(j, side, i, k).wait_recv()

            if k + 1 < self.far:
                @pl.when(self.goes(side, k + 1))
                def _(side=side, j=j):
                    for i in chosen:
                        self.along_z(j, side, i, k + 1).start()

    def spreads(self, j):
        everyone = j in (0, 2 * self.far - 1)
        return self.needed(j) if everyone else self.needed(j) & (self.place.core == 1)

    def early(self, t):
        far = self.far
        if 1 <= t <= far:
            for side in range(2):
                j = min(2 * t - 1 + side, 2 * far - 1)

                @pl.when(self.comes(side, t))
                def _(side=side, j=j):
                    if t < far:
                        self.along_z(j, side, 0, t).wait_recv()
                    else:
                        self.half_along_z(j, side).wait_recv()

                if t < far:
                    @pl.when(self.goes(side, t + 1))
                    def _(side=side, j=j):
                        if t + 1 < far:
                            self.along_z(j, side, 0, t + 1).start()
                        else:
                            self.half_along_z(j, side).start()
            for j in self.ring_rows(t):
                @pl.when(self.spreads(j))
                def _(j=j):
                    for side in range(2):
                        self.along_x(j, side, 0).start()
        for j in self.ring_rows(t - 1):
            @pl.when(self.spreads(j))
            def _(j=j):
                for side in range(2):
                    self.along_x(j, side, 1 + side).wait_recv()
                    self.half_on(j, side, 1 + side).start()

        @pl.when(self.place.core == 0)
        def _():
            if t == 1:
                for direction in range(2):
                    @pl.when(self.goes(direction, 1))
                    def _(direction=direction):
                        for i in (1, 2):
                            self.along_z(0, direction, i, 1).start()
            self.pass_rows(t - 2, (1,))

    def from_sibling(self, k):
        for j in self.ring_rows(k):
            @pl.when(self.needed(j))
            def _(j=j):
                self.give(j, mine=False).wait_recv()

    def late(self, t):
        for j in self.ring_rows(t - 2):
            @pl.when(self.spreads(j))
            def _(j=j):
                for side in range(2):
                    self.half_on(j, side, 3).wait_recv()

        @pl.when(self.place.core == 0)
        def _():
            if t == 2:
                for direction in range(2):
                    @pl.when(self.goes(direction, 1))
                    def _(direction=direction):
                        self.along_z(0, direction, 3, 1).start()
            self.pass_rows(t - 2, (2, 3))

        for j in self.ring_rows(t - 2):
            @pl.when(self.needed(j))
            def _(j=j):
                self.give(j).start()

    def run(self, queries_here):
        core, far, z, nz = self.place.core, self.far, self.place.z, self.nz
        self.mx[...] = jnp.full(self.mx.shape, NEG, jnp.float32)
        self.den[...] = jnp.zeros(self.den.shape, jnp.float32)
        self.acc[...] = jnp.zeros(self.acc.shape, jnp.float32)

        def phase(i, carry):
            for t in range(1, far + 4):
                @pl.when(i == 2 * t - 2)
                def _(t=t):
                    self.early(t)
                    if t > 3:
                        self.from_sibling(t - 3)

                @pl.when(i == 2 * t - 1)
                def _(t=t):
                    self.late(t)
                    if t == 1:
                        queries_here()
                    if t == 3:
                        self.from_sibling(0)

            @pl.when((i == 3) | (i == 5))
            def _():
                self.own_row(jnp.where(i == 3, core, 1 - core))

            odd = lax.rem(i, 2)
            k = lax.div(i, 2) - 2 + odd
            c = jnp.where(odd == 1, core, 1 - core)

            below, above = wrap(z - k, nz), wrap(z + k, nz)
            reached = (k >= 1) & (k <= far)

            @pl.when(reached & (k < far) & (below < z) & (above < z))
            def _():
                self.compute([below, above], c)

            @pl.when(reached & (below < z) & ((k == far) | (above >= z)))
            def _():
                self.compute([below], c)

            return carry

        lax.fori_loop(0, 2 * (far + 3), phase, 0)

    def result(self, h):
        at = slice(h * self.rows, (h + 1) * self.rows)
        return self.acc[at] / jnp.sum(self.den[at], axis=1, keepdims=True)

    def drain(self):
        far = self.far
        for j in range(2 * far):
            @pl.when(self.needed(j))
            def _(j=j):
                self.give(j).wait_send()

            @pl.when(self.spreads(j))
            def _(j=j):
                for side in range(2):
                    self.along_x(j, side, 0).wait_send()
                    self.half_on(j, side, 1 + side).wait_send()

        for side in range(2):
            for k in range(1, far + 1):
                @pl.when(self.goes(side, k))
                def _(side=side, k=k):
                    j = 0 if k == 1 else 2 * k - 3 + side
                    if k == far:
                        self.half_along_z(j, side).wait_send()
                    else:
                        self.along_z(j, side, 0, k).wait_send()

                        @pl.when(self.place.core == 0)
                        def _():
                            for i in range(1, 4):
                                self.along_z(j, side, i, k).wait_send()


def prefill(
    patches, gain, up_t, up_bias, merge_down, down_bias, text, lengths, offsets, input_gain, qkv_weight, qkv_bias, freq,
    ny, nz, nx,
):
    patch_rows, vision = patches.shape
    units, joined = up_t.shape
    part = patch_rows // 4
    pad = -(-part // 16) * 16
    cut = -(-patch_rows // 32) * 16
    blocks = 2 * ny
    wide = 2 * text.shape[1]
    groups = nz * nx
    slots = groups * LMAX
    rows, width = text.shape
    half = rows // 2
    model = merge_down.shape[1]
    query_width = qkv_weight.shape[1] - HD
    heads = query_width // HD
    far = nz // 2

    def kernel(
        p_ref, g_ref, up_hbm, ub_ref, down_hbm, db_ref, text_ref, len_s, off_s, len_v, off_v, gain_ref, qkv_hbm, qb_ref,
        freq_ref, o_ref,
        buf, order, ordered, turned, up, hid, out, inn, down, w_q, w_kv, qkv_bias_of, down_bias_of, text_of, placed_out, placed_in, placed_mine,
        merged_sum, turn_cos, turn_sin, gain_row, own, rel_out, rel_in, d_out, d_in, full, squares, normed, kv, q3, mx, den, acc,
        w_sem, c_send, c_recv, a_send, a_recv, r_send, r_recv, d_send, d_recv,
        fns, fnr, ffs, ffr, fgs, fgr, bns, bnr, bfs, bfr,
        xs, xr, hs, hr, zs, zr, ss, sr,
    ):
        place = Place(ny, nz, nx)
        e, s, core, z, x = place.e, place.s, place.core, place.z, place.x
        other = 1 - core

        query_at, rest_at = pl.ds(0, query_width), pl.ds(query_width, HD)

        def lanes(c, size):
            return pl.ds(pl.multiple_of(c * size, size), size)

        def tokens(c):
            return pl.ds(pl.multiple_of(c * half, half), half)

        loads = (
            pltpu.make_async_copy(up_hbm, turned, w_sem.at[0]),
            pltpu.make_async_copy(down_hbm, down.at[core], w_sem.at[1]),
            pltpu.make_async_copy(qkv_hbm.at[:, rest_at], w_kv.at[:, lanes(core, HD)], w_sem.at[2]),
            pltpu.make_async_copy(qkv_hbm.at[:, query_at], w_q, w_sem.at[3]),
        )
        for load in loads:
            load.start()

        def to_sibling(i, src, dst):
            return remote(src, dst, place.sibling, c_send.at[i], c_recv.at[i])

        def gift(i, c):
            return (
                lambda: to_sibling(0, qkv_bias_of.at[core], qkv_bias_of.at[c]),
                lambda: to_sibling(1, down_bias_of.at[core], down_bias_of.at[c]),
                lambda: to_sibling(2, text_ref.at[tokens(other)], text_of.at[:, lanes(c, width)]),
                lambda: to_sibling(3, qkv_hbm.at[:, rest_at], w_kv.at[:, lanes(c, HD)]),
                lambda: to_sibling(4, down_hbm, down.at[c]),
                lambda: to_sibling(5, normed.at[core], normed.at[c]),
                lambda: to_sibling(6, placed_out, placed_in),
            )[i]()

        barrier = pltpu.get_barrier_semaphore()

        def greet(p, carry):
            pl.semaphore_signal(barrier, inc=1, device_id=(e, wrap(s + p, groups)), device_id_type=MESH)
            return carry

        lax.fori_loop(1, groups, greet, 0)
        for to in (*place.y_side, place.sibling):
            pl.semaphore_signal(barrier, inc=1, device_id=to, device_id_type=MESH)

        front = EncGather(
            place, lambda y, c, h: buf.at[y, c, pl.ds(h * cut, patch_rows - cut if h else cut)], (fns, fnr, ffs, ffr, fgs, fgr), shared=True
        )
        values = p_ref[...].astype(jnp.float32)
        mean_square = jnp.mean(values * values, axis=1, keepdims=True)
        buf[place.y, core] = (
            values * lax.rsqrt(mean_square + EPSILON) * g_ref[...].reshape(1, vision)
        ).astype(jnp.bfloat16)
        pl.semaphore_wait(barrier, groups - 1 + 3)
        front.start(0)
        front.start(1)
        qkv_bias_of[core] = qb_ref[...].reshape(1, query_width + HD)
        down_bias_of[core] = db_ref[...].reshape(1, width)
        for i in range(5):
            gift(i, core).start()
        text_of[:, lanes(core, width)] = text_ref[tokens(core)]

        loads[0].wait()
        def turn(i, carry):
            at = pl.ds(pl.multiple_of(i * 512, 512), 512)
            up[at, :] = turned[:, at].T
            return carry

        turns = joined // 512
        lax.fori_loop(0, turns // 2, turn, 0)
        front.relay()
        lax.fori_loop(turns // 2, turns, turn, 0)
        front.finish_near()

        to = lax.broadcasted_iota(jnp.int32, (4 * pad, patch_rows), 0)
        source = lax.broadcasted_iota(jnp.int32, (4 * pad, patch_rows), 1)
        moved = (source == 4 * (to % pad) + to // pad) & (to % pad < part)
        order[...] = jnp.where(moved, 1.0, 0.0).astype(jnp.bfloat16)

        lane = lax.broadcasted_iota(jnp.int32, (1, blocks * pad), 1)
        merged = jnp.where(lane % pad < part, lane // pad * part + lane % pad, -1)
        code = jnp.full((1, blocks * pad), -1, jnp.int32)
        begin = jnp.int32(0)
        for j in range(len_s.shape[0]):
            end = begin + len_s[j, s]
            inside = (merged >= begin) & (merged < end)
            code = jnp.where(inside, off_s[j, s] // rows * LMAX + merged - begin, code)
            begin = end
        slot = lax.broadcasted_iota(jnp.int32, (slots, blocks * pad), 0)
        pick = jnp.where(slot == code, 1.0, 0.0).astype(jnp.bfloat16)

        ours = off_v[...] // rows == s
        first = jnp.sum(jnp.where(ours, off_v[...] - s * rows, 0).astype(jnp.float32), axis=0, keepdims=True)
        count = jnp.sum(jnp.where(ours, len_v[...], 0).astype(jnp.float32), axis=0, keepdims=True)
        group = lax.broadcasted_iota(jnp.int32, (groups, slots), 0)
        position = lax.broadcasted_iota(jnp.int32, (groups, slots), 1)
        spread_groups = jnp.where(position // LMAX == group, 1.0, 0.0).astype(jnp.bfloat16)
        both = jnp.concatenate([jnp.broadcast_to(first, (8, groups)), jnp.broadcast_to(count, (8, groups))], axis=0)
        both = jnp.dot(both.astype(jnp.bfloat16), spread_groups, preferred_element_type=jnp.float32)
        index = (lax.broadcasted_iota(jnp.int32, (1, slots), 1) % LMAX).astype(jnp.float32)
        target = jnp.where(index < both[8:9], both[:1] + index, -1.0)
        token = lax.broadcasted_iota(jnp.int32, (half, slots), 0)

        def placing(c):
            return jnp.where((token + c * half).astype(jnp.float32) == target, 1.0, 0.0)

        covered = jnp.sum(placing(core), axis=1, keepdims=True) > 0.5

        def merge(*chips):
            count = len(chips) * 2 * pad

            def sort(c, carry):
                for i, y in enumerate(chips):
                    rows_of = jnp.dot(order[...], buf[y, c], preferred_element_type=jnp.float32)
                    ordered[:, i, c] = rows_of.astype(jnp.bfloat16).reshape(4, pad, vision)
                return carry

            lax.fori_loop(0, 2, sort, 0)
            merged_sum[:count] = jnp.broadcast_to(ub_ref[...].reshape(1, units), (count, units))

            def add_part(q, carry):
                grouped = ordered[q, : len(chips)].reshape(count, vision)
                weights = up[pl.ds(pl.multiple_of(q * vision, vision), vision), :]
                merged_sum[:count] += jnp.dot(grouped, weights, preferred_element_type=jnp.float32)
                return carry

            lax.fori_loop(0, 4, add_part, 0)
            inner = merged_sum[:count]
            inner = (0.5 * inner * (1.0 + lax.erf(inner * math.sqrt(0.5)))).astype(jnp.bfloat16)
            for i, y in enumerate(chips):
                hid[y] = inner[i * 2 * pad : (i + 1) * 2 * pad]

        front.take(0)
        merge(place.ys[0])
        front.take(1)
        front.take(2)
        merge(place.ys[1], place.ys[2])
        front.finish_far()
        front.take(3)
        merge(place.ys[3])

        chosen = jnp.dot(pick, hid[...].reshape(blocks * pad, units), preferred_element_type=jnp.float32)
        out[...] = chosen.astype(jnp.bfloat16).reshape(groups, LMAX, units)

        def swap(p, at, arrives):
            return remote(out.at[at], inn.at[arrives], (e, at), a_send.at[p], a_recv.at[p])

        def begin_swap(p, carry):
            swap(p, wrap(s + p, groups), s).start()
            return carry

        lax.fori_loop(1, groups, begin_swap, 0)
        inn[s] = out[s]
        def end_swap(p, carry):
            swap(p, wrap(s + p, groups), wrap(s - p + groups, groups)).wait_recv()
            return carry

        lax.fori_loop(1, groups, end_swap, 0)
        arrived = inn[...].reshape(slots, units)

        def place_tokens(c):
            return jnp.dot(
                placing(c).astype(jnp.bfloat16), arrived, preferred_element_type=jnp.float32
            ).astype(jnp.bfloat16)

        placed_out[...] = place_tokens(other)
        gift(6, core).start()
        placed_mine[...] = place_tokens(core)

        def share(hidden_rows, c, y_to):
            return jnp.dot(hidden_rows, down[c, :, lanes(y_to, wide)], preferred_element_type=jnp.float32)

        def relay(side):
            return remote(rel_out.at[side], rel_in.at[side], place.y_side[side], r_send.at[side], r_recv.at[side])

        def deliver(side, h):
            return remote(
                d_out.at[side, h], d_in.at[side, h], place.y_side[side], d_send.at[side, h], d_recv.at[side, h]
            )

        halves = (slice(0, half // 2), slice(half // 2, half))
        loads[1].wait()
        def target(i):
            return wrap(place.y + jnp.where(i == 0, 2, jnp.where(i == 1, 1, jnp.where(i == 2, -1, 0))), ny)

        def add_own(i, carry):
            own[i] = share(placed_mine[...], core, target(i))
            return carry

        def add_other(i, carry):
            own[i] += share(placed_in[...], other, target(i))
            return carry

        lax.fori_loop(0, 4, add_own, 0)
        gift(4, other).wait_recv()
        gift(6, other).wait_recv()
        for i in range(3):
            lax.fori_loop(i, i + 1 if i < 2 else 4, add_other, 0)
            for side in range(2):
                if i == 0:
                    rel_out[side] = own[0, halves[side]].astype(jnp.bfloat16)
                    relay(side).start()
                if i == 1 + side:
                    d_out[side, 1 - side] = own[i, halves[1 - side]].astype(jnp.bfloat16)
                    deliver(side, 1 - side).start()
        gift(1, other).wait_recv()
        gift(2, other).wait_recv()
        own[3] = own[3] + jnp.concatenate([down_bias_of[0], down_bias_of[1]], axis=1)
        for side in range(2):
            relay(side).wait_recv()
            d_out[side, side] = (own[1 + side, halves[side]] + rel_in[side].astype(jnp.float32)).astype(jnp.bfloat16)
            deliver(side, side).start()

        for c in range(2):
            token_id = lax.broadcasted_iota(jnp.int32, (half, HD), 0) + s * rows + c * half
            sine, cosine = sine_cosine(token_id.astype(jnp.float32) * freq_ref[...])
            turn_cos[c] = cosine
            turn_sin[c] = jnp.where(lax.broadcasted_iota(jnp.int32, (half, HD), 1) < HD // 2, -sine, sine)

        def rotate(block, c):
            return block * turn_cos[c] + pltpu.roll(block, HD // 2, 1) * turn_sin[c]

        back = EncGather(
            place, lambda y, c, h: full.at[y, pl.ds(h * (half // 2), half // 2)], (bns, bnr, bfs, bfr, None, None), shared=False
        )
        for h in range(2):
            at = halves[h]
            total = own[3, at]
            for side in range(2):
                deliver(side, h).wait_recv()
                total = total + d_in[side, h].astype(jnp.float32)
            kept = jnp.where(covered[at], total, text_of[at].astype(jnp.float32))
            full[place.y, at] = kept.astype(jnp.bfloat16)
            back.start(h)
        squares[...] = jnp.zeros(squares.shape, jnp.float32)

        def add_squares(y):
            block = full[y].astype(jnp.float32)
            block = block * block
            summed = block[:, :HD]
            for g in range(1, wide // HD):
                summed = summed + block[:, g * HD : (g + 1) * HD]
            squares[...] += summed

        add_squares(place.ys[0])
        back.relay()
        back.finish_near()
        for i in range(1, 3):
            add_squares(place.ys[i])
        back.finish_far()
        add_squares(place.ys[3])

        scale = lax.rsqrt(jnp.sum(squares[...], axis=1, keepdims=True) * (1.0 / model) + EPSILON)
        gain_row[...] = gain_ref[...].reshape(1, model)

        def norm_part(y, carry):
            at = lanes(y, wide)
            normed[core, :, at] = (full[y].astype(jnp.float32) * scale * gain_row[:, at]).astype(jnp.bfloat16)
            return carry

        lax.fori_loop(0, ny, norm_part, 0)
        gift(5, core).start()
        loads[2].wait()
        gift(0, other).wait_recv()
        gift(3, other).wait_recv()
        both = jnp.dot(normed[core], w_kv[...], preferred_element_type=jnp.float32)
        key = rotate(both[:, :HD] + qkv_bias_of[0, :, query_width:], core).T
        key_high = key.astype(jnp.bfloat16)
        kv[z, core, x, :, :HD] = key_high
        kv[z, core, x, :, HD : 2 * HD] = (key - key_high.astype(jnp.float32)).astype(jnp.bfloat16)
        kv[z, core, x, :, 2 * HD :] = (both[:, HD:] + qkv_bias_of[1, :, query_width:]).astype(jnp.bfloat16)

        plane = PlaneAttention(place, kv, q3, mx, den, acc, (xs, xr, hs, hr, zs, zr, ss, sr), nz, nx)
        plane.start()

        scaling = HD ** (-0.5) * math.log2(math.e)
        loads[3].wait()

        def project(i, carry):
            pairs = heads // 2
            c = jnp.where(i < pairs, core, other)
            first_head = 2 * lax.rem(i, pairs)

            at = pl.ds(pl.multiple_of(first_head * HD, 2 * HD), 2 * HD)
            query = jnp.dot(normed[c], w_q[:, at], preferred_element_type=jnp.float32) + qkv_bias_of[core, :, at]
            for n in range(2):
                head = rotate(query[:, n * HD : (n + 1) * HD], c) * scaling
                high = head.astype(jnp.bfloat16)
                low = (head - high.astype(jnp.float32)).astype(jnp.bfloat16)
                q3[first_head + n, c, :, :HD] = high
                q3[first_head + n, c, :, HD : 2 * HD] = high
                q3[first_head + n, c, :, 2 * HD :] = low
            return carry

        def sibling_tokens():
            gift(5, other).wait_recv()
            lax.fori_loop(heads // 2, heads, project, 0)

        lax.fori_loop(0, heads // 2, project, 0)
        plane.run(sibling_tokens)
        for h in range(heads):
            o_ref[:, h * HD : (h + 1) * HD] = plane.result(h).astype(o_ref.dtype)

        def sent_swap(p, carry):
            swap(p, wrap(s + p, groups), s).wait_send()
            return carry

        lax.fori_loop(1, groups, sent_swap, 0)
        front.drain()
        back.drain()
        for i in range(7):
            gift(i, core).wait_send()
        for side in range(2):
            relay(side).wait_send()
            for h in range(2):
                deliver(side, h).wait_send()
        plane.drain()

    dma = pltpu.SemaphoreType.DMA
    bf16, f32 = jnp.bfloat16, jnp.float32
    vmem = pl.BlockSpec(memory_space=pltpu.VMEM)
    smem = pl.BlockSpec(memory_space=pltpu.SMEM)
    any_space = pl.BlockSpec(memory_space=pl.ANY)
    enc_sems = [dma((2, 2)), dma((2, 2)), dma((2,)), dma((2,)), dma((4, 2)), dma((4, 2))]
    return pl.pallas_call(
        kernel,
        out_shape=jax.ShapeDtypeStruct((rows, query_width), bf16),
        in_specs=[
            vmem, vmem, any_space, vmem, any_space, vmem, vmem, smem, smem, vmem, vmem, vmem, any_space, vmem, vmem,
        ],
        out_specs=vmem,
        scratch_shapes=[
            pltpu.VMEM((ny, 2, patch_rows, vision), bf16),
            pltpu.VMEM((4 * pad, patch_rows), bf16),
            pltpu.VMEM((4, 2, 2, pad, vision), bf16),
            pltpu.VMEM((units, joined), bf16),
            pltpu.VMEM((joined, units), bf16),
            pltpu.VMEM((ny, 2 * pad, units), bf16),
            pltpu.VMEM((groups, LMAX, units), bf16),
            pltpu.VMEM((groups, LMAX, units), bf16),
            pltpu.VMEM((2, *merge_down.shape), bf16),
            pltpu.VMEM((model, query_width), bf16),
            pltpu.VMEM((model, 2 * HD), bf16),
            pltpu.VMEM((2, 1, query_width + HD), f32),
            pltpu.VMEM((2, 1, width), f32),
            pltpu.VMEM((half, wide), bf16),
            pltpu.VMEM((half, units), bf16),
            pltpu.VMEM((half, units), bf16),
            pltpu.VMEM((half, units), bf16),
            pltpu.VMEM((4 * pad, units), f32),
            pltpu.VMEM((2, half, HD), f32),
            pltpu.VMEM((2, half, HD), f32),
            pltpu.VMEM((1, model), f32),
            pltpu.VMEM((4, half, wide), f32),
            pltpu.VMEM((2, half // 2, wide), bf16),
            pltpu.VMEM((2, half // 2, wide), bf16),
            pltpu.VMEM((2, 2, half // 2, wide), bf16),
            pltpu.VMEM((2, 2, half // 2, wide), bf16),
            pltpu.VMEM((ny, half, wide), bf16),
            pltpu.VMEM((half, HD), f32),
            pltpu.VMEM((2, half, model), bf16),
            pltpu.VMEM((nz, 2, nx, half, 3 * HD), bf16),
            pltpu.VMEM((heads, 2, half, 3 * HD), bf16),
            pltpu.VMEM((heads * rows, HD), f32),
            pltpu.VMEM((heads * rows, HD), f32),
            pltpu.VMEM((heads * rows, HD), f32),
            dma((4,)),
            dma((7,)),
            dma((7,)),
            dma((groups,)),
            dma((groups,)),
            dma((2,)),
            dma((2,)),
            dma((2, 2)),
            dma((2, 2)),
            *enc_sems,
            *enc_sems[:4],
            dma((nz, 2)),
            dma((nz, 2)),
            dma((nz, 2)),
            dma((nz, 2)),
            dma((2, 4 * far)),
            dma((2, 4 * far)),
            dma((nz,)),
            dma((nz,)),
        ],
        compiler_params=pltpu.CompilerParams(
            collective_id=1, has_side_effects=True, vmem_limit_bytes=56 * 1024 * 1024
        ),
        name="prefill",
    )(
        patches, gain, up_t, up_bias, merge_down, down_bias, text, lengths, offsets, lengths, offsets, input_gain,
        qkv_weight, qkv_bias, freq,
    )


def local(
    patches, vision_gain, merge_up, merge_up_bias, merge_down, merge_down_bias, text_embed, image_lengths, image_offsets,
    input_gain, qkv_weight, qkv_bias,
):
    freq = np.exp(np.arange(HD // 2) * (-2.0 * np.log(THETA) / HD)).astype(np.float32)
    return prefill(
        patches[0], vision_gain, merge_up.T, merge_up_bias, merge_down, merge_down_bias, text_embed,
        image_lengths.T, image_offsets.T, input_gain, qkv_weight, qkv_bias,
        jnp.asarray(np.concatenate([freq, freq])[None]),
        lax.axis_size("enc") // 2, lax.axis_size("seq") // NX, NX,
    )


def solution(mesh):
    in_specs = (
        P("seq", "enc", None),
        P(),
        P(None, "enc"),
        P("enc"),
        P("enc", None),
        P("enc"),
        P("seq", "enc"),
        P(),
        P(),
        P(),
        P(None, "enc"),
        P("enc"),
    )
    out_specs = P("seq", "enc")
    return jax.shard_map(local, mesh=mesh, in_specs=in_specs, out_specs=out_specs, check_vma=False)
```
